32 devices in a mesh: ctx: 16 (over z, x, core), head: 2 (over y).
Axes of the slice: x: 2, y: 2, z: 4, core: 2. Of those that a mesh axis runs over, the one named last changes fastest.
Arguments:
- hidden_in: bfloat16 [4096, 1536], P(('ctx', 'head')), may hold values from -6 to 6
- block_order: int32 [2, 32], replicated, may hold values from 0 to 31, as said below
- doc_ids: int32 [2, 2048], replicated, may hold values from 0 to 3, as said below
- attn_gain: bfloat16 [2, 1536], P(None, 'ctx'), may hold values from 0.5 to 1.5
- w_query: bfloat16 [2, 1536, 1536], P(None, 'ctx', 'head'), may hold values from -0.15625 to 0.15625
- w_key: bfloat16 [2, 1536, 768], P(None, 'ctx', 'head'), may hold values from -0.15625 to 0.15625
- w_value: bfloat16 [2, 1536, 768], P(None, 'ctx', 'head'), may hold values from -0.15625 to 0.15625
- w_out: bfloat16 [2, 1536, 1536], P(None, 'head', 'ctx'), may hold values from -1.75 to 1.75
- mlp_gain: bfloat16 [2, 1536], P(None, 'ctx'), may hold values from 0.5 to 1.5
- w_gate: bfloat16 [2, 1536, 4096], P(None, 'ctx', 'head'), may hold values from -0.15625 to 0.15625
- w_up: bfloat16 [2, 1536, 4096], P(None, 'ctx', 'head'), may hold values from -0.15625 to 0.15625
- w_down: bfloat16 [2, 4096, 1536], P(None, 'head', 'ctx'), may hold values from -0.09375 to 0.09375
- cotangent: bfloat16 [4096, 1536], P(('ctx', 'head')), may hold values from -6 to 6
Outputs:
- out_hidden: bfloat16 [4096, 1536], P(('ctx', 'head'))
- d_hidden: float32 [4096, 1536], P(('ctx', 'head'))
- d_attn_gain: float32 [2, 1536], P(None, 'ctx')
- d_w_query: float32 [2, 1536, 1536], P(None, 'ctx', 'head')
- d_w_key: float32 [2, 1536, 768], P(None, 'ctx', 'head')
- d_w_value: float32 [2, 1536, 768], P(None, 'ctx', 'head')
- d_w_out: float32 [2, 1536, 1536], P(None, 'head', 'ctx')
- d_mlp_gain: float32 [2, 1536], P(None, 'ctx')
- d_w_gate: float32 [2, 1536, 4096], P(None, 'ctx', 'head')
- d_w_up: float32 [2, 1536, 4096], P(None, 'ctx', 'head')
- d_w_down: float32 [2, 4096, 1536], P(None, 'head', 'ctx')
The draws below stay inside these ranges and needn't reach their ends.
Inputs may be any that keep to these rules, and one draw needn't show every extreme that they name: `block_order`: each row holds every number of 0 to 31 once. `doc_ids`: each row never falls from one position to the next.
All inputs are finite; a program needn't handle non-finite values.
Results may differ from the reference program's by a relative error of at most 0.025.
Values may be sent and summed in bfloat16 or wider, within the bound.
A program may use at most 320 MiB of HBM per device.

```python
import math
import jax
import jax.numpy as jnp
from jax import lax

D = 1536
QUERY_HEADS = 16
KEY_VALUE_HEADS = 8
HEAD_SIZE = 96
FF = 4096
LAYERS = 2
SEQS = 2
NCUTS = 3
BLK = 64
NBLK = 32
TOKEN_TOTAL = 4096
SEQ_LEN = 2048
QW = 1536
KW = 768
N_CTX = 16


def block_layout(key):
    orders = []
    for seq_id in range(SEQS):
        orders.append(jax.random.permutation(jax.random.fold_in(key, seq_id), NBLK))
    return jnp.stack(orders).astype(jnp.int32)


def draw_block_order(key, part):
    return block_layout(key)


def draw_doc_ids(key, part):
    orders = block_layout(key)
    key = jax.random.fold_in(key, 7)
    middle = NBLK // 4 * 2
    held_blocks = jnp.concatenate([orders[:, 0:2], orders[:, middle:middle + 2], orders[:, NBLK - 2:NBLK]], axis=1)
    lower_edge = jnp.min(held_blocks, axis=1) * BLK
    upper_edge = (jnp.max(held_blocks, axis=1) + 1) * BLK
    cut_points = jax.random.randint(key, (SEQS, NCUTS), 0, SEQ_LEN, dtype=jnp.int32)
    inside = (cut_points > lower_edge[:, None]) & (cut_points < upper_edge[:, None])
    cut_points = jnp.where(inside, lower_edge[:, None], cut_points)
    places = jnp.arange(SEQ_LEN, dtype=jnp.int32)
    return jnp.sum((places[None, :, None] >= cut_points[:, None, :]).astype(jnp.int32), axis=2)


def steps_of(rng, extent, pieces, smallest, high):
    loudness, own = 1.0, jax.random.fold_in(rng, 6)
    for position, parts in pieces:
        steps = jnp.exp(jax.random.uniform(jax.random.fold_in(own, position), (parts,), jnp.float32, smallest / len(pieces), high / len(pieces)))
        loudness = loudness * jnp.repeat(steps, extent[position] // parts).reshape([-1 if axis == position else 1 for axis in range(len(extent))])
    return loudness


def centred(stream_key, dims, scale, limit, shards=(), kind=jnp.bfloat16):
    drawn = jax.random.normal(stream_key, dims, jnp.float32) * scale
    if len(shards) > 0:
        drawn = steps_of(stream_key, dims, shards, -0.22, 0.18) * drawn
    return jnp.clip(drawn, min=-limit, max=limit).astype(kind)


def setup_inputs(seed: int = 0) -> dict:
    seeds = jax.random.split(jax.random.key(seed), 14)
    hidden_in = centred(seeds[0], (TOKEN_TOTAL, D), 1.0, 6.0, ((0, 32),))
    block_order = draw_block_order(jax.random.fold_in(seeds[13], 71), 0)
    doc_ids = draw_doc_ids(jax.random.fold_in(seeds[13], 71), 0)
    attn_gain = jnp.clip(1.0 + 0.1 * jax.random.normal(seeds[3], (LAYERS, D), jnp.float32), 0.5, 1.5).astype(jnp.bfloat16)
    w_query = centred(seeds[4], (LAYERS, D, QW), D ** -0.5, 0.15625, ((1, 16), (2, 2)))
    w_key = centred(seeds[5], (LAYERS, D, KW), D ** -0.5, 0.15625, ((1, 16), (2, 2)))
    w_value = centred(seeds[6], (LAYERS, D, KW), D ** -0.5, 0.15625, ((1, 16), (2, 2)))
    w_out = centred(seeds[7], (LAYERS, QW, D), (max(QW * 16 // SEQ_LEN, 1)) ** -0.5, 1.75, ((1, 2), (2, 16)))
    mlp_gain = jnp.clip(1.0 + 0.1 * jax.random.normal(seeds[8], (LAYERS, D), jnp.float32), 0.5, 1.5).astype(jnp.bfloat16)
    w_gate = centred(seeds[9], (LAYERS, D, FF), D ** -0.5, 0.15625, ((1, 16), (2, 2)))
    w_up = centred(seeds[10], (LAYERS, D, FF), D ** -0.5, 0.15625, ((1, 16), (2, 2)))
    w_down = centred(seeds[11], (LAYERS, FF, D), FF ** -0.5, 0.09375, ((1, 2), (2, 16)))
    cotangent = centred(seeds[12], (TOKEN_TOTAL, D), 1.0, 6.0, ((0, 32),))
    return {"hidden_in": hidden_in, "block_order": block_order, "doc_ids": doc_ids, "attn_gain": attn_gain, "w_query": w_query, "w_key": w_key, "w_value": w_value, "w_out": w_out, "mlp_gain": mlp_gain, "w_gate": w_gate, "w_up": w_up, "w_down": w_down, "cotangent": cotangent}


NEG = -1e+30
EPS = 1e-05
THETA = 100000.0

@jax.custom_vjp
def reduced_copy(v):
    return lax.optimization_barrier(v.astype(jnp.bfloat16)).astype(jnp.float32)

@jax.custom_vjp
def reduced_backward(v):
    return v

def low_keep(v):
    return (reduced_copy(v), None)

def low_pass(kept, grad):
    return (grad,)

def back_keep(v):
    return (v, None)

def back_low(kept, grad):
    return (reduced_copy(grad),)
reduced_copy.defvjp(low_keep, low_pass)
reduced_backward.defvjp(back_keep, back_low)

def gain_product(left, right):
    return jnp.dot(left, right, precision=lax.Precision.HIGHEST)

def rms_norm(value_rows, gain):
    return value_rows * lax.rsqrt(lax.optimization_barrier(jnp.mean(value_rows * value_rows, axis=-1, keepdims=True)) + EPS) * gain

def rope_tables(positions):
    half_dim = HEAD_SIZE // 2
    freq_row = jnp.exp(jnp.arange(half_dim, dtype=jnp.float32) * (-2.0 * math.log(THETA) / HEAD_SIZE))
    angles = positions.astype(jnp.float32)[:, None] * freq_row[None, :]
    return (jnp.cos(angles), jnp.sin(angles))

def rotate(tensor, cosine, sine_table):
    half_dim = tensor.shape[-1] // 2
    first_half = tensor[..., :half_dim]
    second_half = tensor[..., half_dim:]
    cos_wide = cosine[:, None, :]
    sin_wide = sine_table[:, None, :]
    return jnp.concatenate([first_half * cos_wide - second_half * sin_wide, second_half * cos_wide + first_half * sin_wide], axis=-1)

def sequence_view(table):
    shaped = table.reshape((N_CTX, SEQS, 2 * BLK) + table.shape[1:])
    return jnp.swapaxes(shaped, 0, 1).reshape((SEQS, SEQ_LEN) + table.shape[1:])

def token_view(table):
    shaped = table.reshape((SEQS, N_CTX, 2 * BLK) + table.shape[2:])
    return jnp.swapaxes(shaped, 0, 1).reshape((TOKEN_TOTAL,) + table.shape[2:])

def attend_block(query_matrix, positions_q, docs_q, keys_all, values_all, positions_k, docs_k):
    block_length = query_matrix.shape[0]
    grouped_heads = query_matrix.reshape(block_length, KEY_VALUE_HEADS, QUERY_HEADS // KEY_VALUE_HEADS, HEAD_SIZE)
    scores = reduced_backward(jnp.einsum('qhgd,khd->hgqk', grouped_heads, keys_all, precision=lax.Precision.HIGHEST))
    allowed = (positions_k[None, :] <= positions_q[:, None]) & (docs_k[None, :] == docs_q[:, None])
    scores = jnp.where(allowed, scores, NEG)
    probs = reduced_copy(jax.nn.softmax(scores, axis=-1))
    mixed = jnp.einsum('hgqk,khd->qhgd', probs, values_all, precision=lax.Precision.HIGHEST)
    return mixed.reshape(block_length, QUERY_HEADS * HEAD_SIZE)

def attention(query_matrix, keys, value_rows, positions_seq, docs_seq):
    query_len = 512 if SEQ_LEN % 512 == 0 else SEQ_LEN
    block_total = SEQ_LEN // query_len

    def one_sequence(packed):
        seq_q, seq_k, seq_v, seq_pos, seq_doc = packed

        def one_block(portion):
            return attend_block(portion[0], portion[1], portion[2], seq_k, seq_v, seq_pos, seq_doc)
        portions = (seq_q.reshape(block_total, query_len, QUERY_HEADS, HEAD_SIZE), seq_pos.reshape(block_total, query_len), seq_doc.reshape(block_total, query_len))
        return lax.map(jax.checkpoint(one_block), portions).reshape(SEQ_LEN, QUERY_HEADS * HEAD_SIZE)
    mixed = lax.map(one_sequence, (sequence_view(query_matrix), sequence_view(keys), sequence_view(value_rows), positions_seq, docs_seq))
    return token_view(mixed)

def reference(hidden_in, block_order, doc_ids, attn_gain, w_query, w_key, w_value, w_out, mlp_gain, w_gate, w_up, w_down, cotangent):
    offsets = jnp.arange(BLK, dtype=jnp.int32)
    positions_seq = (block_order[:, :, None] * BLK + offsets[None, None, :]).reshape(SEQS, SEQ_LEN).astype(jnp.int32)
    docs_seq = jnp.take_along_axis(doc_ids, positions_seq, axis=1)
    positions_tok = token_view(positions_seq)
    cosine, sine_table = rope_tables(positions_tok)
    scale_q = HEAD_SIZE ** (-0.5)

    def forward(inputs, gains_a, wq_all, key_weight_stack, value_weight_stack, wo_all, gains_m, wg_all, wu_all, wd_all):
        residual = inputs
        for layer_number in range(LAYERS):
            normed_rows = reduced_copy(rms_norm(residual, gains_a[layer_number]))
            q_pre = reduced_backward(gain_product(normed_rows, wq_all[layer_number])).reshape(TOKEN_TOTAL, QUERY_HEADS, HEAD_SIZE)
            key_unrotated = reduced_backward(gain_product(normed_rows, key_weight_stack[layer_number])).reshape(TOKEN_TOTAL, KEY_VALUE_HEADS, HEAD_SIZE)
            value_unrotated = reduced_copy(reduced_backward(gain_product(normed_rows, value_weight_stack[layer_number]))).reshape(TOKEN_TOTAL, KEY_VALUE_HEADS, HEAD_SIZE)
            query_matrix = reduced_copy(rotate(q_pre, cosine, sine_table) * scale_q)
            keys = reduced_copy(rotate(key_unrotated, cosine, sine_table))
            mixed = reduced_copy(reduced_backward(attention(query_matrix, keys, value_unrotated, positions_seq, docs_seq)))
            residual = residual + reduced_backward(gain_product(mixed, wo_all[layer_number]))
            normed2 = reduced_copy(rms_norm(residual, gains_m[layer_number]))
            gate_part = reduced_backward(gain_product(normed2, wg_all[layer_number]))
            up_part = reduced_backward(gain_product(normed2, wu_all[layer_number]))
            activated = reduced_copy(jax.nn.silu(gate_part) * up_part)
            residual = residual + reduced_backward(gain_product(activated, wd_all[layer_number]))
        return residual
    floats = tuple((item.astype(jnp.float32) for item in (hidden_in, attn_gain, w_query, w_key, w_value, w_out, mlp_gain, w_gate, w_up, w_down)))
    result, pullback = jax.vjp(forward, *floats)
    grads = pullback(cotangent.astype(jnp.float32))
    return (result.astype(jnp.bfloat16), grads[0], grads[1], grads[2], grads[3], grads[4], grads[5], grads[6], grads[7], grads[8], grads[9])
```

```python
import math

import jax
import jax.numpy as jnp
from jax import lax
from jax.experimental import pallas as pl
from jax.experimental.pallas import tpu as pltpu
from jax.sharding import PartitionSpec as P

HEAD_SIZE = 96
HALF = HEAD_SIZE // 2
SEQS = 2
BLK = 64
ROWS = 2 * BLK

NEG = -1e30
EPS = 1e-05
THETA = 100000.0
VMEM_LIMIT = 56 * 1024 * 1024
BF16 = jnp.bfloat16
F32 = jnp.float32


def ring_of(chips):
    return list(range(0, chips, 2)) + list(range(chips - 1, 0, -2))


def rope_tables(positions):
    freq_row = jnp.exp(jnp.arange(HALF, dtype=F32) * (-2.0 * math.log(THETA) / HEAD_SIZE))
    angles = positions.astype(F32)[:, None] * freq_row[None, :]
    return (jnp.cos(angles), jnp.sin(angles))


def rotate(tensor, cosine, sine_table):
    first, second = tensor[..., :HALF], tensor[..., HALF:]
    cos_wide, sin_wide = cosine[:, None, :], sine_table[:, None, :]
    return jnp.concatenate(
        [first * cos_wide - second * sin_wide, second * cos_wide + first * sin_wide], axis=-1
    )


def rotate_back(tensor, cosine, sine_table):
    first, second = tensor[..., :HALF], tensor[..., HALF:]
    cos_wide, sin_wide = cosine[:, None, :], sine_table[:, None, :]
    return jnp.concatenate(
        [first * cos_wide + second * sin_wide, second * cos_wide - first * sin_wide], axis=-1
    )


def dot(left, right):
    return jnp.dot(left, right, preferred_element_type=F32)


def dot_nt(left, right):
    return lax.dot_general(left, right, (((1,), (1,)), ((), ())), preferred_element_type=F32)


def dot_tn(left, right):
    return lax.dot_general(left, right, (((0,), (0,)), ((), ())), preferred_element_type=F32)


def row_tile(keys):
    return 256 if keys <= 2048 else 64


def gathered(own_ref, sib_ref):
    count = own_ref.shape[0]
    return jnp.concatenate(
        [own_ref[j] for j in range(count)] + [sib_ref[j] for j in range(count)], axis=1
    )


def mask_rows(kpos_ref, qpos_ref, qstart_ref, start, rows):
    kpos = kpos_ref[0]
    parts = []
    done = 0
    while done < rows:
        at = (start + done) % ROWS
        size = min(rows - done, ROWS - at)
        qpos = qpos_ref[0, at : at + size, :]
        qstart = qstart_ref[0, at : at + size, :]
        parts.append((kpos <= qpos) & (kpos >= qstart))
        done += size
    return parts


def masked(scores, parts):
    out = []
    at = 0
    for part in parts:
        size = part.shape[0]
        out.append(jnp.where(part, scores[at : at + size, :], NEG))
        at += size
    return jnp.concatenate(out, axis=0) if len(out) > 1 else out[0]


def attend_kernel(
    q_ref, ko_ref, ks_ref, vo_ref, vs_ref, kpos_ref, qpos_ref, qstart_ref, o_ref, lse_ref
):
    total = q_ref.shape[2]
    kt = gathered(ko_ref, ks_ref)
    vt = gathered(vo_ref, vs_ref)
    tile = min(total, row_tile(kt.shape[1]))
    for at in range(0, total, tile):
        q = q_ref[0, 0, at : at + tile, :]
        scores = masked(dot(q, kt), mask_rows(kpos_ref, qpos_ref, qstart_ref, at, tile))
        top = jnp.max(scores, axis=1, keepdims=True)
        weights = jnp.exp(scores - top)
        norm = jnp.sum(weights, axis=1, keepdims=True)
        probs = (weights * (1.0 / norm)).astype(BF16)
        o_ref[0, 0, at : at + tile, :] = dot_nt(probs, vt).astype(BF16)
        lse_ref[0, 0, at : at + tile, :] = top + jnp.log(norm)


def attend_back_kernel(
    q_ref,
    do_ref,
    lse_ref,
    ko_ref,
    ks_ref,
    vo_ref,
    vs_ref,
    kpos_ref,
    qpos_ref,
    qstart_ref,
    dq_ref,
    dko_ref,
    dks_ref,
    dvo_ref,
    dvs_ref,
):
    total = q_ref.shape[2]
    kt = gathered(ko_ref, ks_ref)
    vt = gathered(vo_ref, vs_ref)
    tile = min(total, row_tile(kt.shape[1]))
    dkt = None
    dvt = None
    for at in range(0, total, tile):
        q = q_ref[0, 0, at : at + tile, :]
        grad = do_ref[0, 0, at : at + tile, :]
        scores = masked(dot(q, kt), mask_rows(kpos_ref, qpos_ref, qstart_ref, at, tile))
        probs = jnp.exp(scores - lse_ref[0, 0, at : at + tile, :])
        dprobs = dot(grad, vt)
        delta = jnp.sum(probs * dprobs, axis=1, keepdims=True)
        dscores = (probs * (dprobs - delta)).astype(BF16)
        dq_ref[0, 0, at : at + tile, :] = dot_nt(dscores, kt)
        dk_part = dot_tn(q, dscores)
        dv_part = dot_tn(grad, probs.astype(BF16))
        dkt = dk_part if dkt is None else dkt + dk_part
        dvt = dv_part if dvt is None else dvt + dv_part
    count = dko_ref.shape[0]
    for j in range(count):
        dko_ref[j] = dkt[:, j * ROWS : (j + 1) * ROWS].astype(BF16)
        dks_ref[j] = dkt[:, (count + j) * ROWS : (count + j + 1) * ROWS].astype(BF16)
        dvo_ref[j] = dvt[:, j * ROWS : (j + 1) * ROWS].astype(BF16)
        dvs_ref[j] = dvt[:, (count + j) * ROWS : (count + j + 1) * ROWS].astype(BF16)


def attention_specs(q, kv_own, kpos):
    slots = kv_own.shape[0]
    kv_heads = kv_own.shape[1] // (2 * HEAD_SIZE)
    keys = kpos.shape[2]
    rows = q.shape[2]
    unit = pl.BlockSpec((1, 1, rows, HEAD_SIZE), lambda s, h: (s, h, 0, 0))
    column = pl.BlockSpec((1, 1, rows, 1), lambda s, h: (s, h, 0, 0))
    k_spec = pl.BlockSpec((slots, HEAD_SIZE, ROWS), lambda s, h: (0, h, s))
    v_spec = pl.BlockSpec((slots, HEAD_SIZE, ROWS), lambda s, h: (0, kv_heads + h, s))
    kpos_spec = pl.BlockSpec((1, 1, keys), lambda s, h: (s, 0, 0))
    q_spec = pl.BlockSpec((1, ROWS, 1), lambda s, h: (s, 0, 0))
    return kv_heads, unit, column, k_spec, v_spec, kpos_spec, q_spec


def attend_forward(q, kv_own, kv_sib, kpos, qpos, qstart):
    kv_heads, unit, column, k_spec, v_spec, kpos_spec, q_spec = attention_specs(q, kv_own, kpos)
    rows, keys = q.shape[2], kpos.shape[2]
    work = SEQS * kv_heads * rows * keys
    return pl.pallas_call(
        attend_kernel,
        grid=(SEQS, kv_heads),
        in_specs=[unit, k_spec, k_spec, v_spec, v_spec, kpos_spec, q_spec, q_spec],
        out_specs=[unit, column],
        out_shape=[
            jax.ShapeDtypeStruct(q.shape, BF16),
            jax.ShapeDtypeStruct(q.shape[:3] + (1,), F32),
        ],
        compiler_params=pltpu.CompilerParams(vmem_limit_bytes=VMEM_LIMIT),
        cost_estimate=pl.CostEstimate(
            flops=8 * HEAD_SIZE * work, bytes_accessed=8 * 2**20, transcendentals=work
        ),
    )(q, kv_own, kv_sib, kv_own, kv_sib, kpos, qpos, qstart)


def attend_backward(q, grad, lse, kv_own, kv_sib, kpos, qpos, qstart):
    kv_heads, unit, column, k_spec, v_spec, kpos_spec, q_spec = attention_specs(q, kv_own, kpos)
    rows, keys = q.shape[2], kpos.shape[2]
    work = SEQS * kv_heads * rows * keys
    slots = kv_own.shape[0]
    grad_spec = pl.BlockSpec((slots, HEAD_SIZE, ROWS), lambda s, h: (0, h, s))
    grad_shape = jax.ShapeDtypeStruct((slots, kv_heads * HEAD_SIZE, SEQS * ROWS), BF16)
    return pl.pallas_call(
        attend_back_kernel,
        grid=(SEQS, kv_heads),
        in_specs=[
            unit, unit, column, k_spec, k_spec, v_spec, v_spec, kpos_spec, q_spec, q_spec
        ],
        out_specs=[unit, grad_spec, grad_spec, grad_spec, grad_spec],
        out_shape=[jax.ShapeDtypeStruct(q.shape, F32)] + [grad_shape] * 4,
        compiler_params=pltpu.CompilerParams(vmem_limit_bytes=VMEM_LIMIT),
        cost_estimate=pl.CostEstimate(
            flops=20 * HEAD_SIZE * work, bytes_accessed=16 * 2**20, transcendentals=work
        ),
    )(q, grad, lse, kv_own, kv_sib, kv_own, kv_sib, kpos, qpos, qstart)


def build(n_ctx):
    chips = n_ctx // 2
    ring = ring_of(chips)

    def shifted(step):
        pairs = []
        for at, chip in enumerate(ring):
            target = ring[(at + step) % chips]
            pairs += [(chip * 2 + core, target * 2 + core) for core in range(2)]
        return pairs

    up, down = shifted(1), shifted(-1)
    sibling = [(i, i ^ 1) for i in range(n_ctx)]

    def send_up(value):
        return lax.ppermute(value, "ctx", up)

    def send_down(value):
        return lax.ppermute(value, "ctx", down)

    def swap_core(value):
        return lax.ppermute(value, "ctx", sibling)

    def swap_head(value):
        return lax.ppermute(value, "head", [(0, 1), (1, 0)])

    def ring_gather(shard):
        got = {0: shard}
        low, high = shard, shard
        half = chips // 2
        for step in range(1, half):
            low, high = send_up(low), send_down(high)
            got[chips - step] = low
            got[step] = high
        cut = shard.shape[0] // 2
        got[half] = jnp.concatenate([send_up(low[:cut]), send_down(high[cut:])], axis=0)
        return [got[j] for j in range(chips)]

    def ring_scatter(slots):
        low = slots[chips - 1][0].astype(BF16)
        high = slots[1][1].astype(BF16)
        for step in range(1, chips):
            low, high = send_up(low), send_down(high)
            own_low = slots[(chips - 1 - step) % chips][0].astype(F32)
            own_high = slots[(1 + step) % chips][1].astype(F32)
            low, high = low.astype(F32) + own_low, high.astype(F32) + own_high
            if step < chips - 1:
                low, high = low.astype(BF16), high.astype(BF16)
        return low, high

    def weight_gather(shard):
        own = jnp.concatenate(ring_gather(shard), axis=0)
        return own, swap_core(own)

    def weight_scatter(grad):
        db, cut = grad.shape[0] // chips, grad.shape[1] // 2
        slots = [
            (grad[j * db : (j + 1) * db, :cut], grad[j * db : (j + 1) * db, cut:])
            for j in range(chips)
        ]
        return jnp.concatenate(ring_scatter(slots), axis=1)

    def local(
        hidden_in,
        block_order,
        doc_ids,
        attn_gain,
        w_query,
        w_key,
        w_value,
        w_out,
        mlp_gain,
        w_gate,
        w_up,
        w_down,
        cotangent,
    ):
        layers, db = w_query.shape[0], w_query.shape[1]
        width = db * n_ctx
        side = width // 2
        q_width, kv_width, ff_width = w_query.shape[2], w_key.shape[2], w_gate.shape[2]
        heads_q, heads_kv = q_width // HEAD_SIZE, kv_width // HEAD_SIZE
        group = heads_q // heads_kv
        own_rows = hidden_in.shape[0]
        token_rows = own_rows * 2
        ctx = lax.axis_index("ctx")
        head = lax.axis_index("head")
        core = ctx % 2
        place_of = [0] * chips
        for at, chip in enumerate(ring):
            place_of[chip] = at
        place = jnp.array(place_of, jnp.int32)[ctx // 2]

        slot_ids = jnp.arange(n_ctx, dtype=jnp.int32)
        along = (place + slot_ids % chips) % chips
        chip_of = jnp.where(along < chips // 2, 2 * along, 2 * (chips - 1 - along) + 1)
        block_of = chip_of * 2 + (core + slot_ids // chips) % 2
        block_hot = (block_of[:, None] == slot_ids[None, :]).astype(F32)
        feature = jnp.arange(width, dtype=jnp.int32)
        wanted = jnp.repeat(block_of, db) * db + feature % db
        to_ring = (feature[:, None] == wanted[None, :]).astype(BF16)

        def reorder(rows):
            return dot(rows, to_ring)

        def restore(rows):
            return lax.dot_general(
                rows,
                to_ring.astype(F32),
                (((1,), (1,)), ((), ())),
                precision=lax.Precision.HIGHEST,
                preferred_element_type=F32,
            )

        fetched = []
        for layer in range(layers):
            attn_shard = jnp.concatenate(
                [w_query[layer], w_key[layer], w_value[layer], w_out[layer].T], axis=1
            )
            mlp_shard = jnp.concatenate([w_gate[layer], w_up[layer], w_down[layer].T], axis=1)
            fetched.append((weight_gather(attn_shard), weight_gather(mlp_shard)))
        gains = lax.all_gather(
            jnp.concatenate([attn_gain, mlp_gain], axis=0), "ctx", axis=1, tiled=True
        )
        gains = reorder(gains)

        offsets = jnp.arange(BLK, dtype=jnp.int32)
        first = (head == 0)[..., None, None]
        order = jnp.where(first, block_order, block_order[::-1])
        docs = jnp.where(first, doc_ids, doc_ids[::-1])
        own_blocks = lax.dynamic_slice(order, (jnp.int32(0), 2 * ctx), (SEQS, 2))
        q_positions = (own_blocks[:, :, None] * BLK + offsets[None, None, :]).reshape(SEQS, ROWS)
        ring_blocks = jnp.einsum(
            "ac,scb->sab", block_hot, order.reshape(SEQS, n_ctx, 2).astype(F32)
        ).astype(jnp.int32)
        k_positions = (ring_blocks[..., None] * BLK + offsets).reshape(SEQS, 1, n_ctx * ROWS)
        doc_blocks = docs.reshape(SEQS, -1, BLK)
        own_hot = (own_blocks[:, :, None] == jnp.arange(doc_blocks.shape[1])).astype(F32)
        q_docs = jnp.einsum("sab,sbj->saj", own_hot, doc_blocks.astype(F32)).astype(jnp.int32)
        q_docs = q_docs.reshape(SEQS, ROWS)
        q_starts = jnp.sum((docs[:, None, :] < q_docs[:, :, None]).astype(jnp.int32), axis=2)
        kpos = k_positions
        qpos, qstart = q_positions[:, :, None], q_starts[:, :, None]
        cosine, sine_table = rope_tables(q_positions.reshape(token_rows))
        scale_q = HEAD_SIZE ** (-0.5)

        def both_rows(rows):
            return jnp.concatenate([rows, swap_head(rows)], axis=0)

        def to_owner(parts):
            return parts[:own_rows] + swap_head(parts[own_rows:].astype(BF16)).astype(F32)

        def project(rows, weight, lo, hi):
            own, sib = weight
            return dot(rows[:, :side], own[:, lo:hi]) + dot(rows[:, side:], sib[:, lo:hi])

        def project_back(rows, weight, lo, hi):
            own, sib = weight
            return jnp.concatenate(
                [dot_nt(rows, own[:, lo:hi]), dot_nt(rows, sib[:, lo:hi])], axis=1
            )

        def weight_grad(left, right):
            lefts = jnp.concatenate([left[:, :side], swap_core(left[:, side:])], axis=0)
            rights = jnp.concatenate([right, swap_core(right)], axis=0)
            return dot_tn(lefts, rights)

        def units(rows):
            shaped = rows.reshape(SEQS, ROWS, heads_kv, group, HEAD_SIZE)
            return shaped.transpose(0, 2, 3, 1, 4).reshape(SEQS, heads_kv, group * ROWS, HEAD_SIZE)

        def from_units(parts):
            shaped = parts.reshape(SEQS, heads_kv, group, ROWS, HEAD_SIZE)
            return shaped.transpose(0, 3, 1, 2, 4).reshape(token_rows, q_width)

        qkv_width = q_width + 2 * kv_width
        attn_width = qkv_width + q_width
        residual = reorder(hidden_in)
        grad_res = reorder(cotangent)
        records = []
        for layer in range(layers):
            attn_w, mlp_w = fetched[layer]
            gain_a, gain_m = gains[layer], gains[layers + layer]
            residual_in = residual
            inverse_a = lax.rsqrt(jnp.mean(residual * residual, axis=-1, keepdims=True) + EPS)
            normed_a = both_rows((residual * inverse_a * gain_a).astype(BF16))
            projected = project(normed_a, attn_w, 0, qkv_width)
            q_rows = rotate(
                projected[:, :q_width].reshape(token_rows, heads_q, HEAD_SIZE), cosine, sine_table
            )
            queries = units((q_rows * scale_q).astype(BF16).reshape(token_rows, q_width))
            keys = rotate(
                projected[:, q_width : q_width + kv_width].reshape(
                    token_rows, heads_kv, HEAD_SIZE
                ),
                cosine,
                sine_table,
            ).reshape(token_rows, kv_width)
            kv_shard = jnp.concatenate([keys, projected[:, q_width + kv_width :]], axis=1)
            kv_own = jnp.stack(ring_gather(kv_shard.astype(BF16).T), axis=0)
            kv_sib = swap_core(kv_own)
            mixed, lse = attend_forward(queries, kv_own, kv_sib, kpos, qpos, qstart)
            attended = from_units(mixed)
            middle = residual + to_owner(project_back(attended, attn_w, qkv_width, attn_width))
            inverse_m = lax.rsqrt(jnp.mean(middle * middle, axis=-1, keepdims=True) + EPS)
            normed_m = both_rows((middle * inverse_m * gain_m).astype(BF16))
            gate_up = project(normed_m, mlp_w, 0, 2 * ff_width)
            gate_part, up_part = gate_up[:, :ff_width], gate_up[:, ff_width:]
            activated = (jax.nn.silu(gate_part) * up_part).astype(BF16)
            residual = middle + to_owner(
                project_back(activated, mlp_w, 2 * ff_width, 3 * ff_width)
            )
            records.append(
                (
                    residual_in,
                    inverse_a,
                    normed_a,
                    queries,
                    kv_own,
                    kv_sib,
                    lse,
                    attended,
                    middle,
                    inverse_m,
                    normed_m,
                    gate_part,
                    up_part,
                    activated,
                )
            )
        out_hidden = lax.dot_general(
            residual.astype(BF16), to_ring, (((1,), (1,)), ((), ())), preferred_element_type=F32
        ).astype(BF16)

        def norm_back(grad_res, normed_gradient, value_rows, inverse_norm, gain):
            normalized = value_rows * inverse_norm
            gain_gradient = jnp.sum(normed_gradient * normalized, axis=0)
            scaled = normed_gradient * gain
            mean = jnp.mean(scaled * normalized, axis=-1, keepdims=True)
            return grad_res + inverse_norm * (scaled - normalized * mean), gain_gradient

        d_attn = [None] * layers
        d_mlp = [None] * layers
        d_gains = [None] * (2 * layers)
        for layer in reversed(range(layers)):
            attn_w, mlp_w = fetched[layer]
            gain_a, gain_m = gains[layer], gains[layers + layer]
            (
                residual_in,
                inverse_a,
                normed_a,
                queries,
                kv_own,
                kv_sib,
                lse,
                attended,
                middle,
                inverse_m,
                normed_m,
                gate_part,
                up_part,
                activated,
            ) = records[layer]
            grad_rows_m = both_rows(grad_res.astype(BF16))
            grad_act = project(grad_rows_m, mlp_w, 2 * ff_width, 3 * ff_width)
            sigmoid_g = jax.nn.sigmoid(gate_part)
            grad_gate = grad_act * up_part * sigmoid_g * (1.0 + gate_part * (1.0 - sigmoid_g))
            grad_up = grad_act * gate_part * sigmoid_g
            grad_gu = jnp.concatenate([grad_gate, grad_up], axis=1).astype(BF16)
            grad_norm_m = to_owner(project_back(grad_gu, mlp_w, 0, 2 * ff_width))
            d_down = weight_scatter(weight_grad(grad_rows_m, activated))
            d_gu = weight_scatter(weight_grad(normed_m, grad_gu))
            grad_res, d_gains[layers + layer] = norm_back(
                grad_res, grad_norm_m, middle, inverse_m, gain_m
            )
            grad_rows_a = both_rows(grad_res.astype(BF16))
            grad_attended = project(grad_rows_a, attn_w, qkv_width, attn_width).astype(BF16)
            d_out = weight_grad(grad_rows_a, attended)
            grad_q, dk_own, dk_sib, dv_own, dv_sib = attend_backward(
                queries, units(grad_attended), lse, kv_own, kv_sib, kpos, qpos, qstart
            )
            dk_back, dv_back = swap_core(dk_sib), swap_core(dv_sib)
            kv_slots = [
                (
                    dk_own[j].astype(F32) + dk_back[j].astype(F32),
                    dv_own[j].astype(F32) + dv_back[j].astype(F32),
                )
                for j in range(chips)
            ]
            grad_k, grad_v = ring_scatter(kv_slots)
            grad_q_pre = rotate_back(
                from_units(grad_q).reshape(token_rows, heads_q, HEAD_SIZE), cosine, sine_table
            )
            grad_k_pre = rotate_back(
                grad_k.T.reshape(token_rows, heads_kv, HEAD_SIZE), cosine, sine_table
            )
            grad_qkv = jnp.concatenate(
                [
                    (grad_q_pre * scale_q).reshape(token_rows, q_width),
                    grad_k_pre.reshape(token_rows, kv_width),
                    grad_v.T,
                ],
                axis=1,
            ).astype(BF16)
            grad_norm_a = to_owner(project_back(grad_qkv, attn_w, 0, qkv_width))
            d_qkv = weight_grad(normed_a, grad_qkv)
            d_attn[layer] = weight_scatter(jnp.concatenate([d_qkv, d_out], axis=1))
            d_mlp[layer] = (d_gu, d_down)
            grad_res, d_gains[layer] = norm_back(
                grad_res, grad_norm_a, residual_in, inverse_a, gain_a
            )
        d_hidden = restore(grad_res)
        d_gains = restore(jnp.stack(d_gains, axis=0))
        d_gains = lax.psum_scatter(d_gains, "ctx", scatter_dimension=1, tiled=True)
        d_gains = d_gains + swap_head(d_gains)
        k_at, v_at = q_width, q_width + kv_width

        def stack(parts):
            return jnp.stack(parts, axis=0)

        return (
            out_hidden,
            d_hidden,
            d_gains[:layers],
            stack([part[:, :k_at] for part in d_attn]),
            stack([part[:, k_at:v_at] for part in d_attn]),
            stack([part[:, v_at:qkv_width] for part in d_attn]),
            stack([part[:, qkv_width:].T for part in d_attn]),
            d_gains[layers:],
            stack([part[0][:, :ff_width] for part in d_mlp]),
            stack([part[0][:, ff_width:] for part in d_mlp]),
            stack([part[1].T for part in d_mlp]),
        )

    return local


def solution(mesh):
    return jax.shard_map(
        build(mesh.shape["ctx"]),
        mesh=mesh,
        in_specs=(
            P(("ctx", "head"), None),
            P(),
            P(),
            P(None, "ctx"),
            P(None, "ctx", "head"),
            P(None, "ctx", "head"),
            P(None, "ctx", "head"),
            P(None, "head", "ctx"),
            P(None, "ctx"),
            P(None, "ctx", "head"),
            P(None, "ctx", "head"),
            P(None, "head", "ctx"),
            P(("ctx", "head"), None),
        ),
        out_specs=(
            P(("ctx", "head"), None),
            P(("ctx", "head"), None),
            P(None, "ctx"),
            P(None, "ctx", "head"),
            P(None, "ctx", "head"),
            P(None, "ctx", "head"),
            P(None, "head", "ctx"),
            P(None, "ctx"),
            P(None, "ctx", "head"),
            P(None, "ctx", "head"),
            P(None, "head", "ctx"),
        ),
        check_vma=False,
    )
```

```python
import functools
import math

import jax
import jax.numpy as jnp
from jax import lax
from jax.experimental import pallas as pl
from jax.experimental.pallas import tpu as pltpu
from jax.sharding import PartitionSpec as P

HEAD_SIZE = 96
HALF = HEAD_SIZE // 2
SEQS = 2
BLK = 64
ROWS = 2 * BLK

NEG = -1e30
EPS = 1e-05
THETA = 100000.0
VMEM_LIMIT = 56 * 1024 * 1024
KERNEL_VMEM = 62 * 1024 * 1024
MESH = pl.DeviceIdType.MESH
BF16 = jnp.bfloat16
F32 = jnp.float32


def ring_of(chips):
    return list(range(0, chips, 2)) + list(range(chips - 1, 0, -2))


def rope_tables(positions):
    freq_row = jnp.exp(jnp.arange(HALF, dtype=F32) * (-2.0 * math.log(THETA) / HEAD_SIZE))
    angles = positions.astype(F32)[:, None] * freq_row[None, :]
    return (jnp.cos(angles), jnp.sin(angles))


def rotate(tensor, cosine, sine_table):
    first, second = tensor[..., :HALF], tensor[..., HALF:]
    cos_wide, sin_wide = cosine[:, None, :], sine_table[:, None, :]
    return jnp.concatenate(
        [first * cos_wide - second * sin_wide, second * cos_wide + first * sin_wide], axis=-1
    )


def rotate_back(tensor, cosine, sine_table):
    first, second = tensor[..., :HALF], tensor[..., HALF:]
    cos_wide, sin_wide = cosine[:, None, :], sine_table[:, None, :]
    return jnp.concatenate(
        [first * cos_wide + second * sin_wide, second * cos_wide - first * sin_wide], axis=-1
    )


def dot(left, right):
    return jnp.dot(left, right, preferred_element_type=F32)


def dot_nt(left, right):
    return lax.dot_general(left, right, (((1,), (1,)), ((), ())), preferred_element_type=F32)


def dot_tn(left, right):
    return lax.dot_general(left, right, (((0,), (0,)), ((), ())), preferred_element_type=F32)


def row_tile(keys):
    return 256 if keys <= 2048 else 64


def gathered(ref):
    return jnp.concatenate([ref[j] for j in range(ref.shape[0])], axis=1)


def mask_rows(kpos_ref, qpos_ref, qstart_ref, start, rows):
    kpos = kpos_ref[0]
    parts = []
    done = 0
    while done < rows:
        at = (start + done) % ROWS
        size = min(rows - done, ROWS - at)
        qpos = qpos_ref[0, at : at + size, :]
        qstart = qstart_ref[0, at : at + size, :]
        parts.append((kpos <= qpos) & (kpos >= qstart))
        done += size
    return parts


def masked(scores, parts):
    out = []
    at = 0
    for part in parts:
        size = part.shape[0]
        out.append(jnp.where(part, scores[at : at + size, :], NEG))
        at += size
    return jnp.concatenate(out, axis=0) if len(out) > 1 else out[0]


def attend_kernel(q_ref, k_ref, v_ref, kpos_ref, qpos_ref, qstart_ref, o_ref, lse_ref):
    total = q_ref.shape[2]
    kt = gathered(k_ref)
    vt = gathered(v_ref)
    tile = min(total, row_tile(kt.shape[1]))
    for at in range(0, total, tile):
        q = q_ref[0, 0, at : at + tile, :]
        scores = masked(dot(q, kt), mask_rows(kpos_ref, qpos_ref, qstart_ref, at, tile))
        top = jnp.max(scores, axis=1, keepdims=True)
        weights = jnp.exp(scores - top)
        norm = jnp.sum(weights, axis=1, keepdims=True)
        probs = (weights * (1.0 / norm)).astype(BF16)
        o_ref[0, 0, at : at + tile, :] = dot_nt(probs, vt).astype(BF16)
        lse_ref[0, 0, at : at + tile, :] = top + jnp.log(norm)


def attend_back_kernel(
    q_ref,
    do_ref,
    lse_ref,
    k_ref,
    v_ref,
    kpos_ref,
    qpos_ref,
    qstart_ref,
    dq_ref,
    dk_ref,
    dv_ref,
):
    total = q_ref.shape[2]
    kt = gathered(k_ref)
    vt = gathered(v_ref)
    tile = min(total, row_tile(kt.shape[1]))
    dkt = None
    dvt = None
    for at in range(0, total, tile):
        q = q_ref[0, 0, at : at + tile, :]
        grad = do_ref[0, 0, at : at + tile, :]
        scores = masked(dot(q, kt), mask_rows(kpos_ref, qpos_ref, qstart_ref, at, tile))
        probs = jnp.exp(scores - lse_ref[0, 0, at : at + tile, :])
        dprobs = dot(grad, vt)
        delta = jnp.sum(probs * dprobs, axis=1, keepdims=True)
        dscores = (probs * (dprobs - delta)).astype(BF16)
        dq_ref[0, 0, at : at + tile, :] = dot_nt(dscores, kt)
        dk_part = dot_tn(q, dscores)
        dv_part = dot_tn(grad, probs.astype(BF16))
        dkt = dk_part if dkt is None else dkt + dk_part
        dvt = dv_part if dvt is None else dvt + dv_part
    for j in range(dk_ref.shape[0]):
        dk_ref[j] = dkt[:, j * ROWS : (j + 1) * ROWS].astype(BF16)
        dv_ref[j] = dvt[:, j * ROWS : (j + 1) * ROWS].astype(BF16)


def attention_specs(q, kv, kpos):
    slots = kv.shape[0]
    kv_heads = kv.shape[1] // (2 * HEAD_SIZE)
    keys = kpos.shape[2]
    rows = q.shape[2]
    unit = pl.BlockSpec((1, 1, rows, HEAD_SIZE), lambda s, h: (s, h, 0, 0))
    column = pl.BlockSpec((1, 1, rows, 1), lambda s, h: (s, h, 0, 0))
    k_spec = pl.BlockSpec((slots, HEAD_SIZE, ROWS), lambda s, h: (0, h, s))
    v_spec = pl.BlockSpec((slots, HEAD_SIZE, ROWS), lambda s, h: (0, kv_heads + h, s))
    kpos_spec = pl.BlockSpec((1, 1, keys), lambda s, h: (s, 0, 0))
    q_spec = pl.BlockSpec((1, ROWS, 1), lambda s, h: (s, 0, 0))
    return kv_heads, unit, column, k_spec, v_spec, kpos_spec, q_spec


def attend_forward(q, kv, kpos, qpos, qstart):
    kv_heads, unit, column, k_spec, v_spec, kpos_spec, q_spec = attention_specs(q, kv, kpos)
    rows, keys = q.shape[2], kpos.shape[2]
    work = SEQS * kv_heads * rows * keys
    return pl.pallas_call(
        attend_kernel,
        grid=(SEQS, kv_heads),
        in_specs=[unit, k_spec, v_spec, kpos_spec, q_spec, q_spec],
        out_specs=[unit, column],
        out_shape=[
            jax.ShapeDtypeStruct(q.shape, BF16),
            jax.ShapeDtypeStruct(q.shape[:3] + (1,), F32),
        ],
        compiler_params=pltpu.CompilerParams(vmem_limit_bytes=VMEM_LIMIT),
        cost_estimate=pl.CostEstimate(
            flops=8 * HEAD_SIZE * work, bytes_accessed=8 * 2**20, transcendentals=work
        ),
    )(q, kv, kv, kpos, qpos, qstart)


def attend_backward(q, grad, lse, kv, kpos, qpos, qstart):
    kv_heads, unit, column, k_spec, v_spec, kpos_spec, q_spec = attention_specs(q, kv, kpos)
    rows, keys = q.shape[2], kpos.shape[2]
    work = SEQS * kv_heads * rows * keys
    slots = kv.shape[0]
    grad_spec = pl.BlockSpec((slots, HEAD_SIZE, ROWS), lambda s, h: (0, h, s))
    grad_shape = jax.ShapeDtypeStruct((slots, kv_heads * HEAD_SIZE, SEQS * ROWS), BF16)
    return pl.pallas_call(
        attend_back_kernel,
        grid=(SEQS, kv_heads),
        in_specs=[unit, unit, column, k_spec, v_spec, kpos_spec, q_spec, q_spec],
        out_specs=[unit, grad_spec, grad_spec],
        out_shape=[jax.ShapeDtypeStruct(q.shape, F32)] + [grad_shape] * 2,
        compiler_params=pltpu.CompilerParams(vmem_limit_bytes=VMEM_LIMIT),
        cost_estimate=pl.CostEstimate(
            flops=20 * HEAD_SIZE * work, bytes_accessed=16 * 2**20, transcendentals=work
        ),
    )(q, grad, lse, kv, kv, kpos, qpos, qstart)


def ring_neighbours(chips):
    ctx = lax.axis_index("ctx")
    chip, core, half = ctx // 2, ctx % 2, chips // 2
    odd = chip % 2
    place = odd * (chips - 1 - chip // 2) + (1 - odd) * (chip // 2)

    def device(at):
        far = at // half
        return ((1 - far) * 2 * at + far * (2 * (chips - 1 - at) + 1)) * 2 + core

    return device((place + 1) % chips), device((place + chips - 1) % chips), ctx + 1 - 2 * core


class Links:
    def __init__(self, chips, send_sems, recv_sems):
        self.chips = chips
        self.right, self.left, self.sib = ring_neighbours(chips)
        self.head = lax.axis_index("head")
        self.ctx = lax.axis_index("ctx")
        self.send_sems, self.recv_sems = send_sems, recv_sems
        self.used = 0
        self.started = []

    def greet(self):
        barrier = pltpu.get_barrier_semaphore()
        for target in (self.right, self.left, self.sib):
            pl.semaphore_signal(barrier, inc=1, device_id=(target, self.head), device_id_type=MESH)
        pl.semaphore_signal(
            barrier, inc=1, device_id=(self.ctx, 1 - self.head), device_id_type=MESH
        )
        pl.semaphore_wait(barrier, 4)

    def copy(self, src, dst, target):
        copy = pltpu.make_async_remote_copy(
            src_ref=src,
            dst_ref=dst,
            send_sem=self.send_sems.at[self.used],
            recv_sem=self.recv_sems.at[self.used],
            device_id=target,
            device_id_type=MESH,
        )
        self.used += 1
        copy.start()
        self.started.append(copy)
        return copy

    def to_right(self, src, dst):
        return self.copy(src, dst, (self.right, self.head))

    def to_left(self, src, dst):
        return self.copy(src, dst, (self.left, self.head))

    def to_sibling(self, src, dst):
        return self.copy(src, dst, (self.sib, self.head))

    def to_head(self, src, dst):
        return self.copy(src, dst, (self.ctx, 1 - self.head))

    def finish(self):
        for copy in self.started:
            copy.wait_send()


class RingGather:
    def __init__(self, links, ref, chains, first=None):
        self.links, self.ref, self.chains = links, ref, chains
        self.first = first
        self.moving = {}
        self.arriving = []
        self.steps = links.chips // 2
        self.events = [(c, s) for s in range(1, self.steps + 1) for c in range(len(chains))]

    @staticmethod
    def copies(chips, chains):
        return chains * (chips + chips)

    def window(self, slot, chain, part=None):
        r0, rn, c0, cn = self.chains[chain]
        if part is not None:
            rn = rn // 2
            r0 = r0 + part * rn
        if slot == 0 and self.first is not None:
            return self.first.at[pl.ds(r0, rn), pl.ds(c0, cn)]
        return self.ref.at[slot, pl.ds(r0, rn), pl.ds(c0, cn)]

    def share(self, slot, chain):
        r0, rn, c0, cn = self.chains[chain]
        there = self.ref.at[self.links.chips + slot, pl.ds(r0, rn), pl.ds(c0, cn)]
        self.arriving.append(self.links.to_sibling(self.window(slot, chain), there))

    def issue(self, event):
        chain, step = event
        chips = self.links.chips
        last = step == self.steps
        up_from, up_to = (chips - step + 1) % chips, chips - step
        r0, rn, c0, cn = self.chains[chain]

        def there(slot, part):
            rows = (r0, rn) if part is None else (r0 + part * (rn // 2), rn // 2)
            return self.ref.at[slot, pl.ds(*rows), pl.ds(c0, cn)]

        up = 0 if last else None
        down = 1 if last else None
        self.moving[event] = (
            self.links.to_right(self.window(up_from, chain, up), there(up_to, up)),
            self.links.to_left(self.window(step - 1, chain, down), there(step, down)),
        )
        if step == 1:
            self.share(0, chain)

    def land(self, event):
        chain, step = event
        for copy in self.moving[event]:
            copy.wait_recv()
        self.share(self.links.chips - step, chain)
        if step != self.steps:
            self.share(step, chain)

    def settle(self):
        for copy in self.arriving:
            copy.wait_recv()


class Queue:
    def __init__(self, rings, depth=2):
        self.items = [(ring, event) for ring in rings for event in ring.events]
        self.depth = depth
        self.landed = 0
        self.issued = 0

    def fill(self):
        while self.issued < len(self.items) and self.issued < self.landed + self.depth:
            ring, event = self.items[self.issued]
            ring.issue(event)
            self.issued += 1

    def pump(self, count=1):
        for _ in range(count):
            if self.landed < len(self.items):
                ring, event = self.items[self.landed]
                ring.land(event)
                self.landed += 1
                self.fill()

    def through(self, ring):
        last = max(i for i, item in enumerate(self.items) if item[0] is ring)
        self.pump(last + 1 - self.landed)


TILE = 512


def rms_inverse(rows):
    return lax.rsqrt(jnp.mean(rows * rows, axis=-1, keepdims=True) + EPS)


def forward_kernel(dims, *refs):
    layers, chips, width, q_width, kv_width, ff = dims
    slots = 2 * chips
    it = iter(refs)
    x_ref = next(it)
    shards = [next(it) for _ in range(2 * layers)]
    cos_ref, sin_ref, kpos_ref, qpos_ref, qstart_ref = (next(it) for _ in range(5))
    weights = [next(it) for _ in range(2 * layers)]
    (
        kv_ref,
        normed_a_ref,
        qt_ref,
        lse_ref,
        att_ref,
        middle_ref,
        normed_m_ref,
        gate_ref,
        up_ref,
        act_ref,
        x_out_ref,
        gain_ref,
    ) = (next(it) for _ in range(12))
    (
        wt, wo, acc, proj_t, att_t, b_send, b_recv, gain_block, send_sems, recv_sems, load_sems, own_sems
    ) = (next(it) for _ in range(12))

    rows = x_ref.shape[0]
    db = width // slots
    heads_kv = kv_width // HEAD_SIZE
    group = q_width // kv_width
    qkv_width = q_width + 2 * kv_width
    links = Links(chips, send_sems, recv_sems)
    own_copies = []
    for i, (shard, weight) in enumerate(zip(shards, weights)):
        own_copies.append(pltpu.make_async_copy(shard, weight.at[0], own_sems.at[i]))
        own_copies[-1].start()
    links.greet()

    rings = []
    for shard, weight in zip(shards, weights):
        wide = shard.shape[1]
        cut = (wide // 256) * 128
        rings.append(
            RingGather(links, weight, [(0, db, 0, cut), (0, db, cut, wide - cut)], first=shard)
        )
    queue = Queue(rings)
    queue.fill()

    def ready(i):
        queue.through(rings[i])
        rings[i].settle()

    def load(i, column, wide, target, sem):
        copy = pltpu.make_async_copy(
            weights[i].at[:, :, pl.ds(column, wide)], target, load_sems.at[sem]
        )
        copy.start()
        return copy

    def flat(ref):
        return ref[...].reshape(width, ref.shape[-1])

    ready(0)
    for copy in own_copies:
        copy.wait()
    side = qkv_width + q_width
    load(0, side, 128, gain_block, 0).wait()
    gain_ref[...] = flat(gain_block).astype(F32).T[: gain_ref.shape[0], :]

    for layer in range(layers):
        attn, mlp = 2 * layer, 2 * layer + 1
        if layer:
            ready(attn)
        tiles = [load(attn, t * TILE, TILE, wt.at[t], t) for t in range(qkv_width // TILE)]
        out_load = load(attn, qkv_width, q_width, wo, 6)

        x = x_ref[...] if layer == 0 else x_out_ref[layer - 1]
        gain_a = gain_ref[layer : layer + 1, :]
        normed_a_ref[layer, 0:rows, :] = (x * rms_inverse(x) * gain_a).astype(BF16)
        swap = links.to_head(
            normed_a_ref.at[layer, pl.ds(0, rows), :], normed_a_ref.at[layer, pl.ds(rows, rows), :]
        )
        for t, tile in enumerate(tiles):
            tile.wait()
            part = dot(normed_a_ref[layer, 0:rows, :], flat(wt.at[t]))
            proj_t[t * TILE : (t + 1) * TILE, 0:rows] = part.T
        swap.wait_recv()
        for t in range(len(tiles)):
            part = dot(normed_a_ref[layer, rows : 2 * rows, :], flat(wt.at[t]))
            proj_t[t * TILE : (t + 1) * TILE, rows : 2 * rows] = part.T
        queue.pump()

        cosine, sine = cos_ref[...], sin_ref[...]

        def turned(at):
            low = proj_t[at : at + HALF, :]
            high = proj_t[at + HALF : at + HEAD_SIZE, :]
            return low * cosine - high * sine, high * cosine + low * sine

        for h in range(heads_kv):
            low, high = turned(q_width + h * HEAD_SIZE)
            kv_ref[layer, 0, h * HEAD_SIZE : h * HEAD_SIZE + HALF, :] = low.astype(BF16)
            kv_ref[layer, 0, h * HEAD_SIZE + HALF : (h + 1) * HEAD_SIZE, :] = high.astype(BF16)
        kv_ref[layer, 0, kv_width : 2 * kv_width, :] = proj_t[
            q_width + kv_width : qkv_width, :
        ].astype(BF16)
        wide = kv_ref.shape[-1]
        kv_ring = RingGather(
            links,
            kv_ref.at[layer],
            [(0, kv_width, 0, wide), (kv_width, kv_width, 0, wide)],
        )
        kv_queue = Queue([kv_ring])
        kv_queue.fill()
        scale = HEAD_SIZE ** (-0.5)
        for h in range(q_width // HEAD_SIZE):
            low, high = turned(h * HEAD_SIZE)
            qt_ref[layer, h * HEAD_SIZE : h * HEAD_SIZE + HALF, :] = (low * scale).astype(BF16)
            qt_ref[layer, h * HEAD_SIZE + HALF : (h + 1) * HEAD_SIZE, :] = (high * scale).astype(
                BF16
            )
        for step in range(len(kv_queue.items)):
            kv_queue.pump()
            if step % 3 == 2:
                queue.pump()
        kv_ring.settle()

        def unit(u, carry):
            s, h = u // heads_kv, u % heads_kv
            k_rows = pl.ds(pl.multiple_of(h * HEAD_SIZE, HEAD_SIZE), HEAD_SIZE)
            v_rows = pl.ds(pl.multiple_of(kv_width + h * HEAD_SIZE, HEAD_SIZE), HEAD_SIZE)
            lanes = pl.ds(pl.multiple_of(s * ROWS, ROWS), ROWS)
            kt = jnp.concatenate([kv_ref[layer, j, k_rows, lanes] for j in range(slots)], axis=1)
            vt = jnp.concatenate([kv_ref[layer, j, v_rows, lanes] for j in range(slots)], axis=1)
            q_rows = [
                pl.ds(pl.multiple_of((h * group + g) * HEAD_SIZE, HEAD_SIZE), HEAD_SIZE)
                for g in range(group)
            ]
            qt = jnp.concatenate([qt_ref[layer, at, lanes] for at in q_rows], axis=1)
            kpos, qpos, qstart = kpos_ref[s], qpos_ref[s], qstart_ref[s]
            allowed = (kpos <= qpos) & (kpos >= qstart)
            scores = masked(dot_tn(qt, kt), [allowed] * group)
            top = jnp.max(scores, axis=1, keepdims=True)
            raised = jnp.exp(scores - top)
            norm = jnp.sum(raised, axis=1, keepdims=True)
            probs = (raised * (1.0 / norm)).astype(BF16)
            mixed = dot_nt(vt, probs)
            for g, at in enumerate(q_rows):
                att_t[at, lanes] = mixed[:, g * ROWS : (g + 1) * ROWS]
            lse_ref[layer, u] = top + jnp.log(norm)
            return carry

        units = SEQS * heads_kv
        for at in range(0, units, 2):
            lax.fori_loop(at, at + 2, unit, 0)
            queue.pump()
        att_ref[layer] = att_t[...].T.astype(BF16)

        out_load.wait()
        branch = (layer * 2) % b_send.shape[0]
        other = dot_nt(att_ref[layer, rows : 2 * rows, :], flat(wo))
        b_send[branch] = other.astype(BF16)
        swap = links.to_head(b_send.at[branch], b_recv.at[branch])
        mine = dot_nt(att_ref[layer, 0:rows, :], flat(wo))
        queue.pump()
        swap.wait_recv()
        middle = x + mine + b_recv[branch].astype(F32)
        middle_ref[layer] = middle
        gain_m = gain_ref[layers + layer : layers + layer + 1, :]
        normed_m_ref[layer, 0:rows, :] = (middle * rms_inverse(middle) * gain_m).astype(BF16)
        swap = links.to_head(
            normed_m_ref.at[layer, pl.ds(0, rows), :], normed_m_ref.at[layer, pl.ds(rows, rows), :]
        )
        ready(mlp)

        def load_tile(t):
            at = (t % 2) * 3
            return [
                load(mlp, part * ff + t * TILE, TILE, wt.at[at + part], at + part)
                for part in range(3)
            ]

        pending = load_tile(0)
        swap.wait_recv()
        normed = normed_m_ref[layer]
        count = ff // TILE
        for t in range(count):
            following = load_tile(t + 1) if t + 1 < count else None
            for copy in pending:
                copy.wait()
            at = (t % 2) * 3
            columns = slice(t * TILE, (t + 1) * TILE)
            gate = dot(normed, flat(wt.at[at]))
            up = dot(normed, flat(wt.at[at + 1]))
            act = (gate * jax.nn.sigmoid(gate) * up).astype(BF16)
            gate_ref[layer, :, columns] = gate.astype(BF16)
            up_ref[layer, :, columns] = up.astype(BF16)
            act_ref[layer, :, columns] = act
            down = dot_nt(act, flat(wt.at[at + 2]))
            if t == 0:
                acc[...] = down
            else:
                acc[...] += down
            pending = following
            queue.pump(2)
        branch = (layer * 2 + 1) % b_send.shape[0]
        b_send[branch] = acc[rows : 2 * rows, :].astype(BF16)
        swap = links.to_head(b_send.at[branch], b_recv.at[branch])
        swap.wait_recv()
        x_out_ref[layer] = middle_ref[layer] + acc[0:rows, :] + b_recv[branch].astype(F32)
    links.finish()


def forward(x, shards, cosine, sine, kpos, qpos, qstart, chips, q_width, kv_width, ff):
    layers = len(shards) // 2
    rows, width = x.shape
    db = shards[0].shape[0]
    slots = 2 * chips
    group = q_width // kv_width
    tokens = 2 * rows
    units = SEQS * kv_width // HEAD_SIZE
    dims = (layers, chips, width, q_width, kv_width, ff)
    copies = (2 * layers + layers) * RingGather.copies(chips, 2) + 4 * layers
    any_spec = pl.BlockSpec(memory_space=pl.ANY)
    vmem = pl.BlockSpec(memory_space=pltpu.VMEM)
    saved = [
        jax.ShapeDtypeStruct((layers, slots, 2 * kv_width, tokens), BF16),
        jax.ShapeDtypeStruct((layers, tokens, width), BF16),
        jax.ShapeDtypeStruct((layers, q_width, tokens), BF16),
        jax.ShapeDtypeStruct((layers, units, group * ROWS, 1), F32),
        jax.ShapeDtypeStruct((layers, tokens, q_width), BF16),
        jax.ShapeDtypeStruct((layers, rows, width), F32),
        jax.ShapeDtypeStruct((layers, tokens, width), BF16),
        jax.ShapeDtypeStruct((layers, tokens, ff), BF16),
        jax.ShapeDtypeStruct((layers, tokens, ff), BF16),
        jax.ShapeDtypeStruct((layers, tokens, ff), BF16),
        jax.ShapeDtypeStruct((layers, rows, width), F32),
        jax.ShapeDtypeStruct((2 * layers, width), F32),
    ]
    out = pl.pallas_call(
        functools.partial(forward_kernel, dims),
        out_shape=[jax.ShapeDtypeStruct((slots,) + shard.shape, BF16) for shard in shards] + saved,
        in_specs=[vmem] + [any_spec] * len(shards) + [vmem] * 5,
        out_specs=[any_spec] * len(shards) + [vmem] * len(saved),
        scratch_shapes=[
            pltpu.VMEM((6, slots, db, TILE), BF16),
            pltpu.VMEM((slots, db, q_width), BF16),
            pltpu.VMEM((tokens, width), F32),
            pltpu.VMEM((q_width + 2 * kv_width, tokens), F32),
            pltpu.VMEM((q_width, tokens), F32),
            pltpu.VMEM((2 * layers, rows, width), BF16),
            pltpu.VMEM((2 * layers, rows, width), BF16),
            pltpu.VMEM((slots, db, 128), BF16),
            pltpu.SemaphoreType.DMA((copies,)),
            pltpu.SemaphoreType.DMA((copies,)),
            pltpu.SemaphoreType.DMA((7,)),
            pltpu.SemaphoreType.DMA((len(shards),)),
        ],
        compiler_params=pltpu.CompilerParams(
            collective_id=0, has_side_effects=True, vmem_limit_bytes=KERNEL_VMEM
        ),
    )(x, *shards, cosine, sine, kpos, qpos, qstart)
    return out[: len(shards)], out[len(shards) :]


def build(n_ctx):
    chips = n_ctx // 2
    ring = ring_of(chips)

    def shifted(step):
        pairs = []
        for at, chip in enumerate(ring):
            target = ring[(at + step) % chips]
            pairs += [(chip * 2 + core, target * 2 + core) for core in range(2)]
        return pairs

    up, down = shifted(1), shifted(-1)
    sibling = [(i, i ^ 1) for i in range(n_ctx)]

    def send_up(value):
        return lax.ppermute(value, "ctx", up)

    def send_down(value):
        return lax.ppermute(value, "ctx", down)

    def swap_core(value):
        return lax.ppermute(value, "ctx", sibling)

    def swap_head(value):
        return lax.ppermute(value, "head", [(0, 1), (1, 0)])

    def ring_gather(shard):
        got = {0: shard}
        low, high = shard, shard
        half = chips // 2
        for step in range(1, half):
            low, high = send_up(low), send_down(high)
            got[chips - step] = low
            got[step] = high
        cut = shard.shape[0] // 2
        got[half] = jnp.concatenate([send_up(low[:cut]), send_down(high[cut:])], axis=0)
        return [got[j] for j in range(chips)]

    def ring_scatter(slots):
        low = slots[chips - 1][0].astype(BF16)
        high = slots[1][1].astype(BF16)
        for step in range(1, chips):
            low, high = send_up(low), send_down(high)
            own_low = slots[(chips - 1 - step) % chips][0].astype(F32)
            own_high = slots[(1 + step) % chips][1].astype(F32)
            low, high = low.astype(F32) + own_low, high.astype(F32) + own_high
            if step < chips - 1:
                low, high = low.astype(BF16), high.astype(BF16)
        return low, high

    def gather(shard):
        own = jnp.concatenate(ring_gather(shard), axis=0)
        return jnp.concatenate([own, swap_core(own)], axis=0)

    def weight_scatter(grad):
        db, cut = grad.shape[0] // chips, grad.shape[1] // 2
        slots = [
            (grad[j * db : (j + 1) * db, :cut], grad[j * db : (j + 1) * db, cut:])
            for j in range(chips)
        ]
        return jnp.concatenate(ring_scatter(slots), axis=1)

    def local(
        hidden_in,
        block_order,
        doc_ids,
        attn_gain,
        w_query,
        w_key,
        w_value,
        w_out,
        mlp_gain,
        w_gate,
        w_up,
        w_down,
        cotangent,
    ):
        layers, db = w_query.shape[0], w_query.shape[1]
        width = db * n_ctx
        side = width // 2
        q_width, kv_width, ff_width = w_query.shape[2], w_key.shape[2], w_gate.shape[2]
        heads_q, heads_kv = q_width // HEAD_SIZE, kv_width // HEAD_SIZE
        group = heads_q // heads_kv
        own_rows = hidden_in.shape[0]
        token_rows = own_rows * 2
        ctx = lax.axis_index("ctx")
        head = lax.axis_index("head")
        core = ctx % 2
        place_of = [0] * chips
        for at, chip in enumerate(ring):
            place_of[chip] = at
        place = jnp.array(place_of, jnp.int32)[ctx // 2]

        slot_ids = jnp.arange(n_ctx, dtype=jnp.int32)
        along = (place + slot_ids % chips) % chips
        chip_of = jnp.where(along < chips // 2, 2 * along, 2 * (chips - 1 - along) + 1)
        block_of = chip_of * 2 + (core + slot_ids // chips) % 2
        block_hot = (block_of[:, None] == slot_ids[None, :]).astype(F32)
        feature = jnp.arange(width, dtype=jnp.int32)
        wanted = jnp.repeat(block_of, db) * db + feature % db
        to_ring = (feature[:, None] == wanted[None, :]).astype(BF16)

        def reorder(rows):
            return dot(rows, to_ring)

        def restore(rows):
            return lax.dot_general(
                rows,
                to_ring.astype(F32),
                (((1,), (1,)), ((), ())),
                precision=lax.Precision.HIGHEST,
                preferred_element_type=F32,
            )

        offsets = jnp.arange(BLK, dtype=jnp.int32)
        first = (head == 0)[..., None, None]
        order = jnp.where(first, block_order, block_order[::-1])
        docs = jnp.where(first, doc_ids, doc_ids[::-1])
        own_blocks = lax.dynamic_slice(order, (jnp.int32(0), 2 * ctx), (SEQS, 2))
        q_positions = (own_blocks[:, :, None] * BLK + offsets[None, None, :]).reshape(SEQS, ROWS)
        ring_blocks = jnp.einsum(
            "ac,scb->sab", block_hot, order.reshape(SEQS, n_ctx, 2).astype(F32)
        ).astype(jnp.int32)
        k_positions = (ring_blocks[..., None] * BLK + offsets).reshape(SEQS, 1, n_ctx * ROWS)
        doc_blocks = docs.reshape(SEQS, -1, BLK)
        own_hot = (own_blocks[:, :, None] == jnp.arange(doc_blocks.shape[1])).astype(F32)
        q_docs = jnp.einsum("sab,sbj->saj", own_hot, doc_blocks.astype(F32)).astype(jnp.int32)
        q_docs = q_docs.reshape(SEQS, ROWS)
        q_starts = jnp.sum((docs[:, None, :] < q_docs[:, :, None]).astype(jnp.int32), axis=2)
        kpos = k_positions
        qpos, qstart = q_positions[:, :, None], q_starts[:, :, None]
        cosine, sine_table = rope_tables(q_positions.reshape(token_rows))
        scale_q = HEAD_SIZE ** (-0.5)

        def both_rows(rows):
            return jnp.concatenate([rows, swap_head(rows)], axis=0)

        def to_owner(parts):
            return parts[:own_rows] + swap_head(parts[own_rows:].astype(BF16)).astype(F32)

        def project(rows, weight, lo, hi):
            return dot(rows, weight[:, lo:hi])

        def project_back(rows, weight, lo, hi):
            return dot_nt(rows, weight[:, lo:hi])

        def weight_grad(left, right):
            lefts = jnp.concatenate([left[:, :side], swap_core(left[:, side:])], axis=0)
            rights = jnp.concatenate([right, swap_core(right)], axis=0)
            return dot_tn(lefts, rights)

        def units(rows):
            shaped = rows.reshape(SEQS, ROWS, heads_kv, group, HEAD_SIZE)
            return shaped.transpose(0, 2, 3, 1, 4).reshape(SEQS, heads_kv, group * ROWS, HEAD_SIZE)

        def from_units(parts):
            shaped = parts.reshape(SEQS, heads_kv, group, ROWS, HEAD_SIZE)
            return shaped.transpose(0, 3, 1, 2, 4).reshape(token_rows, q_width)

        qkv_width = q_width + 2 * kv_width
        attn_width = qkv_width + q_width
        grad_res = reorder(cotangent)
        attn_shards = [
            jnp.concatenate(
                [w_query[layer], w_key[layer], w_value[layer], w_out[layer].T], axis=1
            )
            for layer in range(layers)
        ]
        mlp_shards = [
            jnp.concatenate([w_gate[layer], w_up[layer], w_down[layer].T], axis=1)
            for layer in range(layers)
        ]

        def forward_by_ops(residual):
            gains = lax.all_gather(
                jnp.concatenate([attn_gain, mlp_gain], axis=0), "ctx", axis=1, tiled=True
            )
            gains = reorder(gains)
            fetched = [
                (gather(attn), gather(mlp)) for attn, mlp in zip(attn_shards, mlp_shards)
            ]
            records = []
            for layer in range(layers):
                attn_w, mlp_w = fetched[layer]
                gain_a, gain_m = gains[layer], gains[layers + layer]
                residual_in = residual
                normed_a = both_rows((residual * rms_inverse(residual) * gain_a).astype(BF16))
                projected = project(normed_a, attn_w, 0, qkv_width)
                q_rows = rotate(
                    projected[:, :q_width].reshape(token_rows, heads_q, HEAD_SIZE),
                    cosine,
                    sine_table,
                )
                queries = units((q_rows * scale_q).astype(BF16).reshape(token_rows, q_width))
                keys = rotate(
                    projected[:, q_width : q_width + kv_width].reshape(
                        token_rows, heads_kv, HEAD_SIZE
                    ),
                    cosine,
                    sine_table,
                ).reshape(token_rows, kv_width)
                kv_shard = jnp.concatenate([keys, projected[:, q_width + kv_width :]], axis=1)
                kv_own = jnp.stack(ring_gather(kv_shard.astype(BF16).T), axis=0)
                kv = jnp.concatenate([kv_own, swap_core(kv_own)], axis=0)
                mixed, lse = attend_forward(queries, kv, kpos, qpos, qstart)
                attended = from_units(mixed)
                middle = residual + to_owner(
                    project_back(attended, attn_w, qkv_width, attn_width)
                )
                normed_m = both_rows((middle * rms_inverse(middle) * gain_m).astype(BF16))
                gate_up = project(normed_m, mlp_w, 0, 2 * ff_width)
                gate_part, up_part = gate_up[:, :ff_width], gate_up[:, ff_width:]
                activated = (jax.nn.silu(gate_part) * up_part).astype(BF16)
                residual = middle + to_owner(
                    project_back(activated, mlp_w, 2 * ff_width, 3 * ff_width)
                )
                records.append(
                    (
                        residual_in,
                        normed_a,
                        queries,
                        kv,
                        lse,
                        attended,
                        middle,
                        normed_m,
                        gate_part,
                        up_part,
                        activated,
                    )
                )
            return fetched, gains, records, residual

        def forward_by_kernel(residual):
            columns = jnp.concatenate([attn_gain, mlp_gain], axis=0).T
            columns = jnp.pad(columns, ((0, 0), (0, 128 - columns.shape[1])))
            shards = []
            for layer in range(layers):
                attn = attn_shards[layer]
                if layer == 0:
                    attn = jnp.concatenate([attn, columns], axis=1)
                shards += [attn, mlp_shards[layer]]
            weights, saved = forward(
                residual,
                shards,
                cosine.T,
                sine_table.T,
                kpos,
                qpos,
                qstart,
                chips,
                q_width,
                kv_width,
                ff_width,
            )
            weights = [weight.reshape(width, weight.shape[-1]) for weight in weights]
            fetched = [(weights[2 * layer], weights[2 * layer + 1]) for layer in range(layers)]
            kv, normed_a, qt, lse, att, middle, normed_m, gate, up, act, x_out, gains = saved
            records = []
            for layer in range(layers):
                q_units = qt[layer].reshape(heads_kv, group, HEAD_SIZE, SEQS, ROWS)
                q_units = q_units.transpose(3, 0, 1, 4, 2)
                records.append(
                    (
                        residual if layer == 0 else x_out[layer - 1],
                        normed_a[layer],
                        q_units.reshape(SEQS, heads_kv, group * ROWS, HEAD_SIZE),
                        kv[layer],
                        lse[layer].reshape(SEQS, heads_kv, group * ROWS, 1),
                        att[layer],
                        middle[layer],
                        normed_m[layer],
                        gate[layer].astype(F32),
                        up[layer].astype(F32),
                        act[layer],
                    )
                )
            return fetched, gains, records, x_out[layers - 1]

        in_kernel = n_ctx * ROWS <= 2048
        run_forward = forward_by_kernel if in_kernel else forward_by_ops
        fetched, gains, records, residual = run_forward(reorder(hidden_in))
        out_hidden = lax.dot_general(
            residual.astype(BF16), to_ring, (((1,), (1,)), ((), ())), preferred_element_type=F32
        ).astype(BF16)

        def norm_back(grad_res, normed_gradient, value_rows, inverse_norm, gain):
            normalized = value_rows * inverse_norm
            gain_gradient = jnp.sum(normed_gradient * normalized, axis=0)
            scaled = normed_gradient * gain
            mean = jnp.mean(scaled * normalized, axis=-1, keepdims=True)
            return grad_res + inverse_norm * (scaled - normalized * mean), gain_gradient

        d_attn = [None] * layers
        d_mlp = [None] * layers
        d_gains = [None] * (2 * layers)
        for layer in reversed(range(layers)):
            attn_w, mlp_w = fetched[layer]
            gain_a, gain_m = gains[layer], gains[layers + layer]
            (
                residual_in,
                normed_a,
                queries,
                kv,
                lse,
                attended,
                middle,
                normed_m,
                gate_part,
                up_part,
                activated,
            ) = records[layer]
            inverse_a, inverse_m = rms_inverse(residual_in), rms_inverse(middle)
            grad_rows_m = both_rows(grad_res.astype(BF16))
            grad_act = project(grad_rows_m, mlp_w, 2 * ff_width, 3 * ff_width)
            sigmoid_g = jax.nn.sigmoid(gate_part)
            grad_gate = grad_act * up_part * sigmoid_g * (1.0 + gate_part * (1.0 - sigmoid_g))
            grad_up = grad_act * gate_part * sigmoid_g
            grad_gu = jnp.concatenate([grad_gate, grad_up], axis=1).astype(BF16)
            grad_norm_m = to_owner(project_back(grad_gu, mlp_w, 0, 2 * ff_width))
            d_down = weight_scatter(weight_grad(grad_rows_m, activated))
            d_gu = weight_scatter(weight_grad(normed_m, grad_gu))
            grad_res, d_gains[layers + layer] = norm_back(
                grad_res, grad_norm_m, middle, inverse_m, gain_m
            )
            grad_rows_a = both_rows(grad_res.astype(BF16))
            grad_attended = project(grad_rows_a, attn_w, qkv_width, attn_width).astype(BF16)
            d_out = weight_grad(grad_rows_a, attended)
            grad_q, dk, dv = attend_backward(
                queries, units(grad_attended), lse, kv, kpos, qpos, qstart
            )
            dk_back, dv_back = swap_core(dk[chips:]), swap_core(dv[chips:])
            kv_slots = [
                (
                    dk[j].astype(F32) + dk_back[j].astype(F32),
                    dv[j].astype(F32) + dv_back[j].astype(F32),
                )
                for j in range(chips)
            ]
            grad_k, grad_v = ring_scatter(kv_slots)
            grad_q_pre = rotate_back(
                from_units(grad_q).reshape(token_rows, heads_q, HEAD_SIZE), cosine, sine_table
            )
            grad_k_pre = rotate_back(
                grad_k.T.reshape(token_rows, heads_kv, HEAD_SIZE), cosine, sine_table
            )
            grad_qkv = jnp.concatenate(
                [
                    (grad_q_pre * scale_q).reshape(token_rows, q_width),
                    grad_k_pre.reshape(token_rows, kv_width),
                    grad_v.T,
                ],
                axis=1,
            ).astype(BF16)
            grad_norm_a = to_owner(project_back(grad_qkv, attn_w, 0, qkv_width))
            d_qkv = weight_grad(normed_a, grad_qkv)
            d_attn[layer] = weight_scatter(jnp.concatenate([d_qkv, d_out], axis=1))
            d_mlp[layer] = (d_gu, d_down)
            grad_res, d_gains[layer] = norm_back(
                grad_res, grad_norm_a, residual_in, inverse_a, gain_a
            )
        d_hidden = restore(grad_res)
        d_gains = restore(jnp.stack(d_gains, axis=0))
        d_gains = lax.psum_scatter(d_gains, "ctx", scatter_dimension=1, tiled=True)
        d_gains = d_gains + swap_head(d_gains)
        k_at, v_at = q_width, q_width + kv_width

        def stack(parts):
            return jnp.stack(parts, axis=0)

        return (
            out_hidden,
            d_hidden,
            d_gains[:layers],
            stack([part[:, :k_at] for part in d_attn]),
            stack([part[:, k_at:v_at] for part in d_attn]),
            stack([part[:, v_at:qkv_width] for part in d_attn]),
            stack([part[:, qkv_width:].T for part in d_attn]),
            d_gains[layers:],
            stack([part[0][:, :ff_width] for part in d_mlp]),
            stack([part[0][:, ff_width:] for part in d_mlp]),
            stack([part[1].T for part in d_mlp]),
        )

    return local


def solution(mesh):
    return jax.shard_map(
        build(mesh.shape["ctx"]),
        mesh=mesh,
        in_specs=(
            P(("ctx", "head"), None),
            P(),
            P(),
            P(None, "ctx"),
            P(None, "ctx", "head"),
            P(None, "ctx", "head"),
            P(None, "ctx", "head"),
            P(None, "head", "ctx"),
            P(None, "ctx"),
            P(None, "ctx", "head"),
            P(None, "ctx", "head"),
            P(None, "head", "ctx"),
            P(("ctx", "head"), None),
        ),
        out_specs=(
            P(("ctx", "head"), None),
            P(("ctx", "head"), None),
            P(None, "ctx"),
            P(None, "ctx", "head"),
            P(None, "ctx", "head"),
            P(None, "ctx", "head"),
            P(None, "head", "ctx"),
            P(None, "ctx"),
            P(None, "ctx", "head"),
            P(None, "ctx", "head"),
            P(None, "head", "ctx"),
        ),
        check_vma=False,
    )
```

```python
import functools
import math

import jax
import jax.numpy as jnp
from jax import lax
from jax.experimental import pallas as pl
from jax.experimental.pallas import tpu as pltpu
from jax.sharding import PartitionSpec as P

HEAD_SIZE = 96
HALF = HEAD_SIZE // 2
SEQS = 2
BLK = 64
ROWS = 2 * BLK

NEG = -1e30
EPS = 1e-05
THETA = 100000.0
VMEM_LIMIT = 56 * 1024 * 1024
KERNEL_VMEM = 62 * 1024 * 1024
MESH = pl.DeviceIdType.MESH
BF16 = jnp.bfloat16
F32 = jnp.float32


def ring_of(chips):
    return list(range(0, chips, 2)) + list(range(chips - 1, 0, -2))


def rope_tables(positions):
    freq_row = jnp.exp(jnp.arange(HALF, dtype=F32) * (-2.0 * math.log(THETA) / HEAD_SIZE))
    angles = positions.astype(F32)[:, None] * freq_row[None, :]
    return (jnp.cos(angles), jnp.sin(angles))


def rotate(tensor, cosine, sine_table):
    first, second = tensor[..., :HALF], tensor[..., HALF:]
    cos_wide, sin_wide = cosine[:, None, :], sine_table[:, None, :]
    return jnp.concatenate(
        [first * cos_wide - second * sin_wide, second * cos_wide + first * sin_wide], axis=-1
    )


def rotate_back(tensor, cosine, sine_table):
    first, second = tensor[..., :HALF], tensor[..., HALF:]
    cos_wide, sin_wide = cosine[:, None, :], sine_table[:, None, :]
    return jnp.concatenate(
        [first * cos_wide + second * sin_wide, second * cos_wide - first * sin_wide], axis=-1
    )


def dot(left, right):
    return jnp.dot(left, right, preferred_element_type=F32)


def dot_nt(left, right):
    return lax.dot_general(left, right, (((1,), (1,)), ((), ())), preferred_element_type=F32)


def dot_tn(left, right):
    return lax.dot_general(left, right, (((0,), (0,)), ((), ())), preferred_element_type=F32)


def row_tile(keys):
    return 256 if keys <= 2048 else 64


def gathered(ref):
    return jnp.concatenate([ref[j] for j in range(ref.shape[0])], axis=1)


def mask_rows(kpos_ref, qpos_ref, qstart_ref, start, rows):
    kpos = kpos_ref[0]
    parts = []
    done = 0
    while done < rows:
        at = (start + done) % ROWS
        size = min(rows - done, ROWS - at)
        qpos = qpos_ref[0, at : at + size, :]
        qstart = qstart_ref[0, at : at + size, :]
        parts.append((kpos <= qpos) & (kpos >= qstart))
        done += size
    return parts


def masked(scores, parts):
    out = []
    at = 0
    for part in parts:
        size = part.shape[0]
        out.append(jnp.where(part, scores[at : at + size, :], NEG))
        at += size
    return jnp.concatenate(out, axis=0) if len(out) > 1 else out[0]


def attend_kernel(q_ref, k_ref, v_ref, kpos_ref, qpos_ref, qstart_ref, o_ref, lse_ref):
    total = q_ref.shape[2]
    kt = gathered(k_ref)
    vt = gathered(v_ref)
    tile = min(total, row_tile(kt.shape[1]))
    for at in range(0, total, tile):
        q = q_ref[0, 0, at : at + tile, :]
        scores = masked(dot(q, kt), mask_rows(kpos_ref, qpos_ref, qstart_ref, at, tile))
        top = jnp.max(scores, axis=1, keepdims=True)
        weights = jnp.exp(scores - top)
        norm = jnp.sum(weights, axis=1, keepdims=True)
        probs = (weights * (1.0 / norm)).astype(BF16)
        o_ref[0, 0, at : at + tile, :] = dot_nt(probs, vt).astype(BF16)
        lse_ref[0, 0, at : at + tile, :] = top + jnp.log(norm)


def attend_back_kernel(
    q_ref,
    do_ref,
    lse_ref,
    k_ref,
    v_ref,
    kpos_ref,
    qpos_ref,
    qstart_ref,
    dq_ref,
    dk_ref,
    dv_ref,
):
    total = q_ref.shape[2]
    kt = gathered(k_ref)
    vt = gathered(v_ref)
    tile = min(total, row_tile(kt.shape[1]))
    dkt = None
    dvt = None
    for at in range(0, total, tile):
        q = q_ref[0, 0, at : at + tile, :]
        grad = do_ref[0, 0, at : at + tile, :]
        scores = masked(dot(q, kt), mask_rows(kpos_ref, qpos_ref, qstart_ref, at, tile))
        probs = jnp.exp(scores - lse_ref[0, 0, at : at + tile, :])
        dprobs = dot(grad, vt)
        delta = jnp.sum(probs * dprobs, axis=1, keepdims=True)
        dscores = (probs * (dprobs - delta)).astype(BF16)
        dq_ref[0, 0, at : at + tile, :] = dot_nt(dscores, kt)
        dk_part = dot_tn(q, dscores)
        dv_part = dot_tn(grad, probs.astype(BF16))
        dkt = dk_part if dkt is None else dkt + dk_part
        dvt = dv_part if dvt is None else dvt + dv_part
    for j in range(dk_ref.shape[0]):
        dk_ref[j] = dkt[:, j * ROWS : (j + 1) * ROWS].astype(BF16)
        dv_ref[j] = dvt[:, j * ROWS : (j + 1) * ROWS].astype(BF16)


def attention_specs(q, kv, kpos):
    slots = kv.shape[0]
    kv_heads = kv.shape[1] // (2 * HEAD_SIZE)
    keys = kpos.shape[2]
    rows = q.shape[2]
    unit = pl.BlockSpec((1, 1, rows, HEAD_SIZE), lambda s, h: (s, h, 0, 0))
    column = pl.BlockSpec((1, 1, rows, 1), lambda s, h: (s, h, 0, 0))
    k_spec = pl.BlockSpec((slots, HEAD_SIZE, ROWS), lambda s, h: (0, h, s))
    v_spec = pl.BlockSpec((slots, HEAD_SIZE, ROWS), lambda s, h: (0, kv_heads + h, s))
    kpos_spec = pl.BlockSpec((1, 1, keys), lambda s, h: (s, 0, 0))
    q_spec = pl.BlockSpec((1, ROWS, 1), lambda s, h: (s, 0, 0))
    return kv_heads, unit, column, k_spec, v_spec, kpos_spec, q_spec


def attend_forward(q, kv, kpos, qpos, qstart):
    kv_heads, unit, column, k_spec, v_spec, kpos_spec, q_spec = attention_specs(q, kv, kpos)
    rows, keys = q.shape[2], kpos.shape[2]
    work = SEQS * kv_heads * rows * keys
    return pl.pallas_call(
        attend_kernel,
        grid=(SEQS, kv_heads),
        in_specs=[unit, k_spec, v_spec, kpos_spec, q_spec, q_spec],
        out_specs=[unit, column],
        out_shape=[
            jax.ShapeDtypeStruct(q.shape, BF16),
            jax.ShapeDtypeStruct(q.shape[:3] + (1,), F32),
        ],
        compiler_params=pltpu.CompilerParams(vmem_limit_bytes=VMEM_LIMIT),
        cost_estimate=pl.CostEstimate(
            flops=8 * HEAD_SIZE * work, bytes_accessed=8 * 2**20, transcendentals=work
        ),
    )(q, kv, kv, kpos, qpos, qstart)


def attend_backward(q, grad, lse, kv, kpos, qpos, qstart):
    kv_heads, unit, column, k_spec, v_spec, kpos_spec, q_spec = attention_specs(q, kv, kpos)
    rows, keys = q.shape[2], kpos.shape[2]
    work = SEQS * kv_heads * rows * keys
    slots = kv.shape[0]
    grad_spec = pl.BlockSpec((slots, HEAD_SIZE, ROWS), lambda s, h: (0, h, s))
    grad_shape = jax.ShapeDtypeStruct((slots, kv_heads * HEAD_SIZE, SEQS * ROWS), BF16)
    return pl.pallas_call(
        attend_back_kernel,
        grid=(SEQS, kv_heads),
        in_specs=[unit, unit, column, k_spec, v_spec, kpos_spec, q_spec, q_spec],
        out_specs=[unit, grad_spec, grad_spec],
        out_shape=[jax.ShapeDtypeStruct(q.shape, F32)] + [grad_shape] * 2,
        compiler_params=pltpu.CompilerParams(vmem_limit_bytes=VMEM_LIMIT),
        cost_estimate=pl.CostEstimate(
            flops=20 * HEAD_SIZE * work, bytes_accessed=16 * 2**20, transcendentals=work
        ),
    )(q, grad, lse, kv, kv, kpos, qpos, qstart)


def ring_neighbours(chips):
    ctx = lax.axis_index("ctx")
    chip, core, half = ctx // 2, ctx % 2, chips // 2
    odd = chip % 2
    place = odd * (chips - 1 - chip // 2) + (1 - odd) * (chip // 2)

    def device(at):
        far = at // half
        return ((1 - far) * 2 * at + far * (2 * (chips - 1 - at) + 1)) * 2 + core

    return device((place + 1) % chips), device((place + chips - 1) % chips), ctx + 1 - 2 * core


class Links:
    def __init__(self, chips, send_sems, recv_sems):
        self.chips = chips
        self.right, self.left, self.sib = ring_neighbours(chips)
        self.head = lax.axis_index("head")
        self.ctx = lax.axis_index("ctx")
        self.send_sems, self.recv_sems = send_sems, recv_sems
        self.used = 0
        self.started = []

    def greet(self):
        barrier = pltpu.get_barrier_semaphore()
        for target in (self.right, self.left, self.sib):
            pl.semaphore_signal(barrier, inc=1, device_id=(target, self.head), device_id_type=MESH)
        pl.semaphore_signal(
            barrier, inc=1, device_id=(self.ctx, 1 - self.head), device_id_type=MESH
        )
        pl.semaphore_wait(barrier, 4)

    def copy(self, src, dst, target):
        copy = pltpu.make_async_remote_copy(
            src_ref=src,
            dst_ref=dst,
            send_sem=self.send_sems.at[self.used],
            recv_sem=self.recv_sems.at[self.used],
            device_id=target,
            device_id_type=MESH,
        )
        self.used += 1
        copy.start()
        self.started.append(copy)
        return copy

    def to_right(self, src, dst):
        return self.copy(src, dst, (self.right, self.head))

    def to_left(self, src, dst):
        return self.copy(src, dst, (self.left, self.head))

    def to_sibling(self, src, dst):
        return self.copy(src, dst, (self.sib, self.head))

    def to_head(self, src, dst):
        return self.copy(src, dst, (self.ctx, 1 - self.head))

    def sent(self, copy):
        if any(other is copy for other in self.started):
            copy.wait_send()
            self.started = [other for other in self.started if other is not copy]

    def finish(self):
        for copy in self.started:
            copy.wait_send()
        self.started = []


class RingGather:
    def __init__(self, links, ref, chains, first=None):
        self.links, self.ref, self.chains = links, ref, chains
        self.first = first
        self.moving = {}
        self.arriving = []
        self.steps = links.chips // 2
        self.events = [(c, s) for s in range(1, self.steps + 1) for c in range(len(chains))]

    @staticmethod
    def copies(chips, chains):
        return chains * (chips + chips)

    def window(self, slot, chain, part=None):
        r0, rn, c0, cn = self.chains[chain]
        if part is not None:
            rn = rn // 2
            r0 = r0 + part * rn
        if slot == 0 and self.first is not None:
            return self.first.at[pl.ds(r0, rn), pl.ds(c0, cn)]
        return self.ref.at[slot, pl.ds(r0, rn), pl.ds(c0, cn)]

    def share(self, slot, chain):
        r0, rn, c0, cn = self.chains[chain]
        there = self.ref.at[self.links.chips + slot, pl.ds(r0, rn), pl.ds(c0, cn)]
        self.arriving.append(self.links.to_sibling(self.window(slot, chain), there))

    def issue(self, event):
        chain, step = event
        chips = self.links.chips
        last = step == self.steps
        up_from, up_to = (chips - step + 1) % chips, chips - step
        r0, rn, c0, cn = self.chains[chain]

        def there(slot, part):
            rows = (r0, rn) if part is None else (r0 + part * (rn // 2), rn // 2)
            return self.ref.at[slot, pl.ds(*rows), pl.ds(c0, cn)]

        up = 0 if last else None
        down = 1 if last else None
        self.moving[event] = (
            self.links.to_right(self.window(up_from, chain, up), there(up_to, up)),
            self.links.to_left(self.window(step - 1, chain, down), there(step, down)),
        )
        if step == 1:
            self.share(0, chain)

    def land(self, event):
        chain, step = event
        for copy in self.moving[event]:
            copy.wait_recv()
        self.share(self.links.chips - step, chain)
        if step != self.steps:
            self.share(step, chain)

    def settle(self):
        for copy in self.arriving:
            copy.wait_recv()


class Queue:
    def __init__(self, rings, depth=2):
        self.items = [(ring, event) for ring in rings for event in ring.events]
        self.depth = depth
        self.landed = 0
        self.issued = 0

    def fill(self):
        while self.issued < len(self.items) and self.issued < self.landed + self.depth:
            ring, event = self.items[self.issued]
            ring.issue(event)
            self.issued += 1

    def pump(self, count=1):
        for _ in range(count):
            if self.landed < len(self.items):
                ring, event = self.items[self.landed]
                ring.land(event)
                self.landed += 1
                self.fill()

    def through(self, ring):
        last = max(i for i, item in enumerate(self.items) if item[0] is ring)
        self.pump(last + 1 - self.landed)


TILE = 512


def rms_inverse(rows):
    return lax.rsqrt(jnp.mean(rows * rows, axis=-1, keepdims=True) + EPS)


def forward_kernel(dims, *refs):
    layers, chips, width, q_width, kv_width, ff = dims
    slots = 2 * chips
    it = iter(refs)
    x_ref = next(it)
    shards = [next(it) for _ in range(2 * layers)]
    cos_ref, sin_ref, kpos_ref, qpos_ref, qstart_ref = (next(it) for _ in range(5))
    weights = [next(it) for _ in range(2 * layers)]
    (
        kv_ref,
        normed_a_ref,
        qt_ref,
        lse_ref,
        att_ref,
        middle_ref,
        normed_m_ref,
        gate_ref,
        up_ref,
        act_ref,
        x_out_ref,
        gain_ref,
    ) = (next(it) for _ in range(12))
    (
        wt, wo, acc, proj_t, att_t, b_send, b_recv, gain_block, send_sems, recv_sems, load_sems, own_sems
    ) = (next(it) for _ in range(12))

    rows = x_ref.shape[0]
    db = width // slots
    heads_kv = kv_width // HEAD_SIZE
    group = q_width // kv_width
    qkv_width = q_width + 2 * kv_width
    links = Links(chips, send_sems, recv_sems)
    own_copies = []
    for i, (shard, weight) in enumerate(zip(shards, weights)):
        own_copies.append(pltpu.make_async_copy(shard, weight.at[0], own_sems.at[i]))
        own_copies[-1].start()
    links.greet()

    rings = []
    for shard, weight in zip(shards, weights):
        wide = shard.shape[1]
        cut = (wide // 256) * 128
        rings.append(
            RingGather(links, weight, [(0, db, 0, cut), (0, db, cut, wide - cut)], first=shard)
        )
    queue = Queue(rings)
    queue.fill()

    def ready(i):
        queue.through(rings[i])
        rings[i].settle()

    def load(i, column, wide, target, sem):
        copy = pltpu.make_async_copy(
            weights[i].at[:, :, pl.ds(column, wide)], target, load_sems.at[sem]
        )
        copy.start()
        return copy

    def flat(ref):
        return ref[...].reshape(width, ref.shape[-1])

    ready(0)
    for copy in own_copies:
        copy.wait()
    side = qkv_width + q_width
    load(0, side, 128, gain_block, 0).wait()
    gain_ref[...] = flat(gain_block).astype(F32).T[: gain_ref.shape[0], :]

    for layer in range(layers):
        attn, mlp = 2 * layer, 2 * layer + 1
        if layer:
            ready(attn)
        tiles = [load(attn, t * TILE, TILE, wt.at[t], t) for t in range(qkv_width // TILE)]
        out_load = load(attn, qkv_width, q_width, wo, 6)

        x = x_ref[...] if layer == 0 else x_out_ref[layer - 1]
        gain_a = gain_ref[layer : layer + 1, :]
        normed_a_ref[layer, 0:rows, :] = (x * rms_inverse(x) * gain_a).astype(BF16)
        swap = links.to_head(
            normed_a_ref.at[layer, pl.ds(0, rows), :], normed_a_ref.at[layer, pl.ds(rows, rows), :]
        )
        for t, tile in enumerate(tiles):
            tile.wait()
            part = dot(normed_a_ref[layer, 0:rows, :], flat(wt.at[t]))
            proj_t[t * TILE : (t + 1) * TILE, 0:rows] = part.T
        swap.wait_recv()
        for t in range(len(tiles)):
            part = dot(normed_a_ref[layer, rows : 2 * rows, :], flat(wt.at[t]))
            proj_t[t * TILE : (t + 1) * TILE, rows : 2 * rows] = part.T
        queue.pump()

        cosine, sine = cos_ref[...], sin_ref[...]

        def turned(at):
            low = proj_t[at : at + HALF, :]
            high = proj_t[at + HALF : at + HEAD_SIZE, :]
            return low * cosine - high * sine, high * cosine + low * sine

        for h in range(heads_kv):
            low, high = turned(q_width + h * HEAD_SIZE)
            kv_ref[layer, 0, h * HEAD_SIZE : h * HEAD_SIZE + HALF, :] = low.astype(BF16)
            kv_ref[layer, 0, h * HEAD_SIZE + HALF : (h + 1) * HEAD_SIZE, :] = high.astype(BF16)
        kv_ref[layer, 0, kv_width : 2 * kv_width, :] = proj_t[
            q_width + kv_width : qkv_width, :
        ].astype(BF16)
        wide = kv_ref.shape[-1]
        kv_ring = RingGather(
            links,
            kv_ref.at[layer],
            [(0, kv_width, 0, wide), (kv_width, kv_width, 0, wide)],
        )
        kv_queue = Queue([kv_ring])
        kv_queue.fill()
        scale = HEAD_SIZE ** (-0.5)
        for h in range(q_width // HEAD_SIZE):
            low, high = turned(h * HEAD_SIZE)
            qt_ref[layer, h * HEAD_SIZE : h * HEAD_SIZE + HALF, :] = (low * scale).astype(BF16)
            qt_ref[layer, h * HEAD_SIZE + HALF : (h + 1) * HEAD_SIZE, :] = (high * scale).astype(
                BF16
            )
        for step in range(len(kv_queue.items)):
            kv_queue.pump()
            if step % 3 == 2:
                queue.pump()
        kv_ring.settle()

        def unit(u, carry):
            s, h = u // heads_kv, u % heads_kv
            k_rows = pl.ds(pl.multiple_of(h * HEAD_SIZE, HEAD_SIZE), HEAD_SIZE)
            v_rows = pl.ds(pl.multiple_of(kv_width + h * HEAD_SIZE, HEAD_SIZE), HEAD_SIZE)
            lanes = pl.ds(pl.multiple_of(s * ROWS, ROWS), ROWS)
            kt = jnp.concatenate([kv_ref[layer, j, k_rows, lanes] for j in range(slots)], axis=1)
            vt = jnp.concatenate([kv_ref[layer, j, v_rows, lanes] for j in range(slots)], axis=1)
            q_rows = [
                pl.ds(pl.multiple_of((h * group + g) * HEAD_SIZE, HEAD_SIZE), HEAD_SIZE)
                for g in range(group)
            ]
            qt = jnp.concatenate([qt_ref[layer, at, lanes] for at in q_rows], axis=1)
            kpos, qpos, qstart = kpos_ref[s], qpos_ref[s], qstart_ref[s]
            allowed = (kpos <= qpos) & (kpos >= qstart)
            scores = masked(dot_tn(qt, kt), [allowed] * group)
            top = jnp.max(scores, axis=1, keepdims=True)
            raised = jnp.exp(scores - top)
            norm = jnp.sum(raised, axis=1, keepdims=True)
            probs = (raised * (1.0 / norm)).astype(BF16)
            mixed = dot_nt(vt, probs)
            for g, at in enumerate(q_rows):
                att_t[at, lanes] = mixed[:, g * ROWS : (g + 1) * ROWS]
            lse_ref[layer, u] = top + jnp.log(norm)
            return carry

        units = SEQS * heads_kv
        for at in range(0, units, 2):
            lax.fori_loop(at, at + 2, unit, 0)
            queue.pump()
        att_ref[layer] = att_t[...].T.astype(BF16)

        out_load.wait()
        branch = (layer * 2) % b_send.shape[0]
        other = dot_nt(att_ref[layer, rows : 2 * rows, :], flat(wo))
        b_send[branch] = other.astype(BF16)
        swap = links.to_head(b_send.at[branch], b_recv.at[branch])
        mine = dot_nt(att_ref[layer, 0:rows, :], flat(wo))
        queue.pump()
        swap.wait_recv()
        middle = x + mine + b_recv[branch].astype(F32)
        middle_ref[layer] = middle
        gain_m = gain_ref[layers + layer : layers + layer + 1, :]
        normed_m_ref[layer, 0:rows, :] = (middle * rms_inverse(middle) * gain_m).astype(BF16)
        swap = links.to_head(
            normed_m_ref.at[layer, pl.ds(0, rows), :], normed_m_ref.at[layer, pl.ds(rows, rows), :]
        )
        ready(mlp)

        def load_tile(t):
            at = (t % 2) * 3
            return [
                load(mlp, part * ff + t * TILE, TILE, wt.at[at + part], at + part)
                for part in range(3)
            ]

        pending = load_tile(0)
        swap.wait_recv()
        normed = normed_m_ref[layer]
        count = ff // TILE
        for t in range(count):
            following = load_tile(t + 1) if t + 1 < count else None
            for copy in pending:
                copy.wait()
            at = (t % 2) * 3
            columns = slice(t * TILE, (t + 1) * TILE)
            gate = dot(normed, flat(wt.at[at]))
            up = dot(normed, flat(wt.at[at + 1]))
            act = (gate * jax.nn.sigmoid(gate) * up).astype(BF16)
            gate_ref[layer, :, columns] = gate.astype(BF16)
            up_ref[layer, :, columns] = up.astype(BF16)
            act_ref[layer, :, columns] = act
            down = dot_nt(act, flat(wt.at[at + 2]))
            if t == 0:
                acc[...] = down
            else:
                acc[...] += down
            pending = following
            queue.pump(2)
        branch = (layer * 2 + 1) % b_send.shape[0]
        b_send[branch] = acc[rows : 2 * rows, :].astype(BF16)
        swap = links.to_head(b_send.at[branch], b_recv.at[branch])
        swap.wait_recv()
        x_out_ref[layer] = middle_ref[layer] + acc[0:rows, :] + b_recv[branch].astype(F32)
    links.finish()


def forward(x, shards, cosine, sine, kpos, qpos, qstart, chips, q_width, kv_width, ff):
    layers = len(shards) // 2
    rows, width = x.shape
    db = shards[0].shape[0]
    slots = 2 * chips
    group = q_width // kv_width
    tokens = 2 * rows
    units = SEQS * kv_width // HEAD_SIZE
    dims = (layers, chips, width, q_width, kv_width, ff)
    copies = (2 * layers + layers) * RingGather.copies(chips, 2) + 4 * layers
    any_spec = pl.BlockSpec(memory_space=pl.ANY)
    vmem = pl.BlockSpec(memory_space=pltpu.VMEM)
    saved = [
        jax.ShapeDtypeStruct((layers, slots, 2 * kv_width, tokens), BF16),
        jax.ShapeDtypeStruct((layers, tokens, width), BF16),
        jax.ShapeDtypeStruct((layers, q_width, tokens), BF16),
        jax.ShapeDtypeStruct((layers, units, group * ROWS, 1), F32),
        jax.ShapeDtypeStruct((layers, tokens, q_width), BF16),
        jax.ShapeDtypeStruct((layers, rows, width), F32),
        jax.ShapeDtypeStruct((layers, tokens, width), BF16),
        jax.ShapeDtypeStruct((layers, tokens, ff), BF16),
        jax.ShapeDtypeStruct((layers, tokens, ff), BF16),
        jax.ShapeDtypeStruct((layers, tokens, ff), BF16),
        jax.ShapeDtypeStruct((layers, rows, width), F32),
        jax.ShapeDtypeStruct((2 * layers, width), F32),
    ]
    out = pl.pallas_call(
        functools.partial(forward_kernel, dims),
        out_shape=[jax.ShapeDtypeStruct((slots,) + shard.shape, BF16) for shard in shards] + saved,
        in_specs=[vmem] + [any_spec] * len(shards) + [vmem] * 5,
        out_specs=[any_spec] * len(shards) + [vmem] * len(saved),
        scratch_shapes=[
            pltpu.VMEM((6, slots, db, TILE), BF16),
            pltpu.VMEM((slots, db, q_width), BF16),
            pltpu.VMEM((tokens, width), F32),
            pltpu.VMEM((q_width + 2 * kv_width, tokens), F32),
            pltpu.VMEM((q_width, tokens), F32),
            pltpu.VMEM((2 * layers, rows, width), BF16),
            pltpu.VMEM((2 * layers, rows, width), BF16),
            pltpu.VMEM((slots, db, 128), BF16),
            pltpu.SemaphoreType.DMA((copies,)),
            pltpu.SemaphoreType.DMA((copies,)),
            pltpu.SemaphoreType.DMA((7,)),
            pltpu.SemaphoreType.DMA((len(shards),)),
        ],
        compiler_params=pltpu.CompilerParams(
            collective_id=0, has_side_effects=True, vmem_limit_bytes=KERNEL_VMEM
        ),
    )(x, *shards, cosine, sine, kpos, qpos, qstart)
    return out[: len(shards)], out[len(shards) :]


class RingScatter:
    def __init__(self, links, windows, landing, stage, sems, finish):
        self.links, self.windows, self.landing = links, windows, landing
        self.stage, self.sems, self.finish = stage, sems, finish
        self.last = links.chips - 1
        self.step = 0
        self.moving = []

    def issue(self):
        self.step += 1
        chips = self.links.chips
        slots = ((chips - self.step) % chips, self.step % chips)
        sends = (self.links.to_right, self.links.to_left)
        self.moving = [
            sends[d](self.windows[d](slots[d]), self.landing.at[d, self.step - 1])
            for d in range(2)
        ]

    def land(self):
        chips, wide = self.links.chips, self.landing.shape[-1]
        loads = []
        for d in range(2):
            self.moving[d].wait_recv()
            self.links.sent(self.moving[d])
            load = pltpu.make_async_copy(
                self.landing.at[d, self.step - 1],
                self.stage.at[d, :, pl.ds(0, wide)],
                self.sems.at[d],
            )
            load.start()
            loads.append(load)
        slots = ((chips - 1 - self.step) % chips, (1 + self.step) % chips)
        for d in range(2):
            loads[d].wait()
            window = self.windows[d](slots[d])
            total = window[...].astype(F32) + self.stage[d, :, 0:wide].astype(F32)
            if self.step < self.last:
                window[...] = total.astype(BF16)
            else:
                self.finish(d, total)
        if self.step < self.last:
            self.issue()


class Rounds:
    def __init__(self):
        self.active = []

    def start(self, ring):
        ring.issue()
        ring.left = ring.last
        self.active.append(ring)

    def pump(self, count=1):
        for _ in range(count):
            if self.active:
                ring = self.active.pop(0)
                ring.land()
                ring.left -= 1
                if ring.left:
                    self.active.append(ring)

    def drain(self):
        while self.active:
            self.pump()


def backward_kernel(dims, *refs):
    layers, chips, width, q_width, kv_width, ff = dims
    slots = 2 * chips
    it = iter(refs)
    g_ref = next(it)
    weights = [next(it) for _ in range(2 * layers)]
    (
        kv_ref, normed_a_ref, qt_ref, lse_ref, att_ref, middle_ref, normed_m_ref,
        gate_ref, up_ref, act_ref, x_in_ref, gain_ref,
        cos_ref, sin_ref, kpos_ref, qpos_ref, qstart_ref,
    ) = (next(it) for _ in range(17))
    d_hidden_ref, d_gain_ref = next(it), next(it)
    d_mlp_ref, d_attn_ref = next(it), next(it)
    land_mlp, land_out, land_q, land_kv, land_dkv = (next(it) for _ in range(5))
    (
        wt, kv_buf, dkv_sib, dw_mlp, dw_attn, a_sib, at_buf, g_act, g_gu, g_qkv, g_att, acc,
        g_low, g2_low, b_send, b_recv, qt_l, lse_l, da_t, dq_t, dkv_sum, gu_buf, rows_f32, n_own,
        stage, out_stage, send_sems, recv_sems, load_sems, stage_sems,
    ) = (next(it) for _ in range(30))

    rows = g_ref.shape[0]
    tokens = 2 * rows
    db = width // slots
    side = width // 2
    heads_kv = kv_width // HEAD_SIZE
    group = q_width // kv_width
    qkv_width = q_width + 2 * kv_width
    links = Links(chips, send_sems, recv_sems)
    links.greet()
    rounds = Rounds()
    cosine, sine = cos_ref[...], sin_ref[...]
    scale = HEAD_SIZE ** (-0.5)

    def local(src, dst, sem):
        copy = pltpu.make_async_copy(src, dst, load_sems.at[sem])
        copy.start()
        return copy

    def load(i, column, wide, target, sem):
        return local(weights[i].at[:, :, pl.ds(column, wide)], target, sem)

    def flat(ref):
        return ref[...].reshape(width, ref.shape[-1])

    def out_by(target):
        def finish(d, total):
            wide = total.shape[-1]
            out_stage[d, :, 0:wide] = total
            copy = pltpu.make_async_copy(
                out_stage.at[d, :, pl.ds(0, wide)], target(d), stage_sems.at[d]
            )
            copy.start()
            copy.wait()

        return finish

    def scatter(ref, column, wide, landing, out):
        half = wide // 2

        def window(d):
            return lambda slot: ref.at[slot, :, pl.ds(column + d * half, half)]

        rounds.start(
            RingScatter(
                links,
                (window(0), window(1)),
                landing,
                stage,
                stage_sems,
                out_by(lambda d: out.at[:, pl.ds(column + d * half, half)]),
            )
        )

    def turn_columns(own, sib):
        at_buf[:, 0:tokens] = own.astype(F32).T.astype(BF16)
        at_buf[:, tokens : 2 * tokens] = sib.astype(F32).T.astype(BF16)

    def weight_grad(target, column, right, wide):
        for c in range(0, wide, TILE):
            size = min(TILE, wide - c)
            part = dot(at_buf[...], right[:, c : c + size])
            target[:, :, column + c : column + c + size] = part.reshape(chips, db, size).astype(
                BF16
            )

    def norm_back(grad, value, gain, row):
        inverse = rms_inverse(value)
        normalized = value * inverse
        d_gain_ref[row : row + 1, :] = jnp.sum(grad * normalized, axis=0, keepdims=True)
        scaled = grad * gain
        mean = jnp.mean(scaled * normalized, axis=-1, keepdims=True)
        d_hidden_ref[...] += inverse * (scaled - normalized * mean)


    d_hidden_ref[...] = g_ref[...]
    for layer in reversed(range(layers)):
        attn, mlp = 2 * layer, 2 * layer + 1
        gain_a = gain_ref[layer : layer + 1, :]
        gain_m = gain_ref[layers + layer : layers + layer + 1, :]
        links.finish()

        def load_tile(t):
            at = (t % 2) * 3
            columns = pl.ds(t * TILE, TILE)
            return [
                load(mlp, part * ff + t * TILE, TILE, wt.at[at + part], at + part)
                for part in range(3)
            ] + [
                local(gate_ref.at[layer, :, columns], gu_buf.at[t % 2, 0], 6 + t % 2 * 2),
                local(up_ref.at[layer, :, columns], gu_buf.at[t % 2, 1], 7 + t % 2 * 2),
            ]

        pending = load_tile(0)
        g_low[0:rows, :] = d_hidden_ref[...].astype(BF16)
        swap = links.to_head(g_low.at[pl.ds(0, rows), :], g_low.at[pl.ds(rows, rows), :])
        far = pl.ds(side, side)
        other_rows = pl.ds(tokens, tokens)
        from_sib = [
            links.to_sibling(act_ref.at[layer], g_act.at[other_rows, :]),
            links.to_sibling(normed_m_ref.at[layer, :, far], a_sib.at[1]),
            links.to_sibling(normed_a_ref.at[layer, :, far], a_sib.at[3]),
            links.to_sibling(att_ref.at[layer], g_att.at[other_rows, :]),
        ]
        here = [
            local(act_ref.at[layer], g_act.at[pl.ds(0, tokens), :], 10),
            local(normed_m_ref.at[layer, :, pl.ds(0, side)], n_own.at[0], 11),
            local(normed_a_ref.at[layer, :, pl.ds(0, side)], n_own.at[1], 12),
            local(att_ref.at[layer], g_att.at[pl.ds(0, tokens), :], 13),
            local(middle_ref.at[layer], rows_f32.at[0], 14),
            local(x_in_ref.at[layer], rows_f32.at[1], 15),
            local(qt_ref.at[layer], qt_l, 16),
            local(lse_ref.at[layer], lse_l, 17),
        ]
        rounds.pump()
        swap.wait_recv()
        from_sib_g = links.to_sibling(g_low.at[:, far], a_sib.at[0])
        count = ff // TILE
        from_sib_gu = []
        for t in range(count):
            following = load_tile(t + 1) if t + 1 < count else None
            for copy in pending:
                copy.wait()
            at = (t % 2) * 3
            gate = gu_buf[t % 2, 0].astype(F32)
            up = gu_buf[t % 2, 1].astype(F32)
            d_act = dot(g_low[...], flat(wt.at[at + 2]))
            sig = jax.nn.sigmoid(gate)
            d_gate = (d_act * up * sig * (1.0 + gate * (1.0 - sig))).astype(BF16)
            d_up = (d_act * gate * sig).astype(BF16)
            for part, grad in enumerate((d_gate, d_up)):
                column = part * ff + t * TILE
                g_gu[0:tokens, column : column + TILE] = grad
                from_sib_gu.append(
                    links.to_sibling(
                        g_gu.at[pl.ds(0, tokens), pl.ds(column, TILE)],
                        g_gu.at[other_rows, pl.ds(column, TILE)],
                    )
                )
            back = dot_nt(d_gate, flat(wt.at[at])) + dot_nt(d_up, flat(wt.at[at + 1]))
            if t == 0:
                acc[...] = back
            else:
                acc[...] += back
            pending = following
            rounds.pump(3)
        b_send[0] = acc[rows:tokens, :].astype(BF16)
        swap = links.to_head(b_send.at[0], b_recv.at[0])
        out_loads = [
            load(attn, qkv_width, TILE, wt.at[4], 4),
            load(attn, qkv_width + TILE, q_width - TILE, wt.at[5, :, :, pl.ds(0, q_width - TILE)], 5),
        ]
        rounds.drain()
        for copy in here:
            copy.wait()
        from_sib_g.wait_recv()
        for copy in from_sib:
            copy.wait_recv()
        turn_columns(g_low[:, 0:side], a_sib[0])
        weight_grad(dw_mlp.at[0], 0, g_act, ff)
        scatter(dw_mlp.at[0], 0, ff, land_mlp.at[layer, 0], d_mlp_ref.at[layer, 0])
        swap.wait_recv()
        norm_back(
            acc[0:rows, :] + b_recv[0].astype(F32), rows_f32[0], gain_m, layers + layer
        )
        g2_low[0:rows, :] = d_hidden_ref[...].astype(BF16)
        swap = links.to_head(g2_low.at[pl.ds(0, rows), :], g2_low.at[pl.ds(rows, rows), :])
        for copy in from_sib_gu:
            copy.wait_recv()
        turn_columns(n_own[0], a_sib[1])
        for part in range(2):
            weight_grad(dw_mlp.at[1 + part], 0, g_gu.at[:, pl.ds(part * ff, ff)], ff)
            scatter(
                dw_mlp.at[1 + part], 0, ff, land_mlp.at[layer, 1 + part], d_mlp_ref.at[layer, 1 + part]
            )

        swap.wait_recv()
        from_sib_g = links.to_sibling(g2_low.at[:, far], a_sib.at[2])
        for i, copy in enumerate(out_loads):
            copy.wait()
            size = TILE if i == 0 else q_width - TILE
            part = dot(g2_low[...], flat(wt.at[4 + i, :, :, pl.ds(0, size)]))
            da_t[i * TILE : i * TILE + size, :] = part.T.astype(BF16)
        rounds.pump()

        units = SEQS * heads_kv
        pairs = (heads_kv + 1) // 2

        def unit_copies(u, at):
            s, h = u // heads_kv, u % heads_kv
            lanes = pl.ds(pl.multiple_of(s * ROWS, ROWS), ROWS)
            return [
                pltpu.make_async_copy(
                    kv_ref.at[
                        layer,
                        :,
                        pl.ds(pl.multiple_of(part * kv_width + h * HEAD_SIZE, HEAD_SIZE), HEAD_SIZE),
                        lanes,
                    ],
                    kv_buf.at[at, part],
                    load_sems.at[6 + 2 * at + part],
                )
                for part in range(2)
            ]

        def unit(u, carry):
            at = u % 2
            s, h = u // heads_kv, u % heads_kv
            for copy in unit_copies(u, at):
                copy.wait()
            ahead = jnp.minimum(u + 1, units - 1)

            @pl.when(u + 1 < units)
            def _():
                for copy in unit_copies(ahead, 1 - at):
                    copy.start()

            kt = jnp.concatenate([kv_buf[at, 0, j] for j in range(slots)], axis=1)
            vt = jnp.concatenate([kv_buf[at, 1, j] for j in range(slots)], axis=1)
            lanes = pl.ds(pl.multiple_of(s * ROWS, ROWS), ROWS)
            allowed = (kpos_ref[s] <= qpos_ref[s]) & (kpos_ref[s] >= qstart_ref[s])
            dkt = dvt = None
            for g in range(group):
                head_rows = pl.ds(
                    pl.multiple_of((h * group + g) * HEAD_SIZE, HEAD_SIZE), HEAD_SIZE
                )
                qt = qt_l[head_rows, lanes]
                dot_t = da_t[head_rows, lanes]
                scores = masked(dot_tn(qt, kt), [allowed])
                probs = jnp.exp(scores - lse_l[u, g * ROWS : (g + 1) * ROWS, :])
                dprobs = dot_tn(dot_t, vt)
                delta = jnp.sum(probs * dprobs, axis=1, keepdims=True)
                dscores = (probs * (dprobs - delta)).astype(BF16)
                dq_t[head_rows, lanes] = dot_nt(kt, dscores)
                dk_part = dot(qt, dscores)
                dv_part = dot(dot_t, probs.astype(BF16))
                dkt = dk_part if dkt is None else dkt + dk_part
                dvt = dv_part if dvt is None else dvt + dv_part
            spot = pl.ds(pl.multiple_of((h % 2) * SEQS * ROWS + s * ROWS, ROWS), ROWS)
            for j in range(slots):
                wt[h // 2, j, :, spot] = dkt[:, j * ROWS : (j + 1) * ROWS].astype(BF16)
                wt[pairs + h // 2, j, :, spot] = dvt[:, j * ROWS : (j + 1) * ROWS].astype(BF16)
            return carry

        for copy in unit_copies(0, 0):
            copy.start()
        for u in range(0, units, 2):
            lax.fori_loop(u, u + 2, unit, 0)
            rounds.pump(2)

        sent = []
        for i in range(2 * pairs):
            sent.append(
                links.to_sibling(wt.at[i, pl.ds(chips, chips)], dkv_sib.at[i])
            )
        from_sib_g.wait_recv()
        turn_columns(g2_low[:, 0:side], a_sib[2])
        weight_grad(dw_attn, qkv_width, g_att, q_width)
        scatter(dw_attn, qkv_width, q_width, land_out.at[layer], d_attn_ref.at[layer])
        sums = Rounds()
        for i in range(pairs):
            for j in (i, pairs + i):
                sent[j].wait_recv()
                for slot in range(chips):
                    wt[j, slot] = (wt[j, slot].astype(F32) + dkv_sib[j, slot].astype(F32)).astype(
                        BF16
                    )

            def keep(i):
                def finish(d, total):
                    dkv_sum[d * pairs + i] = total

                return finish

            sums.start(
                RingScatter(
                    links,
                    (
                        lambda slot, i=i: wt.at[i, slot],
                        lambda slot, i=i: wt.at[pairs + i, slot],
                    ),
                    land_dkv.at[layer, i],
                    stage,
                    stage_sems,
                    keep(i),
                )
            )

        def turned_back(low, high):
            return low * cosine + high * sine, high * cosine - low * sine

        for h in range(q_width // HEAD_SIZE):
            at = h * HEAD_SIZE
            low, high = turned_back(
                dq_t[at : at + HALF, :], dq_t[at + HALF : at + HEAD_SIZE, :]
            )
            dq_t[at : at + HALF, :] = low * scale
            dq_t[at + HALF : at + HEAD_SIZE, :] = high * scale
        g_qkv[0:tokens, 0:q_width] = dq_t[...].T.astype(BF16)
        mine = pl.ds(0, tokens)
        from_sib_q = links.to_sibling(
            g_qkv.at[mine, pl.ds(0, q_width)], g_qkv.at[other_rows, pl.ds(0, q_width)]
        )
        step = 0
        while sums.active:
            sums.pump()
            step += 1
            if step % 2 == 0:
                rounds.pump()
            if step == 4:
                from_sib_q.wait_recv()
                turn_columns(n_own[1], a_sib[3])
                weight_grad(dw_attn, 0, g_qkv, q_width)
                scatter(dw_attn, 0, q_width, land_q.at[layer], d_attn_ref.at[layer])
        for h in range(heads_kv):
            spot = slice((h % 2) * SEQS * ROWS, (h % 2 + 1) * SEQS * ROWS)
            block = dkv_sum[h // 2, :, spot]
            low, high = turned_back(block[0:HALF, :], block[HALF:HEAD_SIZE, :])
            at = h * HEAD_SIZE
            dq_t[at : at + HALF, :] = low
            dq_t[at + HALF : at + HEAD_SIZE, :] = high
            dq_t[kv_width + at : kv_width + at + HEAD_SIZE, :] = dkv_sum[pairs + h // 2, :, spot]
        g_qkv[0:tokens, q_width:qkv_width] = dq_t[0 : 2 * kv_width, :].T.astype(BF16)
        from_sib_kv = links.to_sibling(
            g_qkv.at[mine, pl.ds(q_width, 2 * kv_width)],
            g_qkv.at[other_rows, pl.ds(q_width, 2 * kv_width)],
        )
        links.finish()
        tiles = [
            load(attn, t * TILE, TILE, wt.at[t], t) for t in range(qkv_width // TILE)
        ]
        for t, tile in enumerate(tiles):
            tile.wait()
            back = dot_nt(g_qkv[0:tokens, t * TILE : (t + 1) * TILE], flat(wt.at[t]))
            if t == 0:
                acc[...] = back
            else:
                acc[...] += back
        b_send[1] = acc[rows:tokens, :].astype(BF16)
        swap = links.to_head(b_send.at[1], b_recv.at[1])
        from_sib_kv.wait_recv()
        weight_grad(dw_attn, q_width, g_qkv.at[:, pl.ds(q_width, 2 * kv_width)], 2 * kv_width)
        scatter(dw_attn, q_width, 2 * kv_width, land_kv.at[layer], d_attn_ref.at[layer])
        rounds.pump()
        swap.wait_recv()
        norm_back(acc[0:rows, :] + b_recv[1].astype(F32), rows_f32[1], gain_a, layer)
    rounds.drain()
    links.finish()


def backward(grad, weights, saved, tables, chips, q_width, kv_width, ff):
    layers = len(weights) // 2
    rows, width = grad.shape
    slots = 2 * chips
    db = width // slots
    tokens = 2 * rows
    heads_kv = kv_width // HEAD_SIZE
    units = SEQS * heads_kv
    pairs = (heads_kv + 1) // 2
    group = q_width // kv_width
    steps = chips - 1
    qkv_width = q_width + 2 * kv_width
    dims = (layers, chips, width, q_width, kv_width, ff)
    rings = 3 + 3 + pairs
    copies = layers * (rings * 2 * steps + 4 + 4 + 1 + 2 * (ff // TILE) + 1 + 2 * pairs + 2)
    any_spec = pl.BlockSpec(memory_space=pl.ANY)
    vmem = pl.BlockSpec(memory_space=pltpu.VMEM)

    def landing(*shape):
        return jax.ShapeDtypeStruct(shape, BF16)

    out = pl.pallas_call(
        functools.partial(backward_kernel, dims),
        out_shape=[
            jax.ShapeDtypeStruct((rows, width), F32),
            jax.ShapeDtypeStruct((2 * layers, width), F32),
            jax.ShapeDtypeStruct((layers, 3, db, ff), F32),
            jax.ShapeDtypeStruct((layers, db, qkv_width + q_width), F32),
            landing(layers, 3, 2, steps, db, ff // 2),
            landing(layers, 2, steps, db, q_width // 2),
            landing(layers, 2, steps, db, q_width // 2),
            landing(layers, 2, steps, db, kv_width),
            landing(layers, pairs, 2, steps, HEAD_SIZE, 2 * SEQS * ROWS),
        ],
        in_specs=[vmem] + [any_spec] * (len(weights) + 11) + [vmem] * 6,
        out_specs=[vmem] * 2 + [any_spec] * 7,
        scratch_shapes=[
            pltpu.VMEM((6, slots, db, TILE), BF16),
            pltpu.VMEM((2, 2, slots, HEAD_SIZE, ROWS), BF16),
            pltpu.VMEM((2 * pairs, chips, HEAD_SIZE, 2 * SEQS * ROWS), BF16),
            pltpu.VMEM((3, chips, db, ff), BF16),
            pltpu.VMEM((chips, db, qkv_width + q_width), BF16),
            pltpu.VMEM((4, tokens, width // 2), BF16),
            pltpu.VMEM((width // 2, 2 * tokens), BF16),
            pltpu.VMEM((2 * tokens, ff), BF16),
            pltpu.VMEM((2 * tokens, 2 * ff), BF16),
            pltpu.VMEM((2 * tokens, qkv_width), BF16),
            pltpu.VMEM((2 * tokens, q_width), BF16),
            pltpu.VMEM((tokens, width), F32),
            pltpu.VMEM((tokens, width), BF16),
            pltpu.VMEM((tokens, width), BF16),
            pltpu.VMEM((2, rows, width), BF16),
            pltpu.VMEM((2, rows, width), BF16),
            pltpu.VMEM((q_width, tokens), BF16),
            pltpu.VMEM((units, group * ROWS, 1), F32),
            pltpu.VMEM((q_width, tokens), BF16),
            pltpu.VMEM((q_width, tokens), F32),
            pltpu.VMEM((2 * pairs, HEAD_SIZE, 2 * SEQS * ROWS), F32),
            pltpu.VMEM((2, 2, tokens, TILE), BF16),
            pltpu.VMEM((2, rows, width), F32),
            pltpu.VMEM((2, tokens, width // 2), BF16),
            pltpu.VMEM((2, db, ff // 2), BF16),
            pltpu.VMEM((2, db, ff // 2), F32),
            pltpu.SemaphoreType.DMA((copies,)),
            pltpu.SemaphoreType.DMA((copies,)),
            pltpu.SemaphoreType.DMA((18,)),
            pltpu.SemaphoreType.DMA((2,)),
        ],
        compiler_params=pltpu.CompilerParams(
            collective_id=1, has_side_effects=True, vmem_limit_bytes=KERNEL_VMEM
        ),
    )(grad, *weights, *saved, *tables)
    return out[:4]


def build(n_ctx):
    chips = n_ctx // 2
    ring = ring_of(chips)

    def shifted(step):
        pairs = []
        for at, chip in enumerate(ring):
            target = ring[(at + step) % chips]
            pairs += [(chip * 2 + core, target * 2 + core) for core in range(2)]
        return pairs

    up, down = shifted(1), shifted(-1)
    sibling = [(i, i ^ 1) for i in range(n_ctx)]

    def send_up(value):
        return lax.ppermute(value, "ctx", up)

    def send_down(value):
        return lax.ppermute(value, "ctx", down)

    def swap_core(value):
        return lax.ppermute(value, "ctx", sibling)

    def swap_head(value):
        return lax.ppermute(value, "head", [(0, 1), (1, 0)])

    def ring_gather(shard):
        half = chips // 2

        def step(carry, unused):
            carry = (send_up(carry[0]), send_down(carry[1]))
            return carry, carry

        (low, high), (lows, highs) = lax.scan(step, (shard, shard), None, length=half - 1)
        cut = shard.shape[0] // 2
        across = jnp.concatenate([send_up(low[:cut]), send_down(high[cut:])], axis=0)
        return jnp.concatenate([shard[None], highs, across[None], lows[::-1]], axis=0)

    def ring_scatter(lows, highs):
        def own(parts, slot):
            return lax.dynamic_index_in_dim(parts, slot, 0, keepdims=False).astype(F32)

        def step(carry, at):
            low, high = (send_up(carry[0]), send_down(carry[1]))
            low = low.astype(F32) + own(lows, (chips - 1 - at) % chips)
            high = high.astype(F32) + own(highs, (1 + at) % chips)
            return (low.astype(BF16), high.astype(BF16)), None

        start = (lows[chips - 1].astype(BF16), highs[1].astype(BF16))
        steps = jnp.arange(1, chips - 1, dtype=jnp.int32)
        (low, high), unused = lax.scan(step, start, steps)
        return (
            send_up(low).astype(F32) + lows[0].astype(F32),
            send_down(high).astype(F32) + highs[0].astype(F32),
        )

    def gather(shard):
        own = ring_gather(shard).reshape(chips * shard.shape[0], shard.shape[1])
        return jnp.concatenate([own, swap_core(own)], axis=0)

    def weight_scatter(grad):
        db, cut = grad.shape[0] // chips, grad.shape[1] // 2
        parts = grad.reshape(chips, db, grad.shape[1])
        return jnp.concatenate(ring_scatter(parts[:, :, :cut], parts[:, :, cut:]), axis=1)

    def local(
        hidden_in,
        block_order,
        doc_ids,
        attn_gain,
        w_query,
        w_key,
        w_value,
        w_out,
        mlp_gain,
        w_gate,
        w_up,
        w_down,
        cotangent,
    ):
        layers, db = w_query.shape[0], w_query.shape[1]
        width = db * n_ctx
        side = width // 2
        q_width, kv_width, ff_width = w_query.shape[2], w_key.shape[2], w_gate.shape[2]
        heads_q, heads_kv = q_width // HEAD_SIZE, kv_width // HEAD_SIZE
        group = heads_q // heads_kv
        own_rows = hidden_in.shape[0]
        token_rows = own_rows * 2
        ctx = lax.axis_index("ctx")
        head = lax.axis_index("head")
        core = ctx % 2
        place_of = [0] * chips
        for at, chip in enumerate(ring):
            place_of[chip] = at
        place = jnp.array(place_of, jnp.int32)[ctx // 2]

        slot_ids = jnp.arange(n_ctx, dtype=jnp.int32)
        along = (place + slot_ids % chips) % chips
        chip_of = jnp.where(along < chips // 2, 2 * along, 2 * (chips - 1 - along) + 1)
        block_of = chip_of * 2 + (core + slot_ids // chips) % 2
        block_hot = (block_of[:, None] == slot_ids[None, :]).astype(F32)
        feature = jnp.arange(width, dtype=jnp.int32)
        wanted = jnp.repeat(block_of, db) * db + feature % db
        to_ring = (feature[:, None] == wanted[None, :]).astype(BF16)

        def reorder(rows):
            return dot(rows, to_ring)

        def restore(rows):
            return lax.dot_general(
                rows,
                to_ring.astype(F32),
                (((1,), (1,)), ((), ())),
                precision=lax.Precision.HIGHEST,
                preferred_element_type=F32,
            )

        offsets = jnp.arange(BLK, dtype=jnp.int32)
        first = (head == 0)[..., None, None]
        order = jnp.where(first, block_order, block_order[::-1])
        docs = jnp.where(first, doc_ids, doc_ids[::-1])
        own_blocks = lax.dynamic_slice(order, (jnp.int32(0), 2 * ctx), (SEQS, 2))
        q_positions = (own_blocks[:, :, None] * BLK + offsets[None, None, :]).reshape(SEQS, ROWS)
        ring_blocks = jnp.einsum(
            "ac,scb->sab", block_hot, order.reshape(SEQS, n_ctx, 2).astype(F32)
        ).astype(jnp.int32)
        k_positions = (ring_blocks[..., None] * BLK + offsets).reshape(SEQS, 1, n_ctx * ROWS)
        doc_blocks = docs.reshape(SEQS, -1, BLK)
        own_hot = (own_blocks[:, :, None] == jnp.arange(doc_blocks.shape[1])).astype(F32)
        q_docs = jnp.einsum("sab,sbj->saj", own_hot, doc_blocks.astype(F32)).astype(jnp.int32)
        q_docs = q_docs.reshape(SEQS, ROWS)
        q_starts = jnp.sum((docs[:, None, :] < q_docs[:, :, None]).astype(jnp.int32), axis=2)
        kpos = k_positions
        qpos, qstart = q_positions[:, :, None], q_starts[:, :, None]
        cosine, sine_table = rope_tables(q_positions.reshape(token_rows))
        scale_q = HEAD_SIZE ** (-0.5)

        def both_rows(rows):
            return jnp.concatenate([rows, swap_head(rows)], axis=0)

        def to_owner(parts):
            return parts[:own_rows] + swap_head(parts[own_rows:].astype(BF16)).astype(F32)

        def project(rows, weight, lo, hi):
            return dot(rows, weight[:, lo:hi])

        def project_back(rows, weight, lo, hi):
            return dot_nt(rows, weight[:, lo:hi])

        def weight_grad(left, right):
            lefts = jnp.concatenate([left[:, :side], swap_core(left[:, side:])], axis=0)
            rights = jnp.concatenate([right, swap_core(right)], axis=0)
            return dot_tn(lefts, rights)

        def units(rows):
            shaped = rows.reshape(SEQS, ROWS, heads_kv, group, HEAD_SIZE)
            return shaped.transpose(0, 2, 3, 1, 4).reshape(SEQS, heads_kv, group * ROWS, HEAD_SIZE)

        def from_units(parts):
            shaped = parts.reshape(SEQS, heads_kv, group, ROWS, HEAD_SIZE)
            return shaped.transpose(0, 3, 1, 2, 4).reshape(token_rows, q_width)

        qkv_width = q_width + 2 * kv_width
        attn_width = qkv_width + q_width
        grad_res = reorder(cotangent)
        attn_shards = [
            jnp.concatenate(
                [w_query[layer], w_key[layer], w_value[layer], w_out[layer].T], axis=1
            )
            for layer in range(layers)
        ]
        mlp_shards = [
            jnp.concatenate([w_gate[layer], w_up[layer], w_down[layer].T], axis=1)
            for layer in range(layers)
        ]

        def forward_by_ops(residual):
            gains = lax.all_gather(
                jnp.concatenate([attn_gain, mlp_gain], axis=0), "ctx", axis=1, tiled=True
            )
            gains = reorder(gains)
            fetched = [
                (gather(attn), gather(mlp)) for attn, mlp in zip(attn_shards, mlp_shards)
            ]
            records = []
            for layer in range(layers):
                attn_w, mlp_w = fetched[layer]
                gain_a, gain_m = gains[layer], gains[layers + layer]
                residual_in = residual
                normed_a = both_rows((residual * rms_inverse(residual) * gain_a).astype(BF16))
                projected = project(normed_a, attn_w, 0, qkv_width)
                q_rows = rotate(
                    projected[:, :q_width].reshape(token_rows, heads_q, HEAD_SIZE),
                    cosine,
                    sine_table,
                )
                queries = units((q_rows * scale_q).astype(BF16).reshape(token_rows, q_width))
                keys = rotate(
                    projected[:, q_width : q_width + kv_width].reshape(
                        token_rows, heads_kv, HEAD_SIZE
                    ),
                    cosine,
                    sine_table,
                ).reshape(token_rows, kv_width)
                kv_shard = jnp.concatenate([keys, projected[:, q_width + kv_width :]], axis=1)
                kv_own = ring_gather(kv_shard.astype(BF16).T)
                kv = jnp.concatenate([kv_own, swap_core(kv_own)], axis=0)
                mixed, lse = attend_forward(queries, kv, kpos, qpos, qstart)
                attended = from_units(mixed)
                middle = residual + to_owner(
                    project_back(attended, attn_w, qkv_width, attn_width)
                )
                normed_m = both_rows((middle * rms_inverse(middle) * gain_m).astype(BF16))
                gate_up = project(normed_m, mlp_w, 0, 2 * ff_width)
                gate_part, up_part = gate_up[:, :ff_width], gate_up[:, ff_width:]
                activated = (jax.nn.silu(gate_part) * up_part).astype(BF16)
                residual = middle + to_owner(
                    project_back(activated, mlp_w, 2 * ff_width, 3 * ff_width)
                )
                records.append(
                    (
                        residual_in,
                        normed_a,
                        queries,
                        kv,
                        lse,
                        attended,
                        middle,
                        normed_m,
                        gate_part,
                        up_part,
                        activated,
                    )
                )
            return fetched, gains, records, residual

        def forward_by_kernel(residual):
            columns = jnp.concatenate([attn_gain, mlp_gain], axis=0).T
            columns = jnp.pad(columns, ((0, 0), (0, 128 - columns.shape[1])))
            shards = []
            for layer in range(layers):
                attn = attn_shards[layer]
                if layer == 0:
                    attn = jnp.concatenate([attn, columns], axis=1)
                shards += [attn, mlp_shards[layer]]
            weights, saved = forward(
                residual,
                shards,
                cosine.T,
                sine_table.T,
                kpos,
                qpos,
                qstart,
                chips,
                q_width,
                kv_width,
                ff_width,
            )
            residual_ins = jnp.concatenate([residual[None], saved[10][: layers - 1]], axis=0)
            tables = (cosine.T, sine_table.T, kpos, qpos, qstart)
            records = [*saved[:10], residual_ins, saved[11]]
            return weights, tables, records, saved[10][layers - 1]

        in_kernel = n_ctx * ROWS <= 2048 and db == HEAD_SIZE
        run_forward = forward_by_kernel if in_kernel else forward_by_ops
        fetched, gains, records, residual = run_forward(reorder(hidden_in))
        out_hidden = lax.dot_general(
            residual.astype(BF16), to_ring, (((1,), (1,)), ((), ())), preferred_element_type=F32
        ).astype(BF16)

        def norm_back(grad_res, normed_gradient, value_rows, inverse_norm, gain):
            normalized = value_rows * inverse_norm
            gain_gradient = jnp.sum(normed_gradient * normalized, axis=0)
            scaled = normed_gradient * gain
            mean = jnp.mean(scaled * normalized, axis=-1, keepdims=True)
            return grad_res + inverse_norm * (scaled - normalized * mean), gain_gradient

        def backward_by_ops(grad_res):
            d_attn = [None] * layers
            d_mlp = [None] * layers
            d_gains = [None] * (2 * layers)
            for layer in reversed(range(layers)):
                attn_w, mlp_w = fetched[layer]
                gain_a, gain_m = gains[layer], gains[layers + layer]
                (
                    residual_in,
                    normed_a,
                    queries,
                    kv,
                    lse,
                    attended,
                    middle,
                    normed_m,
                    gate_part,
                    up_part,
                    activated,
                ) = records[layer]
                inverse_a, inverse_m = rms_inverse(residual_in), rms_inverse(middle)
                grad_rows_m = both_rows(grad_res.astype(BF16))
                grad_act = project(grad_rows_m, mlp_w, 2 * ff_width, 3 * ff_width)
                sigmoid_g = jax.nn.sigmoid(gate_part)
                grad_gate = grad_act * up_part * sigmoid_g * (1.0 + gate_part * (1.0 - sigmoid_g))
                grad_up = grad_act * gate_part * sigmoid_g
                grad_gu = jnp.concatenate([grad_gate, grad_up], axis=1).astype(BF16)
                grad_norm_m = to_owner(project_back(grad_gu, mlp_w, 0, 2 * ff_width))
                d_down = weight_scatter(weight_grad(grad_rows_m, activated))
                d_gu = weight_scatter(weight_grad(normed_m, grad_gu))
                grad_res, d_gains[layers + layer] = norm_back(
                    grad_res, grad_norm_m, middle, inverse_m, gain_m
                )
                grad_rows_a = both_rows(grad_res.astype(BF16))
                grad_attended = project(grad_rows_a, attn_w, qkv_width, attn_width).astype(BF16)
                d_out = weight_grad(grad_rows_a, attended)
                grad_q, dk, dv = attend_backward(
                    queries, units(grad_attended), lse, kv, kpos, qpos, qstart
                )
                dk_back, dv_back = swap_core(dk[chips:]), swap_core(dv[chips:])
                grad_k, grad_v = ring_scatter(
                    dk[:chips].astype(F32) + dk_back.astype(F32),
                    dv[:chips].astype(F32) + dv_back.astype(F32),
                )
                grad_q_pre = rotate_back(
                    from_units(grad_q).reshape(token_rows, heads_q, HEAD_SIZE), cosine, sine_table
                )
                grad_k_pre = rotate_back(
                    grad_k.T.reshape(token_rows, heads_kv, HEAD_SIZE), cosine, sine_table
                )
                grad_qkv = jnp.concatenate(
                    [
                        (grad_q_pre * scale_q).reshape(token_rows, q_width),
                        grad_k_pre.reshape(token_rows, kv_width),
                        grad_v.T,
                    ],
                    axis=1,
                ).astype(BF16)
                grad_norm_a = to_owner(project_back(grad_qkv, attn_w, 0, qkv_width))
                d_qkv = weight_grad(normed_a, grad_qkv)
                d_attn[layer] = weight_scatter(jnp.concatenate([d_qkv, d_out], axis=1))
                d_mlp[layer] = (d_gu, d_down)
                grad_res, d_gains[layer] = norm_back(
                    grad_res, grad_norm_a, residual_in, inverse_a, gain_a
                )
            d_mlp = [
                jnp.stack([down, gu[:, :ff_width], gu[:, ff_width:]], axis=0) for gu, down in d_mlp
            ]
            return (
                grad_res,
                jnp.stack(d_gains, axis=0),
                jnp.stack(d_mlp, axis=0),
                jnp.stack(d_attn, axis=0),
            )

        if in_kernel:
            grad_res, d_gains, d_mlp, d_attn = backward(
                grad_res, fetched, records, gains, chips, q_width, kv_width, ff_width
            )
        else:
            grad_res, d_gains, d_mlp, d_attn = backward_by_ops(grad_res)
        d_hidden = restore(grad_res)
        d_gains = restore(d_gains)
        d_gains = d_gains + swap_head(d_gains)
        bit = 1
        while bit < n_ctx:
            d_gains = d_gains + lax.ppermute(d_gains, "ctx", [(i, i ^ bit) for i in range(n_ctx)])
            bit *= 2
        d_gains = lax.dynamic_slice(d_gains, (0, ctx * db), (2 * layers, db))
        k_at, v_at = q_width, q_width + kv_width
        return (
            out_hidden,
            d_hidden,
            d_gains[:layers],
            d_attn[:, :, :k_at],
            d_attn[:, :, k_at:v_at],
            d_attn[:, :, v_at:qkv_width],
            d_attn[:, :, qkv_width:].transpose(0, 2, 1),
            d_gains[layers:],
            d_mlp[:, 1],
            d_mlp[:, 2],
            d_mlp[:, 0].transpose(0, 2, 1),
        )

    return local


def solution(mesh):
    return jax.shard_map(
        build(mesh.shape["ctx"]),
        mesh=mesh,
        in_specs=(
            P(("ctx", "head"), None),
            P(),
            P(),
            P(None, "ctx"),
            P(None, "ctx", "head"),
            P(None, "ctx", "head"),
            P(None, "ctx", "head"),
            P(None, "head", "ctx"),
            P(None, "ctx"),
            P(None, "ctx", "head"),
            P(None, "ctx", "head"),
            P(None, "head", "ctx"),
            P(("ctx", "head"), None),
        ),
        out_specs=(
            P(("ctx", "head"), None),
            P(("ctx", "head"), None),
            P(None, "ctx"),
            P(None, "ctx", "head"),
            P(None, "ctx", "head"),
            P(None, "ctx", "head"),
            P(None, "head", "ctx"),
            P(None, "ctx"),
            P(None, "ctx", "head"),
            P(None, "ctx", "head"),
            P(None, "head", "ctx"),
        ),
        check_vma=False,
    )
```

```python
import functools
import math

import jax
import jax.numpy as jnp
from jax import lax
from jax.experimental import pallas as pl
from jax.experimental.pallas import tpu as pltpu
from jax.sharding import PartitionSpec as P

HEAD_SIZE = 96
HALF = HEAD_SIZE // 2
SEQS = 2
BLK = 64
ROWS = 2 * BLK

NEG = -1e30
EPS = 1e-05
THETA = 100000.0
VMEM_LIMIT = 56 * 1024 * 1024
KERNEL_VMEM = 62 * 1024 * 1024
MESH = pl.DeviceIdType.MESH
BF16 = jnp.bfloat16
F32 = jnp.float32


def ring_of(chips):
    return list(range(0, chips, 2)) + list(range(chips - 1, 0, -2))


def rope_tables(positions):
    freq_row = jnp.exp(jnp.arange(HALF, dtype=F32) * (-2.0 * math.log(THETA) / HEAD_SIZE))
    angles = positions.astype(F32)[:, None] * freq_row[None, :]
    return (jnp.cos(angles), jnp.sin(angles))


def rotate(tensor, cosine, sine_table):
    first, second = tensor[..., :HALF], tensor[..., HALF:]
    cos_wide, sin_wide = cosine[:, None, :], sine_table[:, None, :]
    return jnp.concatenate(
        [first * cos_wide - second * sin_wide, second * cos_wide + first * sin_wide], axis=-1
    )


def rotate_back(tensor, cosine, sine_table):
    first, second = tensor[..., :HALF], tensor[..., HALF:]
    cos_wide, sin_wide = cosine[:, None, :], sine_table[:, None, :]
    return jnp.concatenate(
        [first * cos_wide + second * sin_wide, second * cos_wide - first * sin_wide], axis=-1
    )


def dot(left, right):
    return jnp.dot(left, right, preferred_element_type=F32)


def dot_nt(left, right):
    return lax.dot_general(left, right, (((1,), (1,)), ((), ())), preferred_element_type=F32)


def dot_tn(left, right):
    return lax.dot_general(left, right, (((0,), (0,)), ((), ())), preferred_element_type=F32)


def row_tile(keys):
    return 256 if keys <= 2048 else 64


def gathered(ref):
    return jnp.concatenate([ref[j] for j in range(ref.shape[0])], axis=1)


def mask_rows(kpos_ref, qpos_ref, qstart_ref, start, rows):
    kpos = kpos_ref[0]
    parts = []
    done = 0
    while done < rows:
        at = (start + done) % ROWS
        size = min(rows - done, ROWS - at)
        qpos = qpos_ref[0, at : at + size, :]
        qstart = qstart_ref[0, at : at + size, :]
        parts.append((kpos <= qpos) & (kpos >= qstart))
        done += size
    return parts


def masked(scores, parts):
    out = []
    at = 0
    for part in parts:
        size = part.shape[0]
        out.append(jnp.where(part, scores[at : at + size, :], NEG))
        at += size
    return jnp.concatenate(out, axis=0) if len(out) > 1 else out[0]


def attend_kernel(q_ref, k_ref, v_ref, kpos_ref, qpos_ref, qstart_ref, o_ref, lse_ref):
    total = q_ref.shape[2]
    kt = gathered(k_ref)
    vt = gathered(v_ref)
    tile = min(total, row_tile(kt.shape[1]))
    for at in range(0, total, tile):
        q = q_ref[0, 0, at : at + tile, :]
        scores = masked(dot(q, kt), mask_rows(kpos_ref, qpos_ref, qstart_ref, at, tile))
        top = jnp.max(scores, axis=1, keepdims=True)
        weights = jnp.exp(scores - top)
        norm = jnp.sum(weights, axis=1, keepdims=True)
        probs = (weights * (1.0 / norm)).astype(BF16)
        o_ref[0, 0, at : at + tile, :] = dot_nt(probs, vt).astype(BF16)
        lse_ref[0, 0, at : at + tile, :] = top + jnp.log(norm)


def attend_back_kernel(
    q_ref,
    do_ref,
    lse_ref,
    k_ref,
    v_ref,
    kpos_ref,
    qpos_ref,
    qstart_ref,
    dq_ref,
    dk_ref,
    dv_ref,
):
    total = q_ref.shape[2]
    kt = gathered(k_ref)
    vt = gathered(v_ref)
    tile = min(total, row_tile(kt.shape[1]))
    dkt = None
    dvt = None
    for at in range(0, total, tile):
        q = q_ref[0, 0, at : at + tile, :]
        grad = do_ref[0, 0, at : at + tile, :]
        scores = masked(dot(q, kt), mask_rows(kpos_ref, qpos_ref, qstart_ref, at, tile))
        probs = jnp.exp(scores - lse_ref[0, 0, at : at + tile, :])
        dprobs = dot(grad, vt)
        delta = jnp.sum(probs * dprobs, axis=1, keepdims=True)
        dscores = (probs * (dprobs - delta)).astype(BF16)
        dq_ref[0, 0, at : at + tile, :] = dot_nt(dscores, kt)
        dk_part = dot_tn(q, dscores)
        dv_part = dot_tn(grad, probs.astype(BF16))
        dkt = dk_part if dkt is None else dkt + dk_part
        dvt = dv_part if dvt is None else dvt + dv_part
    for j in range(dk_ref.shape[0]):
        dk_ref[j] = dkt[:, j * ROWS : (j + 1) * ROWS].astype(BF16)
        dv_ref[j] = dvt[:, j * ROWS : (j + 1) * ROWS].astype(BF16)


def attention_specs(q, kv, kpos):
    slots = kv.shape[0]
    kv_heads = kv.shape[1] // (2 * HEAD_SIZE)
    keys = kpos.shape[2]
    rows = q.shape[2]
    unit = pl.BlockSpec((1, 1, rows, HEAD_SIZE), lambda s, h: (s, h, 0, 0))
    column = pl.BlockSpec((1, 1, rows, 1), lambda s, h: (s, h, 0, 0))
    k_spec = pl.BlockSpec((slots, HEAD_SIZE, ROWS), lambda s, h: (0, h, s))
    v_spec = pl.BlockSpec((slots, HEAD_SIZE, ROWS), lambda s, h: (0, kv_heads + h, s))
    kpos_spec = pl.BlockSpec((1, 1, keys), lambda s, h: (s, 0, 0))
    q_spec = pl.BlockSpec((1, ROWS, 1), lambda s, h: (s, 0, 0))
    return kv_heads, unit, column, k_spec, v_spec, kpos_spec, q_spec


def attend_forward(q, kv, kpos, qpos, qstart):
    kv_heads, unit, column, k_spec, v_spec, kpos_spec, q_spec = attention_specs(q, kv, kpos)
    rows, keys = q.shape[2], kpos.shape[2]
    work = SEQS * kv_heads * rows * keys
    return pl.pallas_call(
        attend_kernel,
        grid=(SEQS, kv_heads),
        in_specs=[unit, k_spec, v_spec, kpos_spec, q_spec, q_spec],
        out_specs=[unit, column],
        out_shape=[
            jax.ShapeDtypeStruct(q.shape, BF16),
            jax.ShapeDtypeStruct(q.shape[:3] + (1,), F32),
        ],
        compiler_params=pltpu.CompilerParams(vmem_limit_bytes=VMEM_LIMIT),
        cost_estimate=pl.CostEstimate(
            flops=8 * HEAD_SIZE * work, bytes_accessed=8 * 2**20, transcendentals=work
        ),
    )(q, kv, kv, kpos, qpos, qstart)


def attend_backward(q, grad, lse, kv, kpos, qpos, qstart):
    kv_heads, unit, column, k_spec, v_spec, kpos_spec, q_spec = attention_specs(q, kv, kpos)
    rows, keys = q.shape[2], kpos.shape[2]
    work = SEQS * kv_heads * rows * keys
    slots = kv.shape[0]
    grad_spec = pl.BlockSpec((slots, HEAD_SIZE, ROWS), lambda s, h: (0, h, s))
    grad_shape = jax.ShapeDtypeStruct((slots, kv_heads * HEAD_SIZE, SEQS * ROWS), BF16)
    return pl.pallas_call(
        attend_back_kernel,
        grid=(SEQS, kv_heads),
        in_specs=[unit, unit, column, k_spec, v_spec, kpos_spec, q_spec, q_spec],
        out_specs=[unit, grad_spec, grad_spec],
        out_shape=[jax.ShapeDtypeStruct(q.shape, F32)] + [grad_shape] * 2,
        compiler_params=pltpu.CompilerParams(vmem_limit_bytes=VMEM_LIMIT),
        cost_estimate=pl.CostEstimate(
            flops=20 * HEAD_SIZE * work, bytes_accessed=16 * 2**20, transcendentals=work
        ),
    )(q, grad, lse, kv, kv, kpos, qpos, qstart)


def ring_neighbours(chips):
    ctx = lax.axis_index("ctx")
    chip, core, half = ctx // 2, ctx % 2, chips // 2
    odd = chip % 2
    place = odd * (chips - 1 - chip // 2) + (1 - odd) * (chip // 2)

    def device(at):
        far = at // half
        return ((1 - far) * 2 * at + far * (2 * (chips - 1 - at) + 1)) * 2 + core

    return device((place + 1) % chips), device((place + chips - 1) % chips), ctx + 1 - 2 * core


class Links:
    def __init__(self, chips, send_sems, recv_sems):
        self.chips = chips
        self.right, self.left, self.sib = ring_neighbours(chips)
        self.head = lax.axis_index("head")
        self.ctx = lax.axis_index("ctx")
        self.send_sems, self.recv_sems = send_sems, recv_sems
        self.used = 0
        self.started = []

    def greet(self):
        barrier = pltpu.get_barrier_semaphore()
        for target in (self.right, self.left, self.sib):
            pl.semaphore_signal(barrier, inc=1, device_id=(target, self.head), device_id_type=MESH)
        pl.semaphore_signal(
            barrier, inc=1, device_id=(self.ctx, 1 - self.head), device_id_type=MESH
        )
        pl.semaphore_wait(barrier, 4)

    def copy(self, src, dst, target):
        copy = pltpu.make_async_remote_copy(
            src_ref=src,
            dst_ref=dst,
            send_sem=self.send_sems.at[self.used],
            recv_sem=self.recv_sems.at[self.used],
            device_id=target,
            device_id_type=MESH,
        )
        self.used += 1
        copy.start()
        self.started.append(copy)
        return copy

    def to_right(self, src, dst):
        return self.copy(src, dst, (self.right, self.head))

    def to_left(self, src, dst):
        return self.copy(src, dst, (self.left, self.head))

    def to_sibling(self, src, dst):
        return self.copy(src, dst, (self.sib, self.head))

    def to_head(self, src, dst):
        return self.copy(src, dst, (self.ctx, 1 - self.head))

    def sent(self, copy):
        if any(other is copy for other in self.started):
            copy.wait_send()
            self.started = [other for other in self.started if other is not copy]

    def finish(self):
        for copy in self.started:
            copy.wait_send()
        self.started = []


class RingGather:
    def __init__(self, links, ref, chains, first=None):
        self.links, self.ref, self.chains = links, ref, chains
        self.first = first
        self.moving = {}
        self.arriving = []
        self.steps = links.chips // 2
        self.events = [(c, s) for s in range(1, self.steps + 1) for c in range(len(chains))]

    @staticmethod
    def copies(chips, chains):
        return chains * (chips + chips)

    def window(self, slot, chain, part=None):
        r0, rn, c0, cn = self.chains[chain]
        if part is not None:
            rn = rn // 2
            r0 = r0 + part * rn
        if slot == 0 and self.first is not None:
            return self.first.at[pl.ds(r0, rn), pl.ds(c0, cn)]
        return self.ref.at[slot, pl.ds(r0, rn), pl.ds(c0, cn)]

    def share(self, slot, chain):
        r0, rn, c0, cn = self.chains[chain]
        there = self.ref.at[self.links.chips + slot, pl.ds(r0, rn), pl.ds(c0, cn)]
        self.arriving.append(self.links.to_sibling(self.window(slot, chain), there))

    def issue(self, event):
        chain, step = event
        chips = self.links.chips
        last = step == self.steps
        up_from, up_to = (chips - step + 1) % chips, chips - step
        r0, rn, c0, cn = self.chains[chain]

        def there(slot, part):
            rows = (r0, rn) if part is None else (r0 + part * (rn // 2), rn // 2)
            return self.ref.at[slot, pl.ds(*rows), pl.ds(c0, cn)]

        up = 0 if last else None
        down = 1 if last else None
        self.moving[event] = (
            self.links.to_right(self.window(up_from, chain, up), there(up_to, up)),
            self.links.to_left(self.window(step - 1, chain, down), there(step, down)),
        )
        if step == 1:
            self.share(0, chain)

    def land(self, event):
        chain, step = event
        for copy in self.moving[event]:
            copy.wait_recv()
        self.share(self.links.chips - step, chain)
        if step != self.steps:
            self.share(step, chain)

    def settle(self):
        for copy in self.arriving:
            copy.wait_recv()


class Queue:
    def __init__(self, rings, depth=4):
        self.waiting = [(ring, event) for ring in rings for event in ring.events]
        self.depth = depth
        self.flying = []
        self.landed = set()
        self.fill()

    def fill(self):
        for item in list(self.waiting):
            if len(self.flying) == self.depth:
                break
            ring, (chain, step) = item
            if step == 1 or (id(ring), chain, step - 1) in self.landed:
                ring.issue((chain, step))
                self.waiting.remove(item)
                self.flying.append(item)

    def pump(self, count=1):
        for _ in range(count):
            if self.flying:
                ring, event = self.flying.pop(0)
                ring.land(event)
                self.landed.add((id(ring), *event))
                self.fill()

    def through(self, ring):
        while any(item[0] is ring for item in self.flying + self.waiting):
            self.pump()


TILE = 512


def rms_inverse(rows):
    return lax.rsqrt(jnp.mean(rows * rows, axis=-1, keepdims=True) + EPS)


def windows_of(wide, count):
    blocks = wide // 128
    edges = [blocks * i // count * 128 for i in range(count + 1)]
    return [(low, high - low) for low, high in zip(edges, edges[1:])]


CHAINS = (4, 4, 2)


def forward_kernel(dims, *refs):
    layers, chips, width, q_width, kv_width, ff = dims
    slots = 2 * chips
    parts = len(CHAINS)
    it = iter(refs)
    x_ref, g_ref = next(it), next(it)
    shards = [next(it) for _ in range(parts * layers)]
    cos_ref, sin_ref, kpos_ref, qpos_ref, qstart_ref = (next(it) for _ in range(5))
    weights = [next(it) for _ in range(parts * layers)]
    saved = [next(it) for _ in range(10)]
    x_out_ref, gain_ref, g_rows_ref = next(it), next(it), next(it)
    kept = [next(it) for _ in range(10)]
    (
        kv_ref, normed_a_ref, qt_ref, lse_ref, att_ref, middle_ref, normed_m_ref, gate_ref, up_ref, act_ref
    ) = kept
    (
        wt, wo, acc, proj_t, att_t, b_send, b_recv, gain_block,
        g_rows, send_sems, recv_sems, load_sems, own_sems, save_sems,
    ) = (next(it) for _ in range(14))

    rows = x_ref.shape[0]
    db = width // slots
    heads_kv = kv_width // HEAD_SIZE
    group = q_width // kv_width
    qkv_width = q_width + 2 * kv_width
    links = Links(chips, send_sems, recv_sems)
    own_copies = []
    for i, (shard, weight) in enumerate(zip(shards, weights)):
        own_copies.append(pltpu.make_async_copy(shard, weight.at[0], own_sems.at[i]))
        own_copies[-1].start()
    links.greet()

    rings = []
    for i, (shard, weight) in enumerate(zip(shards, weights)):
        chains = [(0, db, c0, cn) for c0, cn in windows_of(shard.shape[1], CHAINS[i % parts])]
        rings.append(RingGather(links, weight, chains, first=shard))
    queue = Queue(rings)

    def ready(i):
        queue.through(rings[i])
        rings[i].settle()
        own_copies[i].wait()

    def load(i, column, wide, target, sem):
        copy = pltpu.make_async_copy(
            weights[i].at[:, :, pl.ds(column, wide)], target, load_sems.at[sem]
        )
        copy.start()
        return copy

    def flat(ref):
        return ref[...].reshape(width, ref.shape[-1])

    saving = []

    def save(i, layer):
        copy = pltpu.make_async_copy(
            kept[i].at[layer], saved[i].at[layer], save_sems.at[layer * len(kept) + i]
        )
        copy.start()
        saving.append(copy)

    g_rows[0:rows, :] = g_ref[...]
    g_swap = links.to_head(g_rows.at[pl.ds(0, rows), :], g_rows.at[pl.ds(rows, rows), :])

    ready(0)
    side = qkv_width + q_width
    load(0, side, 128, gain_block, 0).wait()
    gain_ref[...] = flat(gain_block).astype(F32).T[: gain_ref.shape[0], :]

    for layer in range(layers):
        attn, gate_up, down_w = parts * layer, parts * layer + 1, parts * layer + 2
        if layer:
            ready(attn)
        tiles = qkv_width // TILE
        order = list(reversed(range(tiles)))
        tile_loads = {t: load(attn, t * TILE, TILE, wt.at[t], t) for t in order}
        out_load = load(attn, qkv_width, q_width, wo, 6)

        x = x_ref[...] if layer == 0 else x_out_ref[layer - 1]
        gain_a = gain_ref[layer : layer + 1, :]
        normed_a_ref[layer, 0:rows, :] = (x * rms_inverse(x) * gain_a).astype(BF16)
        swap = links.to_head(
            normed_a_ref.at[layer, pl.ds(0, rows), :], normed_a_ref.at[layer, pl.ds(rows, rows), :]
        )

        def project(t, at):
            part = dot(normed_a_ref[layer, at : at + rows, :], flat(wt.at[t]))
            proj_t[t * TILE : (t + 1) * TILE, at : at + rows] = part.T

        for t in order:
            tile_loads[t].wait()
            project(t, 0)
        swap.wait_recv()
        first_kv = q_width // TILE
        for t in order:
            if t >= first_kv:
                project(t, rows)

        cosine, sine = cos_ref[...], sin_ref[...]

        def turned(at):
            low = proj_t[at : at + HALF, :]
            high = proj_t[at + HALF : at + HEAD_SIZE, :]
            return low * cosine - high * sine, high * cosine + low * sine

        for h in range(heads_kv):
            low, high = turned(q_width + h * HEAD_SIZE)
            kv_ref[layer, 0, h * HEAD_SIZE : h * HEAD_SIZE + HALF, :] = low.astype(BF16)
            kv_ref[layer, 0, h * HEAD_SIZE + HALF : (h + 1) * HEAD_SIZE, :] = high.astype(BF16)
        kv_ref[layer, 0, kv_width : 2 * kv_width, :] = proj_t[
            q_width + kv_width : qkv_width, :
        ].astype(BF16)
        wide = kv_ref.shape[-1]
        half = kv_width // 2
        kv_rings = [
            RingGather(
                links,
                kv_ref.at[layer],
                [(i * half, half, 0, wide), (kv_width + i * half, half, 0, wide)],
            )
            for i in range(2)
        ]
        kv_queue = Queue(kv_rings)
        for t in order:
            if t < first_kv:
                project(t, rows)
        scale = HEAD_SIZE ** (-0.5)
        for h in range(q_width // HEAD_SIZE):
            low, high = turned(h * HEAD_SIZE)
            qt_ref[layer, h * HEAD_SIZE : h * HEAD_SIZE + HALF, :] = (low * scale).astype(BF16)
            qt_ref[layer, h * HEAD_SIZE + HALF : (h + 1) * HEAD_SIZE, :] = (high * scale).astype(
                BF16
            )
        save(1, layer)
        save(2, layer)

        def unit(u, carry):
            h, s = u // SEQS, u % SEQS
            k_rows = pl.ds(pl.multiple_of(h * HEAD_SIZE, HEAD_SIZE), HEAD_SIZE)
            v_rows = pl.ds(pl.multiple_of(kv_width + h * HEAD_SIZE, HEAD_SIZE), HEAD_SIZE)
            lanes = pl.ds(pl.multiple_of(s * ROWS, ROWS), ROWS)
            kt = jnp.concatenate([kv_ref[layer, j, k_rows, lanes] for j in range(slots)], axis=1)
            vt = jnp.concatenate([kv_ref[layer, j, v_rows, lanes] for j in range(slots)], axis=1)
            q_rows = [
                pl.ds(pl.multiple_of((h * group + g) * HEAD_SIZE, HEAD_SIZE), HEAD_SIZE)
                for g in range(group)
            ]
            qt = jnp.concatenate([qt_ref[layer, at, lanes] for at in q_rows], axis=1)
            kpos, qpos, qstart = kpos_ref[s], qpos_ref[s], qstart_ref[s]
            allowed = (kpos <= qpos) & (kpos >= qstart)
            scores = masked(dot_tn(qt, kt), [allowed] * group)
            top = jnp.max(scores, axis=1, keepdims=True)
            raised = jnp.exp(scores - top)
            norm = jnp.sum(raised, axis=1, keepdims=True)
            probs = (raised * (1.0 / norm)).astype(BF16)
            mixed = dot_nt(vt, probs)
            for g, at in enumerate(q_rows):
                att_t[at, lanes] = mixed[:, g * ROWS : (g + 1) * ROWS]
            lse_ref[layer, u] = top + jnp.log(norm)
            return carry

        units = SEQS * heads_kv
        for i, ring in enumerate(kv_rings):
            kv_queue.through(ring)
            ring.settle()
            queue.pump(2)
            low, high = units * i // 2, units * (i + 1) // 2
            if i == 0:
                for u in range(low, high):
                    lax.fori_loop(u, u + 1, unit, 0)
                    kv_queue.pump(2)
            else:
                save(0, layer)
                middle_unit = (low + high) // 2
                lax.fori_loop(low, middle_unit, unit, 0)
                queue.pump(2)
                lax.fori_loop(middle_unit, high, unit, 0)
        queue.pump(2)
        att_ref[layer] = att_t[...].T.astype(BF16)
        save(3, layer)
        save(4, layer)

        out_load.wait()
        branch = (layer * 2) % b_send.shape[0]
        other = dot_nt(att_ref[layer, rows : 2 * rows, :], flat(wo))
        b_send[branch] = other.astype(BF16)
        swap = links.to_head(b_send.at[branch], b_recv.at[branch])
        mine = dot_nt(att_ref[layer, 0:rows, :], flat(wo))
        queue.pump(2)
        swap.wait_recv()
        middle = x + mine + b_recv[branch].astype(F32)
        middle_ref[layer] = middle
        save(5, layer)
        gain_m = gain_ref[layers + layer : layers + layer + 1, :]
        normed_m_ref[layer, 0:rows, :] = (middle * rms_inverse(middle) * gain_m).astype(BF16)
        swap = links.to_head(
            normed_m_ref.at[layer, pl.ds(0, rows), :], normed_m_ref.at[layer, pl.ds(rows, rows), :]
        )
        ready(gate_up)

        def load_tile(t):
            at = (t % 2) * 2
            return [
                load(gate_up, part * ff + t * TILE, TILE, wt.at[at + part], at + part)
                for part in range(2)
            ]

        pending = load_tile(0)
        swap.wait_recv()
        save(6, layer)
        normed = normed_m_ref[layer]
        count = ff // TILE
        for t in range(count):
            following = load_tile(t + 1) if t + 1 < count else None
            for copy in pending:
                copy.wait()
            at = (t % 2) * 2
            columns = slice(t * TILE, (t + 1) * TILE)
            gate = dot(normed, flat(wt.at[at]))
            up = dot(normed, flat(wt.at[at + 1]))
            gate_ref[layer, :, columns] = gate.astype(BF16)
            up_ref[layer, :, columns] = up.astype(BF16)
            act_ref[layer, :, columns] = (gate * jax.nn.sigmoid(gate) * up).astype(BF16)
            pending = following
            queue.pump()
        for i in (7, 8, 9):
            save(i, layer)
        ready(down_w)
        if layer == layers - 1:
            break

        def load_down(t):
            return load(down_w, t * TILE, TILE, wt.at[4 + t % 2], 4 + t % 2)

        pending = load_down(0)
        for t in range(count):
            following = load_down(t + 1) if t + 1 < count else None
            pending.wait()
            down = dot_nt(act_ref[layer, :, t * TILE : (t + 1) * TILE], flat(wt.at[4 + t % 2]))
            if t == 0:
                acc[...] = down
            else:
                acc[...] += down
            pending = following
        branch = (layer * 2 + 1) % b_send.shape[0]
        b_send[branch] = acc[rows : 2 * rows, :].astype(BF16)
        swap = links.to_head(b_send.at[branch], b_recv.at[branch])
        queue.pump(2)
        swap.wait_recv()
        x_out_ref[layer] = middle_ref[layer] + acc[0:rows, :] + b_recv[branch].astype(F32)
    g_swap.wait_recv()
    g_copy = pltpu.make_async_copy(g_rows, g_rows_ref, load_sems.at[0])
    g_copy.start()
    g_copy.wait()
    for copy in saving:
        copy.wait()
    links.finish()


def forward(x, grad, shards, cosine, sine, kpos, qpos, qstart, chips, q_width, kv_width, ff):
    parts = len(CHAINS)
    layers = len(shards) // parts
    rows, width = x.shape
    db = shards[0].shape[0]
    slots = 2 * chips
    group = q_width // kv_width
    tokens = 2 * rows
    units = SEQS * kv_width // HEAD_SIZE
    dims = (layers, chips, width, q_width, kv_width, ff)
    copies = layers * (RingGather.copies(chips, sum(CHAINS) + 4) + 4)
    any_spec = pl.BlockSpec(memory_space=pltpu.HBM)
    vmem = pl.BlockSpec(memory_space=pltpu.VMEM)
    saved = [
        ((layers, slots, 2 * kv_width, tokens), BF16),
        ((layers, tokens, width), BF16),
        ((layers, q_width, tokens), BF16),
        ((layers, units, group * ROWS, 1), F32),
        ((layers, tokens, q_width), BF16),
        ((layers, rows, width), F32),
        ((layers, tokens, width), BF16),
        ((layers, tokens, ff), BF16),
        ((layers, tokens, ff), BF16),
        ((layers, tokens, ff), BF16),
    ]
    out = pl.pallas_call(
        functools.partial(forward_kernel, dims),
        out_shape=[jax.ShapeDtypeStruct((slots,) + shard.shape, BF16) for shard in shards]
        + [jax.ShapeDtypeStruct(*entry) for entry in saved]
        + [
            jax.ShapeDtypeStruct((layers - 1, rows, width), F32),
            jax.ShapeDtypeStruct((2 * layers, width), F32),
            jax.ShapeDtypeStruct((tokens, width), BF16),
        ],
        in_specs=[vmem] * 2 + [any_spec] * len(shards) + [vmem] * 5,
        out_specs=[any_spec] * (len(shards) + len(saved)) + [vmem] * 2 + [any_spec],
        scratch_shapes=[pltpu.VMEM(*entry) for entry in saved]
        + [
            pltpu.VMEM((6, slots, db, TILE), BF16),
            pltpu.VMEM((slots, db, q_width), BF16),
            pltpu.VMEM((tokens, width), F32),
            pltpu.VMEM((q_width + 2 * kv_width, tokens), F32),
            pltpu.VMEM((q_width, tokens), F32),
            pltpu.VMEM((2 * layers, rows, width), BF16),
            pltpu.VMEM((2 * layers, rows, width), BF16),
            pltpu.VMEM((slots, db, 128), BF16),
            pltpu.VMEM((tokens, width), BF16),
            pltpu.SemaphoreType.DMA((copies,)),
            pltpu.SemaphoreType.DMA((copies,)),
            pltpu.SemaphoreType.DMA((7,)),
            pltpu.SemaphoreType.DMA((len(shards),)),
            pltpu.SemaphoreType.DMA((layers * len(saved),)),
        ],
        compiler_params=pltpu.CompilerParams(
            collective_id=0, has_side_effects=True, vmem_limit_bytes=KERNEL_VMEM
        ),
    )(x, grad, *shards, cosine, sine, kpos, qpos, qstart)
    return out[: len(shards)], out[len(shards) :]


class RingScatter:
    def __init__(self, links, windows, landings, finish, stage=None, sems=None):
        self.links, self.windows, self.landings = links, windows, landings
        self.stage, self.sems, self.finish = stage, sems, finish
        self.last = links.chips - 1
        self.step = 0
        self.moving = []

    def issue(self):
        self.step += 1
        chips = self.links.chips
        slots = ((chips - self.step) % chips, self.step % chips)
        sends = (self.links.to_right, self.links.to_left)
        self.moving = [
            sends[d](self.windows[d](slots[d]), self.landings[d](self.step - 1)) for d in range(2)
        ]

    def arrive(self, place=0):
        self.here, self.loads = [], []
        for d in range(2):
            self.moving[d].wait_recv()
            self.links.sent(self.moving[d])
            here = self.landings[d](self.step - 1)
            if self.stage is not None:
                there = self.stage.at[place, d, :, pl.ds(0, here.shape[-1])]
                load = pltpu.make_async_copy(here, there, self.sems.at[2 * place + d])
                load.start()
                self.loads.append(load)
                here = there
            self.here.append(here)

    def absorb(self):
        chips = self.links.chips
        for load in self.loads:
            load.wait()
        slots = ((chips - 1 - self.step) % chips, (1 + self.step) % chips)
        for d in range(2):
            window = self.windows[d](slots[d])
            total = window[...].astype(F32) + self.here[d][...].astype(F32)
            if self.step < self.last:
                window[...] = total.astype(BF16)
            else:
                self.finish(d, total)
        if self.step < self.last:
            self.issue()
            return False
        return True


class Rounds:
    def __init__(self, at_once=False):
        self.active, self.loading, self.place, self.at_once = [], None, 0, at_once

    def start(self, ring):
        ring.issue()
        self.active.append(ring)
        return ring

    def absorb(self):
        if self.loading is not None:
            ring, self.loading = self.loading, None
            if not ring.absorb():
                self.active.append(ring)

    def pump(self, count=1):
        self.absorb()
        for _ in range(count):
            if not self.active:
                break
            ring = self.active.pop(0)
            self.place = 1 - self.place
            ring.arrive(self.place)
            self.absorb()
            self.loading = ring
        if self.at_once:
            self.absorb()

    def drain(self, rings=None):
        def under_way():
            pending = self.active + ([] if self.loading is None else [self.loading])
            return [ring for ring in pending if rings is None or any(ring is one for one in rings)]

        while under_way():
            self.pump()


def backward_kernel(dims, *refs):
    layers, chips, width, q_width, kv_width, ff = dims
    slots = 2 * chips
    it = iter(refs)
    g_ref, g_rows_ref = next(it), next(it)
    parts = len(CHAINS)
    weights = [next(it) for _ in range(parts * layers)]
    (
        kv_ref, normed_a_ref, qt_ref, lse_ref, att_ref, middle_ref, normed_m_ref,
        gate_ref, up_ref, act_ref, x_in_ref, gain_ref,
        cos_ref, sin_ref, kpos_ref, qpos_ref, qstart_ref,
    ) = (next(it) for _ in range(17))
    d_hidden_ref, d_gain_ref, x_out_ref = next(it), next(it), next(it)
    d_query_ref, d_key_ref, d_value_ref, d_out_ref, d_w_gate_ref, d_w_up_ref, d_down_ref = (
        next(it) for _ in range(7)
    )
    land_down, land_gu, land_out, land_q = (next(it) for _ in range(4))
    (
        wt, kv_buf, dkv_sib, dw_mlp, dw_attn, a_sib, at_buf, g_act, g_gu, g_att, acc,
        g_low, g2_low, b_send, b_recv, qt_l, lse_l, da_t, dq_t, dkv_sum, gu_buf, rows_f32, n_own,
        stage, out_stage, turn_stage, land_kv, land_dkv, send_sems, recv_sems, load_sems, stage_sems,
    ) = (next(it) for _ in range(32))

    rows = g_ref.shape[0]
    tokens = 2 * rows
    db = width // slots
    side = width // 2
    heads_kv = kv_width // HEAD_SIZE
    group = q_width // kv_width
    qkv_width = q_width + 2 * kv_width
    links = Links(chips, send_sems, recv_sems)
    links.greet()
    g_qkv = g_gu.at[:, pl.ds(0, qkv_width)]
    rounds = Rounds()
    cosine, sine = cos_ref[...], sin_ref[...]
    scale = HEAD_SIZE ** (-0.5)

    def local(src, dst, sem):
        copy = pltpu.make_async_copy(src, dst, load_sems.at[sem])
        copy.start()
        return copy

    def load(i, column, wide, target, sem):
        return local(weights[i].at[:, :, pl.ds(column, wide)], target, sem)

    def flat(ref):
        return ref[...].reshape(width, ref.shape[-1])

    def write(d, total, target, turned):
        if turned:
            total = total.T
            source = turn_stage.at[d, pl.ds(0, total.shape[0]), :]
        else:
            source = out_stage.at[d, :, pl.ds(0, total.shape[1])]
        source[...] = total
        copy = pltpu.make_async_copy(source, target, stage_sems.at[4 + d])
        copy.start()
        copy.wait()

    def scatter(ref, column, sizes, landing, out, at, turned=False, staged=True):
        offsets = (0, sizes[0])

        def window(d):
            return lambda slot: ref.at[slot, :, pl.ds(column + offsets[d], sizes[d])]

        def land(d):
            return lambda step: landing.at[d, step, :, pl.ds(0, sizes[d])]

        def finish(d, total):
            there = pl.ds(at + offsets[d], sizes[d])
            write(d, total, out.at[there, :] if turned else out.at[:, there], turned)

        return rounds.start(
            RingScatter(
                links,
                (window(0), window(1)),
                (land(0), land(1)),
                finish,
                stage if staged else None,
                stage_sems,
            )
        )

    def turn_columns(own, sib):
        at_buf[:, 0:tokens] = own.astype(F32).T.astype(BF16)
        at_buf[:, tokens : 2 * tokens] = sib.astype(F32).T.astype(BF16)

    def weight_grad(target, column, right, wide):
        for c in range(0, wide, TILE):
            size = min(TILE, wide - c)
            part = dot(at_buf[...], right[:, c : c + size])
            target[:, :, column + c : column + c + size] = part.reshape(chips, db, size).astype(
                BF16
            )

    def norm_back(grad, value, gain, row):
        inverse = rms_inverse(value)
        normalized = value * inverse
        d_gain_ref[row : row + 1, :] = jnp.sum(grad * normalized, axis=0, keepdims=True)
        scaled = grad * gain
        mean = jnp.mean(scaled * normalized, axis=-1, keepdims=True)
        d_hidden_ref[...] += inverse * (scaled - normalized * mean)


    local(g_ref, d_hidden_ref, 10).wait()
    pairs = (heads_kv + 1) // 2
    mlp_rings, attn_rings = [], []
    for layer in reversed(range(layers)):
        attn, gate_up, down_w = parts * layer, parts * layer + 1, parts * layer + 2
        gain_a = gain_ref[layer : layer + 1, :]
        gain_m = gain_ref[layers + layer : layers + layer + 1, :]
        links.finish()

        def load_tile(t):
            at = (t % 2) * 3
            columns = pl.ds(t * TILE, TILE)
            return [
                load(down_w, t * TILE, TILE, wt.at[at + 2], at + 2),
                load(gate_up, t * TILE, TILE, wt.at[at], at),
                load(gate_up, ff + t * TILE, TILE, wt.at[at + 1], at + 1),
                local(gate_ref.at[layer, :, columns], gu_buf.at[t % 2, 0], 6 + t % 2 * 2),
                local(up_ref.at[layer, :, columns], gu_buf.at[t % 2, 1], 7 + t % 2 * 2),
            ]

        if layer == layers - 1:
            g_load = local(g_rows_ref, g_low, 11)
        else:
            g_low[0:rows, :] = d_hidden_ref[...].astype(BF16)
            swap = links.to_head(g_low.at[pl.ds(0, rows), :], g_low.at[pl.ds(rows, rows), :])
        far = pl.ds(side, side)
        other_rows = pl.ds(tokens, tokens)
        from_sib_act = links.to_sibling(act_ref.at[layer], g_act.at[other_rows, :])
        here_act = local(act_ref.at[layer], g_act.at[pl.ds(0, tokens), :], 10)
        pending = load_tile(0)
        from_sib = [
            links.to_sibling(normed_m_ref.at[layer, :, far], a_sib.at[1]),
            links.to_sibling(normed_a_ref.at[layer, :, far], a_sib.at[3]),
            links.to_sibling(att_ref.at[layer], g_att.at[other_rows, :]),
        ]
        here = [
            local(normed_m_ref.at[layer, :, pl.ds(0, side)], n_own, 13),
            local(att_ref.at[layer], g_att.at[pl.ds(0, tokens), :], 15),
            local(middle_ref.at[layer], rows_f32, 14),
            local(qt_ref.at[layer], qt_l, 16),
            local(lse_ref.at[layer], lse_l, 17),
        ]
        rounds.drain(mlp_rings)
        if layer == layers - 1:
            g_load.wait()
        else:
            swap.wait_recv()
        from_sib_g = links.to_sibling(g_low.at[:, far], a_sib.at[0])
        here_act.wait()
        from_sib_act.wait_recv()
        from_sib_g.wait_recv()
        turn_columns(g_low[:, 0:side], a_sib[0])
        weight_grad(dw_mlp.at[0], 0, g_act, ff)
        mlp_rings = []
        for i in range(2):
            size = ff // 4
            mlp_rings.append(
                scatter(
                    dw_mlp.at[0],
                    2 * i * size,
                    (size, size),
                    land_down.at[layer, i],
                    d_down_ref.at[layer],
                    2 * i * size,
                    turned=True,
                )
            )
        count = ff // TILE
        from_sib_gu = []
        for t in range(count):
            following = load_tile(t + 1) if t + 1 < count else None
            for copy in pending:
                copy.wait()
            at = (t % 2) * 3
            gate = gu_buf[t % 2, 0].astype(F32)
            up = gu_buf[t % 2, 1].astype(F32)
            d_act = dot(g_low[...], flat(wt.at[at + 2]))
            sig = jax.nn.sigmoid(gate)
            d_gate = (d_act * up * sig * (1.0 + gate * (1.0 - sig))).astype(BF16)
            d_up = (d_act * gate * sig).astype(BF16)
            for part, grad in enumerate((d_gate, d_up)):
                column = part * ff + t * TILE
                g_gu[0:tokens, column : column + TILE] = grad
                from_sib_gu.append(
                    links.to_sibling(
                        g_gu.at[pl.ds(0, tokens), pl.ds(column, TILE)],
                        g_gu.at[other_rows, pl.ds(column, TILE)],
                    )
                )
            if t == 0:
                acc[...] = dot_nt(d_gate, flat(wt.at[at]))
            else:
                acc[...] += dot_nt(d_gate, flat(wt.at[at]))
            acc[...] += dot_nt(d_up, flat(wt.at[at + 1]))
            pending = following
            rounds.pump(3 if len(rounds.active) > 2 else 1)
        b_send[0] = acc[rows:tokens, :].astype(BF16)
        swap = links.to_head(b_send.at[0], b_recv.at[0])
        out_loads = [
            load(attn, qkv_width, TILE, wt.at[4], 4),
            load(attn, qkv_width + TILE, q_width - TILE, wt.at[5, :, :, pl.ds(0, q_width - TILE)], 5),
        ]
        for copy in here:
            copy.wait()
        for copy in from_sib + from_sib_gu:
            copy.wait_recv()

        def gate_up_grad(part):
            weight_grad(dw_mlp.at[1 + part], 0, g_gu.at[:, pl.ds(part * ff, ff)], ff)
            out = (d_w_gate_ref, d_w_up_ref)[part].at[layer]
            return scatter(
                dw_mlp.at[1 + part], 0, (ff // 2, ff // 2), land_gu.at[layer, part], out, 0
            )

        turn_columns(n_own[...], a_sib[1])
        here = [local(normed_a_ref.at[layer, :, pl.ds(0, side)], n_own, 12)]
        mlp_rings.append(gate_up_grad(0))
        rounds.pump(2)
        swap.wait_recv()
        norm_back(
            acc[0:rows, :] + b_recv[0].astype(F32), rows_f32[...], gain_m, layers + layer
        )
        g2_low[0:rows, :] = d_hidden_ref[...].astype(BF16)
        swap = links.to_head(g2_low.at[pl.ds(0, rows), :], g2_low.at[pl.ds(rows, rows), :])
        mlp_rings.append(gate_up_grad(1))
        rounds.pump(2)
        rounds.drain(attn_rings)

        swap.wait_recv()
        from_sib_g = links.to_sibling(g2_low.at[:, far], a_sib.at[2])
        for i, copy in enumerate(out_loads):
            copy.wait()
            size = TILE if i == 0 else q_width - TILE
            part = dot(g2_low[...], flat(wt.at[4 + i, :, :, pl.ds(0, size)]))
            da_t[i * TILE : i * TILE + size, :] = part.T.astype(BF16)
        rounds.pump()
        if layer == layers - 1:
            def load_down(t):
                return load(down_w, t * TILE, TILE, wt.at[4 + t % 2], 4 + t % 2)

            pending = load_down(0)
            for t in range(count):
                following = load_down(t + 1) if t + 1 < count else None
                pending.wait()
                down = dot_nt(g_act[0:tokens, t * TILE : (t + 1) * TILE], flat(wt.at[4 + t % 2]))
                if t == 0:
                    acc[...] = down
                else:
                    acc[...] += down
                pending = following
            b_send[2] = acc[rows:tokens, :].astype(BF16)
            out_swap = links.to_head(b_send.at[2], b_recv.at[2])
            rows_f32[...] += acc[0:rows, :]
            rounds.pump(2)

        units = SEQS * heads_kv

        def unit_copies(u, at):
            h, s = u // SEQS, u % SEQS
            lanes = pl.ds(pl.multiple_of(s * ROWS, ROWS), ROWS)
            return [
                pltpu.make_async_copy(
                    kv_ref.at[
                        layer,
                        :,
                        pl.ds(pl.multiple_of(part * kv_width + h * HEAD_SIZE, HEAD_SIZE), HEAD_SIZE),
                        lanes,
                    ],
                    kv_buf.at[at, part],
                    load_sems.at[6 + 2 * at + part],
                )
                for part in range(2)
            ]

        def unit(u, carry):
            at = u % 2
            h, s = u // SEQS, u % SEQS
            for copy in unit_copies(u, at):
                copy.wait()
            ahead = jnp.minimum(u + 1, units - 1)

            @pl.when(u + 1 < units)
            def _():
                for copy in unit_copies(ahead, 1 - at):
                    copy.start()

            kt = jnp.concatenate([kv_buf[at, 0, j] for j in range(slots)], axis=1)
            vt = jnp.concatenate([kv_buf[at, 1, j] for j in range(slots)], axis=1)
            lanes = pl.ds(pl.multiple_of(s * ROWS, ROWS), ROWS)
            allowed = (kpos_ref[s] <= qpos_ref[s]) & (kpos_ref[s] >= qstart_ref[s])
            dkt = dvt = None
            for g in range(group):
                head_rows = pl.ds(
                    pl.multiple_of((h * group + g) * HEAD_SIZE, HEAD_SIZE), HEAD_SIZE
                )
                qt = qt_l[head_rows, lanes]
                dot_t = da_t[head_rows, lanes]
                scores = masked(dot_tn(qt, kt), [allowed])
                probs = jnp.exp(scores - lse_l[u, g * ROWS : (g + 1) * ROWS, :])
                dprobs = dot_tn(dot_t, vt)
                delta = jnp.sum(probs * dprobs, axis=1, keepdims=True)
                dscores = (probs * (dprobs - delta)).astype(BF16)
                dq_t[head_rows, lanes] = dot_nt(kt, dscores)
                dk_part = dot(qt, dscores)
                dv_part = dot(dot_t, probs.astype(BF16))
                dkt = dk_part if dkt is None else dkt + dk_part
                dvt = dv_part if dvt is None else dvt + dv_part
            spot = pl.ds(pl.multiple_of((h % 2) * SEQS * ROWS + s * ROWS, ROWS), ROWS)
            for j in range(slots):
                wt[h // 2, j, :, spot] = dkt[:, j * ROWS : (j + 1) * ROWS].astype(BF16)
                wt[pairs + h // 2, j, :, spot] = dvt[:, j * ROWS : (j + 1) * ROWS].astype(BF16)
            return carry

        sums = Rounds(at_once=True)
        sent = {}

        def offer(i):
            for j in (i, pairs + i):
                sent[j] = links.to_sibling(wt.at[j, pl.ds(chips, chips)], dkv_sib.at[j])

        def total_up(i):
            for j in (i, pairs + i):
                sent[j].wait_recv()
                for slot in range(chips):
                    wt[j, slot] = (wt[j, slot].astype(F32) + dkv_sib[j, slot].astype(F32)).astype(
                        BF16
                    )

            def finish(d, total):
                dkv_sum[d * pairs + i] = total

            sums.start(
                RingScatter(
                    links,
                    (lambda slot: wt.at[i, slot], lambda slot: wt.at[pairs + i, slot]),
                    (
                        lambda step: land_dkv.at[i, 0, step],
                        lambda step: land_dkv.at[i, 1, step],
                    ),
                    finish,
                )
            )

        for copy in unit_copies(0, 0):
            copy.start()
        for i in range(pairs):
            low, high = units * i // pairs, units * (i + 1) // pairs
            if i == 0:
                middle_unit = (low + high) // 2
                lax.fori_loop(low, middle_unit, unit, 0)
                rounds.pump(3)
                lax.fori_loop(middle_unit, high, unit, 0)
                rounds.pump(3)
            else:
                for u in range(low, high):
                    lax.fori_loop(u, u + 1, unit, 0)
                    if u == low:
                        total_up(i - 1)
                    else:
                        sums.pump(2)
                    rounds.pump()
            offer(i)

        if layer == layers - 1:
            out_swap.wait_recv()
            links.sent(out_swap)
            b_send[2] = (rows_f32[...] + b_recv[2].astype(F32)).astype(BF16)
            local(b_send.at[2], x_out_ref, 11).wait()
        here.append(local(x_in_ref.at[layer], rows_f32, 15))
        from_sib_g.wait_recv()
        turn_columns(g2_low[:, 0:side], a_sib[2])
        weight_grad(dw_attn, qkv_width, g_att, q_width)
        half = q_width // 2
        attn_rings = [
            scatter(
                dw_attn, qkv_width, (half, half), land_out.at[layer], d_out_ref.at[layer], 0, turned=True
            )
        ]
        total_up(pairs - 1)

        def turned_back(low, high):
            return low * cosine + high * sine, high * cosine - low * sine

        for h in range(q_width // HEAD_SIZE):
            at = h * HEAD_SIZE
            low, high = turned_back(
                dq_t[at : at + HALF, :], dq_t[at + HALF : at + HEAD_SIZE, :]
            )
            dq_t[at : at + HALF, :] = low * scale
            dq_t[at + HALF : at + HEAD_SIZE, :] = high * scale
        for copy in from_sib_gu:
            links.sent(copy)
        g_qkv[0:tokens, 0:q_width] = dq_t[...].T.astype(BF16)
        mine = pl.ds(0, tokens)
        from_sib_q = links.to_sibling(
            g_qkv.at[mine, pl.ds(0, q_width)], g_qkv.at[other_rows, pl.ds(0, q_width)]
        )
        step = 0
        while sums.active:
            sums.pump()
            step += 1
            if step % 3 == 0:
                rounds.pump()
            if step == 4:
                from_sib_q.wait_recv()
                for copy in here:
                    copy.wait()
                turn_columns(n_own[...], a_sib[3])
                weight_grad(dw_attn, 0, g_qkv, q_width)
                attn_rings.append(
                    scatter(
                        dw_attn, 0, (half, half), land_q.at[layer], d_query_ref.at[layer], 0
                    )
                )
        for h in range(heads_kv):
            spot = slice((h % 2) * SEQS * ROWS, (h % 2 + 1) * SEQS * ROWS)
            block = dkv_sum[h // 2, :, spot]
            low, high = turned_back(block[0:HALF, :], block[HALF:HEAD_SIZE, :])
            at = h * HEAD_SIZE
            dq_t[at : at + HALF, :] = low
            dq_t[at + HALF : at + HEAD_SIZE, :] = high
            dq_t[kv_width + at : kv_width + at + HEAD_SIZE, :] = dkv_sum[pairs + h // 2, :, spot]
        g_qkv[0:tokens, q_width:qkv_width] = dq_t[0 : 2 * kv_width, :].T.astype(BF16)
        from_sib_kv = links.to_sibling(
            g_qkv.at[mine, pl.ds(q_width, 2 * kv_width)],
            g_qkv.at[other_rows, pl.ds(q_width, 2 * kv_width)],
        )
        links.finish()
        tiles = [
            load(attn, t * TILE, TILE, wt.at[t], t) for t in range(qkv_width // TILE)
        ]
        for t, tile in enumerate(tiles):
            tile.wait()
            back = dot_nt(g_qkv[0:tokens, t * TILE : (t + 1) * TILE], flat(wt.at[t]))
            if t == 0:
                acc[...] = back
            else:
                acc[...] += back
        b_send[1] = acc[rows:tokens, :].astype(BF16)
        swap = links.to_head(b_send.at[1], b_recv.at[1])
        from_sib_kv.wait_recv()
        weight_grad(dw_attn, q_width, g_qkv.at[:, pl.ds(q_width, 2 * kv_width)], 2 * kv_width)
        long = -(-kv_width // 256) * 128
        short = kv_width - long
        for i, (out, sizes) in enumerate(
            ((d_key_ref, (long, short)), (d_value_ref, (short, long)))
        ):
            attn_rings.append(
                scatter(
                    dw_attn,
                    q_width + i * kv_width,
                    sizes,
                    land_kv.at[i],
                    out.at[layer],
                    0,
                    staged=False,
                )
            )
        rounds.pump()
        swap.wait_recv()
        norm_back(acc[0:rows, :] + b_recv[1].astype(F32), rows_f32[...], gain_a, layer)
    rounds.drain()
    links.finish()


def backward(grad, grad_rows, weights, saved, tables, chips, q_width, kv_width, ff):
    layers = len(weights) // len(CHAINS)
    rows, width = grad.shape
    slots = 2 * chips
    db = width // slots
    tokens = 2 * rows
    heads_kv = kv_width // HEAD_SIZE
    units = SEQS * heads_kv
    pairs = (heads_kv + 1) // 2
    group = q_width // kv_width
    steps = chips - 1
    qkv_width = q_width + 2 * kv_width
    dims = (layers, chips, width, q_width, kv_width, ff)
    rings = 4 + 4 + pairs
    copies = 1 + layers * (rings * 2 * steps + 4 + 4 + 1 + 2 * (ff // TILE) + 1 + 2 * pairs + 2)
    any_spec = pl.BlockSpec(memory_space=pltpu.HBM)
    vmem = pl.BlockSpec(memory_space=pltpu.VMEM)

    def landing(*shape):
        return jax.ShapeDtypeStruct(shape, BF16)

    out = pl.pallas_call(
        functools.partial(backward_kernel, dims),
        out_shape=[
            jax.ShapeDtypeStruct((rows, width), F32),
            jax.ShapeDtypeStruct((2 * layers, width), F32),
            jax.ShapeDtypeStruct((rows, width), BF16),
            jax.ShapeDtypeStruct((layers, db, q_width), F32),
            jax.ShapeDtypeStruct((layers, db, kv_width), F32),
            jax.ShapeDtypeStruct((layers, db, kv_width), F32),
            jax.ShapeDtypeStruct((layers, q_width, db), F32),
            jax.ShapeDtypeStruct((layers, db, ff), F32),
            jax.ShapeDtypeStruct((layers, db, ff), F32),
            jax.ShapeDtypeStruct((layers, ff, db), F32),
            landing(layers, 2, 2, steps, db, ff // 4),
            landing(layers, 2, 2, steps, db, ff // 2),
            landing(layers, 2, steps, db, q_width // 2),
            landing(layers, 2, steps, db, q_width // 2),
        ],
        in_specs=[any_spec] * (len(weights) + 13) + [vmem] * 6,
        out_specs=[vmem] * 2 + [any_spec] * 12,
        scratch_shapes=[
            pltpu.VMEM((6, slots, db, TILE), BF16),
            pltpu.VMEM((2, 2, slots, HEAD_SIZE, ROWS), BF16),
            pltpu.VMEM((2 * pairs, chips, HEAD_SIZE, 2 * SEQS * ROWS), BF16),
            pltpu.VMEM((3, chips, db, ff), BF16),
            pltpu.VMEM((chips, db, qkv_width + q_width), BF16),
            pltpu.VMEM((4, tokens, width // 2), BF16),
            pltpu.VMEM((width // 2, 2 * tokens), BF16),
            pltpu.VMEM((2 * tokens, ff), BF16),
            pltpu.VMEM((2 * tokens, 2 * ff), BF16),
            pltpu.VMEM((2 * tokens, q_width), BF16),
            pltpu.VMEM((tokens, width), F32),
            pltpu.VMEM((tokens, width), BF16),
            pltpu.VMEM((tokens, width), BF16),
            pltpu.VMEM((3, rows, width), BF16),
            pltpu.VMEM((3, rows, width), BF16),
            pltpu.VMEM((q_width, tokens), BF16),
            pltpu.VMEM((units, group * ROWS, 1), F32),
            pltpu.VMEM((q_width, tokens), BF16),
            pltpu.VMEM((q_width, tokens), F32),
            pltpu.VMEM((2 * pairs, HEAD_SIZE, 2 * SEQS * ROWS), F32),
            pltpu.VMEM((2, 2, tokens, TILE), BF16),
            pltpu.VMEM((rows, width), F32),
            pltpu.VMEM((tokens, width // 2), BF16),
            pltpu.VMEM((2, 2, db, ff // 2), BF16),
            pltpu.VMEM((2, db, ff // 2), F32),
            pltpu.VMEM((2, ff // 4, db), F32),
            pltpu.VMEM((2, 2, steps, db, -(-kv_width // 256) * 128), BF16),
            pltpu.VMEM((pairs, 2, steps, HEAD_SIZE, 2 * SEQS * ROWS), BF16),
            pltpu.SemaphoreType.DMA((copies,)),
            pltpu.SemaphoreType.DMA((copies,)),
            pltpu.SemaphoreType.DMA((18,)),
            pltpu.SemaphoreType.DMA((6,)),
        ],
        compiler_params=pltpu.CompilerParams(
            collective_id=1, has_side_effects=True, vmem_limit_bytes=KERNEL_VMEM
        ),
    )(grad, grad_rows, *weights, *saved, *tables)
    return out[:10]


def build(n_ctx):
    chips = n_ctx // 2
    ring = ring_of(chips)

    def shifted(step):
        pairs = []
        for at, chip in enumerate(ring):
            target = ring[(at + step) % chips]
            pairs += [(chip * 2 + core, target * 2 + core) for core in range(2)]
        return pairs

    up, down = shifted(1), shifted(-1)
    sibling = [(i, i ^ 1) for i in range(n_ctx)]

    def send_up(value):
        return lax.ppermute(value, "ctx", up)

    def send_down(value):
        return lax.ppermute(value, "ctx", down)

    def swap_core(value):
        return lax.ppermute(value, "ctx", sibling)

    def swap_head(value):
        return lax.ppermute(value, "head", [(0, 1), (1, 0)])

    def ring_gather(shard):
        half = chips // 2

        def step(carry, unused):
            carry = (send_up(carry[0]), send_down(carry[1]))
            return carry, carry

        (low, high), (lows, highs) = lax.scan(step, (shard, shard), None, length=half - 1)
        cut = shard.shape[0] // 2
        across = jnp.concatenate([send_up(low[:cut]), send_down(high[cut:])], axis=0)
        return jnp.concatenate([shard[None], highs, across[None], lows[::-1]], axis=0)

    def ring_scatter(lows, highs):
        def own(parts, slot):
            return lax.dynamic_index_in_dim(parts, slot, 0, keepdims=False).astype(F32)

        def step(carry, at):
            low, high = (send_up(carry[0]), send_down(carry[1]))
            low = low.astype(F32) + own(lows, (chips - 1 - at) % chips)
            high = high.astype(F32) + own(highs, (1 + at) % chips)
            return (low.astype(BF16), high.astype(BF16)), None

        start = (lows[chips - 1].astype(BF16), highs[1].astype(BF16))
        steps = jnp.arange(1, chips - 1, dtype=jnp.int32)
        (low, high), unused = lax.scan(step, start, steps)
        return (
            send_up(low).astype(F32) + lows[0].astype(F32),
            send_down(high).astype(F32) + highs[0].astype(F32),
        )

    def gather(shard):
        own = ring_gather(shard).reshape(chips * shard.shape[0], shard.shape[1])
        return jnp.concatenate([own, swap_core(own)], axis=0)

    def weight_scatter(grad):
        db, cut = grad.shape[0] // chips, grad.shape[1] // 2
        parts = grad.reshape(chips, db, grad.shape[1])
        return jnp.concatenate(ring_scatter(parts[:, :, :cut], parts[:, :, cut:]), axis=1)

    def local(
        hidden_in,
        block_order,
        doc_ids,
        attn_gain,
        w_query,
        w_key,
        w_value,
        w_out,
        mlp_gain,
        w_gate,
        w_up,
        w_down,
        cotangent,
    ):
        layers, db = w_query.shape[0], w_query.shape[1]
        width = db * n_ctx
        side = width // 2
        q_width, kv_width, ff_width = w_query.shape[2], w_key.shape[2], w_gate.shape[2]
        heads_q, heads_kv = q_width // HEAD_SIZE, kv_width // HEAD_SIZE
        group = heads_q // heads_kv
        own_rows = hidden_in.shape[0]
        token_rows = own_rows * 2
        ctx = lax.axis_index("ctx")
        head = lax.axis_index("head")
        core = ctx % 2
        place_of = [0] * chips
        for at, chip in enumerate(ring):
            place_of[chip] = at
        place = jnp.array(place_of, jnp.int32)[ctx // 2]

        slot_ids = jnp.arange(n_ctx, dtype=jnp.int32)
        along = (place + slot_ids % chips) % chips
        chip_of = jnp.where(along < chips // 2, 2 * along, 2 * (chips - 1 - along) + 1)
        block_of = chip_of * 2 + (core + slot_ids // chips) % 2
        block_hot = (block_of[:, None] == slot_ids[None, :]).astype(F32)
        feature = jnp.arange(width, dtype=jnp.int32)
        wanted = jnp.repeat(block_of, db) * db + feature % db
        to_ring = (feature[:, None] == wanted[None, :]).astype(BF16)

        def reorder(rows):
            return dot(rows, to_ring)

        def restore(rows):
            return dot_nt(rows, to_ring)

        def thirds(rows):
            high = lax.reduce_precision(rows, 8, 7)
            middle = lax.reduce_precision(rows - high, 8, 7)
            return [part.astype(BF16) for part in (high, middle, rows - high - middle)]

        offsets = jnp.arange(BLK, dtype=jnp.int32)

        def own_first(table):
            return jnp.where(head == 0, table, jnp.stack([table[1], table[0]], axis=0))

        order, docs = own_first(block_order), own_first(doc_ids)
        own_blocks = lax.dynamic_slice(order, (jnp.int32(0), 2 * ctx), (SEQS, 2))
        q_positions = (own_blocks[:, :, None] * BLK + offsets[None, None, :]).reshape(SEQS, ROWS)
        ring_blocks = jnp.einsum(
            "ac,scb->sab", block_hot, order.reshape(SEQS, n_ctx, 2).astype(F32)
        ).astype(jnp.int32)
        k_positions = (ring_blocks[..., None] * BLK + offsets).reshape(SEQS, 1, n_ctx * ROWS)
        doc_blocks = docs.reshape(SEQS, -1, BLK)
        own_hot = (own_blocks[:, :, None] == jnp.arange(doc_blocks.shape[1])).astype(F32)
        q_docs = jnp.einsum("sab,sbj->saj", own_hot, doc_blocks.astype(F32)).astype(jnp.int32)
        q_docs = q_docs.reshape(SEQS, ROWS)
        q_starts = jnp.sum((docs[:, None, :] < q_docs[:, :, None]).astype(jnp.int32), axis=2)
        kpos = k_positions
        qpos, qstart = q_positions[:, :, None], q_starts[:, :, None]
        cosine, sine_table = rope_tables(q_positions.reshape(token_rows))
        scale_q = HEAD_SIZE ** (-0.5)

        def both_rows(rows):
            return jnp.concatenate([rows, swap_head(rows)], axis=0)

        def to_owner(parts):
            return parts[:own_rows] + swap_head(parts[own_rows:].astype(BF16)).astype(F32)

        def project(rows, weight, lo, hi):
            return dot(rows, weight[:, lo:hi])

        def project_back(rows, weight, lo, hi):
            return dot_nt(rows, weight[:, lo:hi])

        def weight_grad(left, right):
            lefts = jnp.concatenate([left[:, :side], swap_core(left[:, side:])], axis=0)
            rights = jnp.concatenate([right, swap_core(right)], axis=0)
            return dot_tn(lefts, rights)

        def units(rows):
            shaped = rows.reshape(SEQS, ROWS, heads_kv, group, HEAD_SIZE)
            return shaped.transpose(0, 2, 3, 1, 4).reshape(SEQS, heads_kv, group * ROWS, HEAD_SIZE)

        def from_units(parts):
            shaped = parts.reshape(SEQS, heads_kv, group, ROWS, HEAD_SIZE)
            return shaped.transpose(0, 3, 1, 2, 4).reshape(token_rows, q_width)

        qkv_width = q_width + 2 * kv_width
        attn_width = qkv_width + q_width
        both = reorder(jnp.concatenate([hidden_in, cotangent], axis=0))
        grad_res = both[own_rows:]
        attn_shards = [
            jnp.concatenate(
                [w_query[layer], w_key[layer], w_value[layer], w_out[layer].T], axis=1
            )
            for layer in range(layers)
        ]
        gate_up_shards = [
            jnp.concatenate([w_gate[layer], w_up[layer]], axis=1) for layer in range(layers)
        ]

        def forward_by_ops(residual):
            gains = lax.all_gather(
                jnp.concatenate([attn_gain, mlp_gain], axis=0), "ctx", axis=1, tiled=True
            )
            gains = reorder(gains)
            fetched = [
                (
                    gather(attn_shards[layer]),
                    gather(
                        jnp.concatenate([gate_up_shards[layer], w_down[layer].T], axis=1)
                    ),
                )
                for layer in range(layers)
            ]
            records = []
            for layer in range(layers):
                attn_w, mlp_w = fetched[layer]
                gain_a, gain_m = gains[layer], gains[layers + layer]
                residual_in = residual
                normed_a = both_rows((residual * rms_inverse(residual) * gain_a).astype(BF16))
                projected = project(normed_a, attn_w, 0, qkv_width)
                q_rows = rotate(
                    projected[:, :q_width].reshape(token_rows, heads_q, HEAD_SIZE),
                    cosine,
                    sine_table,
                )
                queries = units((q_rows * scale_q).astype(BF16).reshape(token_rows, q_width))
                keys = rotate(
                    projected[:, q_width : q_width + kv_width].reshape(
                        token_rows, heads_kv, HEAD_SIZE
                    ),
                    cosine,
                    sine_table,
                ).reshape(token_rows, kv_width)
                kv_shard = jnp.concatenate([keys, projected[:, q_width + kv_width :]], axis=1)
                kv_own = ring_gather(kv_shard.astype(BF16).T)
                kv = jnp.concatenate([kv_own, swap_core(kv_own)], axis=0)
                mixed, lse = attend_forward(queries, kv, kpos, qpos, qstart)
                attended = from_units(mixed)
                middle = residual + to_owner(
                    project_back(attended, attn_w, qkv_width, attn_width)
                )
                normed_m = both_rows((middle * rms_inverse(middle) * gain_m).astype(BF16))
                gate_up = project(normed_m, mlp_w, 0, 2 * ff_width)
                gate_part, up_part = gate_up[:, :ff_width], gate_up[:, ff_width:]
                activated = (jax.nn.silu(gate_part) * up_part).astype(BF16)
                residual = middle + to_owner(
                    project_back(activated, mlp_w, 2 * ff_width, 3 * ff_width)
                )
                records.append(
                    (
                        residual_in,
                        normed_a,
                        queries,
                        kv,
                        lse,
                        attended,
                        middle,
                        normed_m,
                        gate_part,
                        up_part,
                        activated,
                    )
                )
            return fetched, gains, records, residual

        def forward_by_kernel(residual):
            columns = jnp.concatenate([attn_gain, mlp_gain], axis=0).T
            columns = jnp.pad(columns, ((0, 0), (0, 128 - columns.shape[1])))
            shards = []
            for layer in range(layers):
                attn = attn_shards[layer]
                if layer == 0:
                    attn = jnp.concatenate([attn, columns], axis=1)
                shards += [attn, gate_up_shards[layer], w_down[layer].T]
            weights, saved = forward(
                residual,
                grad_res.astype(BF16),
                shards,
                cosine.T,
                sine_table.T,
                kpos,
                qpos,
                qstart,
                chips,
                q_width,
                kv_width,
                ff_width,
            )
            residual_ins = jnp.concatenate([residual[None], saved[10]], axis=0)
            tables = (cosine.T, sine_table.T, kpos, qpos, qstart)
            records = [*saved[:10], residual_ins, saved[11]]
            return weights, tables, records, saved[12]

        in_kernel = n_ctx * ROWS <= 2048 and db == HEAD_SIZE
        run_forward = forward_by_kernel if in_kernel else forward_by_ops
        fetched, gains, records, last = run_forward(both[:own_rows])
        def norm_back(grad_res, normed_gradient, value_rows, inverse_norm, gain):
            normalized = value_rows * inverse_norm
            gain_gradient = jnp.sum(normed_gradient * normalized, axis=0)
            scaled = normed_gradient * gain
            mean = jnp.mean(scaled * normalized, axis=-1, keepdims=True)
            return grad_res + inverse_norm * (scaled - normalized * mean), gain_gradient

        def backward_by_ops(grad_res):
            d_attn = [None] * layers
            d_mlp = [None] * layers
            d_gains = [None] * (2 * layers)
            for layer in reversed(range(layers)):
                attn_w, mlp_w = fetched[layer]
                gain_a, gain_m = gains[layer], gains[layers + layer]
                (
                    residual_in,
                    normed_a,
                    queries,
                    kv,
                    lse,
                    attended,
                    middle,
                    normed_m,
                    gate_part,
                    up_part,
                    activated,
                ) = records[layer]
                inverse_a, inverse_m = rms_inverse(residual_in), rms_inverse(middle)
                grad_rows_m = both_rows(grad_res.astype(BF16))
                grad_act = project(grad_rows_m, mlp_w, 2 * ff_width, 3 * ff_width)
                sigmoid_g = jax.nn.sigmoid(gate_part)
                grad_gate = grad_act * up_part * sigmoid_g * (1.0 + gate_part * (1.0 - sigmoid_g))
                grad_up = grad_act * gate_part * sigmoid_g
                grad_gu = jnp.concatenate([grad_gate, grad_up], axis=1).astype(BF16)
                grad_norm_m = to_owner(project_back(grad_gu, mlp_w, 0, 2 * ff_width))
                d_down = weight_scatter(weight_grad(grad_rows_m, activated))
                d_gu = weight_scatter(weight_grad(normed_m, grad_gu))
                grad_res, d_gains[layers + layer] = norm_back(
                    grad_res, grad_norm_m, middle, inverse_m, gain_m
                )
                grad_rows_a = both_rows(grad_res.astype(BF16))
                grad_attended = project(grad_rows_a, attn_w, qkv_width, attn_width).astype(BF16)
                d_out = weight_grad(grad_rows_a, attended)
                grad_q, dk, dv = attend_backward(
                    queries, units(grad_attended), lse, kv, kpos, qpos, qstart
                )
                dk_back, dv_back = swap_core(dk[chips:]), swap_core(dv[chips:])
                grad_k, grad_v = ring_scatter(
                    dk[:chips].astype(F32) + dk_back.astype(F32),
                    dv[:chips].astype(F32) + dv_back.astype(F32),
                )
                grad_q_pre = rotate_back(
                    from_units(grad_q).reshape(token_rows, heads_q, HEAD_SIZE), cosine, sine_table
                )
                grad_k_pre = rotate_back(
                    grad_k.T.reshape(token_rows, heads_kv, HEAD_SIZE), cosine, sine_table
                )
                grad_qkv = jnp.concatenate(
                    [
                        (grad_q_pre * scale_q).reshape(token_rows, q_width),
                        grad_k_pre.reshape(token_rows, kv_width),
                        grad_v.T,
                    ],
                    axis=1,
                ).astype(BF16)
                grad_norm_a = to_owner(project_back(grad_qkv, attn_w, 0, qkv_width))
                d_qkv = weight_grad(normed_a, grad_qkv)
                d_attn[layer] = weight_scatter(jnp.concatenate([d_qkv, d_out], axis=1))
                d_mlp[layer] = (d_gu, d_down)
                grad_res, d_gains[layer] = norm_back(
                    grad_res, grad_norm_a, residual_in, inverse_a, gain_a
                )
            attn_grads, mlp_grads = jnp.stack(d_attn, axis=0), [jnp.stack(part) for part in zip(*d_mlp)]
            k_at, v_at = q_width, q_width + kv_width
            return (
                grad_res,
                jnp.stack(d_gains, axis=0),
                last.astype(BF16),
                attn_grads[:, :, :k_at],
                attn_grads[:, :, k_at:v_at],
                attn_grads[:, :, v_at:qkv_width],
                attn_grads[:, :, qkv_width:].transpose(0, 2, 1),
                mlp_grads[0][:, :, :ff_width],
                mlp_grads[0][:, :, ff_width:],
                mlp_grads[1].transpose(0, 2, 1),
            )

        if in_kernel:
            grads = backward(
                grad_res, last, fetched, records, gains, chips, q_width, kv_width, ff_width
            )
        else:
            grads = backward_by_ops(grad_res)
        grad_res, d_gains, x_out, *weight_grads = grads
        count = 2 * layers
        rows_low = jnp.concatenate(thirds(d_gains), axis=0)
        d_gains = restore(rows_low).reshape(3, count, width).sum(axis=0)
        d_gains = d_gains + swap_head(d_gains)
        bit = 1
        while bit < n_ctx:
            d_gains = d_gains + lax.ppermute(d_gains, "ctx", [(i, i ^ bit) for i in range(n_ctx)])
            bit *= 2
        d_gains = lax.dynamic_slice(d_gains, (0, ctx * db), (2 * layers, db))
        restored = restore(jnp.concatenate([x_out, *thirds(grad_res)], axis=0))
        out_hidden = restored[:own_rows].astype(BF16)
        d_hidden = restored[own_rows:].reshape(3, own_rows, width).sum(axis=0)
        return (
            out_hidden,
            d_hidden,
            d_gains[:layers],
            *weight_grads[:4],
            d_gains[layers:],
            *weight_grads[4:],
        )

    return local


def solution(mesh):
    return jax.shard_map(
        build(mesh.shape["ctx"]),
        mesh=mesh,
        in_specs=(
            P(("ctx", "head"), None),
            P(),
            P(),
            P(None, "ctx"),
            P(None, "ctx", "head"),
            P(None, "ctx", "head"),
            P(None, "ctx", "head"),
            P(None, "head", "ctx"),
            P(None, "ctx"),
            P(None, "ctx", "head"),
            P(None, "ctx", "head"),
            P(None, "head", "ctx"),
            P(("ctx", "head"), None),
        ),
        out_specs=(
            P(("ctx", "head"), None),
            P(("ctx", "head"), None),
            P(None, "ctx"),
            P(None, "ctx", "head"),
            P(None, "ctx", "head"),
            P(None, "ctx", "head"),
            P(None, "head", "ctx"),
            P(None, "ctx"),
            P(None, "ctx", "head"),
            P(None, "ctx", "head"),
            P(None, "head", "ctx"),
        ),
        check_vma=False,
    )
```

```python
import functools
import math

import jax
import jax.numpy as jnp
from jax import lax
from jax.experimental import pallas as pl
from jax.experimental.pallas import tpu as pltpu
from jax.sharding import PartitionSpec as P

HEAD_SIZE = 96
HALF = HEAD_SIZE // 2
SEQS = 2
BLK = 64
ROWS = 2 * BLK

NEG = -1e30
EPS = 1e-05
THETA = 100000.0
VMEM_LIMIT = 56 * 1024 * 1024
KERNEL_VMEM = 62 * 1024 * 1024
MESH = pl.DeviceIdType.MESH
BF16 = jnp.bfloat16
F32 = jnp.float32


def ring_of(chips):
    return list(range(0, chips, 2)) + list(range(chips - 1, 0, -2))


def rope_tables(positions):
    freq_row = jnp.exp(jnp.arange(HALF, dtype=F32) * (-2.0 * math.log(THETA) / HEAD_SIZE))
    angles = positions.astype(F32)[:, None] * freq_row[None, :]
    return (jnp.cos(angles), jnp.sin(angles))


def rotate(tensor, cosine, sine_table):
    first, second = tensor[..., :HALF], tensor[..., HALF:]
    cos_wide, sin_wide = cosine[:, None, :], sine_table[:, None, :]
    return jnp.concatenate(
        [first * cos_wide - second * sin_wide, second * cos_wide + first * sin_wide], axis=-1
    )


def rotate_back(tensor, cosine, sine_table):
    first, second = tensor[..., :HALF], tensor[..., HALF:]
    cos_wide, sin_wide = cosine[:, None, :], sine_table[:, None, :]
    return jnp.concatenate(
        [first * cos_wide + second * sin_wide, second * cos_wide - first * sin_wide], axis=-1
    )


def dot(left, right):
    return jnp.dot(left, right, preferred_element_type=F32)


def dot_nt(left, right):
    return lax.dot_general(left, right, (((1,), (1,)), ((), ())), preferred_element_type=F32)


def dot_tn(left, right):
    return lax.dot_general(left, right, (((0,), (0,)), ((), ())), preferred_element_type=F32)


def row_tile(keys):
    return 256 if keys <= 2048 else 64


def gathered(ref):
    return jnp.concatenate([ref[j] for j in range(ref.shape[0])], axis=1)


def mask_rows(kpos_ref, qpos_ref, qstart_ref, start, rows):
    kpos = kpos_ref[0]
    parts = []
    done = 0
    while done < rows:
        at = (start + done) % ROWS
        size = min(rows - done, ROWS - at)
        qpos = qpos_ref[0, at : at + size, :]
        qstart = qstart_ref[0, at : at + size, :]
        parts.append((kpos <= qpos) & (kpos >= qstart))
        done += size
    return parts


def masked(scores, parts):
    out = []
    at = 0
    for part in parts:
        size = part.shape[0]
        out.append(jnp.where(part, scores[at : at + size, :], NEG))
        at += size
    return jnp.concatenate(out, axis=0) if len(out) > 1 else out[0]


def attend_kernel(q_ref, k_ref, v_ref, kpos_ref, qpos_ref, qstart_ref, o_ref, lse_ref):
    total = q_ref.shape[2]
    kt = gathered(k_ref)
    vt = gathered(v_ref)
    tile = min(total, row_tile(kt.shape[1]))
    for at in range(0, total, tile):
        q = q_ref[0, 0, at : at + tile, :]
        scores = masked(dot(q, kt), mask_rows(kpos_ref, qpos_ref, qstart_ref, at, tile))
        top = jnp.max(scores, axis=1, keepdims=True)
        weights = jnp.exp(scores - top)
        norm = jnp.sum(weights, axis=1, keepdims=True)
        probs = (weights * (1.0 / norm)).astype(BF16)
        o_ref[0, 0, at : at + tile, :] = dot_nt(probs, vt).astype(BF16)
        lse_ref[0, 0, at : at + tile, :] = top + jnp.log(norm)


def attend_back_kernel(
    q_ref,
    do_ref,
    lse_ref,
    k_ref,
    v_ref,
    kpos_ref,
    qpos_ref,
    qstart_ref,
    dq_ref,
    dk_ref,
    dv_ref,
):
    total = q_ref.shape[2]
    kt = gathered(k_ref)
    vt = gathered(v_ref)
    tile = min(total, row_tile(kt.shape[1]))
    dkt = None
    dvt = None
    for at in range(0, total, tile):
        q = q_ref[0, 0, at : at + tile, :]
        grad = do_ref[0, 0, at : at + tile, :]
        scores = masked(dot(q, kt), mask_rows(kpos_ref, qpos_ref, qstart_ref, at, tile))
        probs = jnp.exp(scores - lse_ref[0, 0, at : at + tile, :])
        dprobs = dot(grad, vt)
        delta = jnp.sum(probs * dprobs, axis=1, keepdims=True)
        dscores = (probs * (dprobs - delta)).astype(BF16)
        dq_ref[0, 0, at : at + tile, :] = dot_nt(dscores, kt)
        dk_part = dot_tn(q, dscores)
        dv_part = dot_tn(grad, probs.astype(BF16))
        dkt = dk_part if dkt is None else dkt + dk_part
        dvt = dv_part if dvt is None else dvt + dv_part
    for j in range(dk_ref.shape[0]):
        dk_ref[j] = dkt[:, j * ROWS : (j + 1) * ROWS].astype(BF16)
        dv_ref[j] = dvt[:, j * ROWS : (j + 1) * ROWS].astype(BF16)


def attention_specs(q, kv, kpos):
    slots = kv.shape[0]
    kv_heads = kv.shape[1] // (2 * HEAD_SIZE)
    keys = kpos.shape[2]
    rows = q.shape[2]
    unit = pl.BlockSpec((1, 1, rows, HEAD_SIZE), lambda s, h: (s, h, 0, 0))
    column = pl.BlockSpec((1, 1, rows, 1), lambda s, h: (s, h, 0, 0))
    k_spec = pl.BlockSpec((slots, HEAD_SIZE, ROWS), lambda s, h: (0, h, s))
    v_spec = pl.BlockSpec((slots, HEAD_SIZE, ROWS), lambda s, h: (0, kv_heads + h, s))
    kpos_spec = pl.BlockSpec((1, 1, keys), lambda s, h: (s, 0, 0))
    q_spec = pl.BlockSpec((1, ROWS, 1), lambda s, h: (s, 0, 0))
    return kv_heads, unit, column, k_spec, v_spec, kpos_spec, q_spec


def attend_forward(q, kv, kpos, qpos, qstart):
    kv_heads, unit, column, k_spec, v_spec, kpos_spec, q_spec = attention_specs(q, kv, kpos)
    rows, keys = q.shape[2], kpos.shape[2]
    work = SEQS * kv_heads * rows * keys
    return pl.pallas_call(
        attend_kernel,
        grid=(SEQS, kv_heads),
        in_specs=[unit, k_spec, v_spec, kpos_spec, q_spec, q_spec],
        out_specs=[unit, column],
        out_shape=[
            jax.ShapeDtypeStruct(q.shape, BF16),
            jax.ShapeDtypeStruct(q.shape[:3] + (1,), F32),
        ],
        compiler_params=pltpu.CompilerParams(vmem_limit_bytes=VMEM_LIMIT),
        cost_estimate=pl.CostEstimate(
            flops=8 * HEAD_SIZE * work, bytes_accessed=8 * 2**20, transcendentals=work
        ),
    )(q, kv, kv, kpos, qpos, qstart)


def attend_backward(q, grad, lse, kv, kpos, qpos, qstart):
    kv_heads, unit, column, k_spec, v_spec, kpos_spec, q_spec = attention_specs(q, kv, kpos)
    rows, keys = q.shape[2], kpos.shape[2]
    work = SEQS * kv_heads * rows * keys
    slots = kv.shape[0]
    grad_spec = pl.BlockSpec((slots, HEAD_SIZE, ROWS), lambda s, h: (0, h, s))
    grad_shape = jax.ShapeDtypeStruct((slots, kv_heads * HEAD_SIZE, SEQS * ROWS), BF16)
    return pl.pallas_call(
        attend_back_kernel,
        grid=(SEQS, kv_heads),
        in_specs=[unit, unit, column, k_spec, v_spec, kpos_spec, q_spec, q_spec],
        out_specs=[unit, grad_spec, grad_spec],
        out_shape=[jax.ShapeDtypeStruct(q.shape, F32)] + [grad_shape] * 2,
        compiler_params=pltpu.CompilerParams(vmem_limit_bytes=VMEM_LIMIT),
        cost_estimate=pl.CostEstimate(
            flops=20 * HEAD_SIZE * work, bytes_accessed=16 * 2**20, transcendentals=work
        ),
    )(q, grad, lse, kv, kv, kpos, qpos, qstart)


def ring_neighbours(chips):
    ctx = lax.axis_index("ctx")
    chip, core, half = ctx // 2, ctx % 2, chips // 2
    odd = chip % 2
    place = odd * (chips - 1 - chip // 2) + (1 - odd) * (chip // 2)

    def device(at):
        far = at // half
        return ((1 - far) * 2 * at + far * (2 * (chips - 1 - at) + 1)) * 2 + core

    return device((place + 1) % chips), device((place + chips - 1) % chips), ctx + 1 - 2 * core


class Links:
    def __init__(self, chips, send_sems, recv_sems):
        self.chips = chips
        self.right, self.left, self.sib = ring_neighbours(chips)
        self.head = lax.axis_index("head")
        self.ctx = lax.axis_index("ctx")
        self.send_sems, self.recv_sems = send_sems, recv_sems
        self.used = 0
        self.started = []

    def greet(self):
        barrier = pltpu.get_barrier_semaphore()
        for target in (self.right, self.left, self.sib):
            pl.semaphore_signal(barrier, inc=1, device_id=(target, self.head), device_id_type=MESH)
        pl.semaphore_signal(
            barrier, inc=1, device_id=(self.ctx, 1 - self.head), device_id_type=MESH
        )
        pl.semaphore_wait(barrier, 4)

    def copy(self, src, dst, target):
        copy = pltpu.make_async_remote_copy(
            src_ref=src,
            dst_ref=dst,
            send_sem=self.send_sems.at[self.used],
            recv_sem=self.recv_sems.at[self.used],
            device_id=target,
            device_id_type=MESH,
        )
        self.used += 1
        copy.start()
        self.started.append(copy)
        return copy

    def to_right(self, src, dst):
        return self.copy(src, dst, (self.right, self.head))

    def to_left(self, src, dst):
        return self.copy(src, dst, (self.left, self.head))

    def to_sibling(self, src, dst):
        return self.copy(src, dst, (self.sib, self.head))

    def to_head(self, src, dst):
        return self.copy(src, dst, (self.ctx, 1 - self.head))

    def sent(self, copy):
        if any(other is copy for other in self.started):
            copy.wait_send()
            self.started = [other for other in self.started if other is not copy]

    def finish(self):
        for copy in self.started:
            copy.wait_send()
        self.started = []


class RingGather:
    def __init__(self, links, ref, chains, first=None):
        self.links, self.ref, self.chains = links, ref, chains
        self.first = first
        self.moving = {}
        self.arriving = []
        self.steps = links.chips // 2
        self.events = [(c, s) for s in range(1, self.steps + 1) for c in range(len(chains))]

    @staticmethod
    def copies(chips, chains):
        return chains * (chips + chips)

    def window(self, slot, chain, part=None):
        r0, rn, c0, cn = self.chains[chain]
        if part is not None:
            rn = rn // 2
            r0 = r0 + part * rn
        if slot == 0 and self.first is not None:
            return self.first.at[pl.ds(r0, rn), pl.ds(c0, cn)]
        return self.ref.at[slot, pl.ds(r0, rn), pl.ds(c0, cn)]

    def share(self, slot, chain):
        r0, rn, c0, cn = self.chains[chain]
        there = self.ref.at[self.links.chips + slot, pl.ds(r0, rn), pl.ds(c0, cn)]
        self.arriving.append(self.links.to_sibling(self.window(slot, chain), there))

    def issue(self, event):
        chain, step = event
        chips = self.links.chips
        last = step == self.steps
        up_from, up_to = (chips - step + 1) % chips, chips - step
        r0, rn, c0, cn = self.chains[chain]

        def there(slot, part):
            rows = (r0, rn) if part is None else (r0 + part * (rn // 2), rn // 2)
            return self.ref.at[slot, pl.ds(*rows), pl.ds(c0, cn)]

        up = 0 if last else None
        down = 1 if last else None
        self.moving[event] = (
            self.links.to_right(self.window(up_from, chain, up), there(up_to, up)),
            self.links.to_left(self.window(step - 1, chain, down), there(step, down)),
        )
        if step == 1:
            self.share(0, chain)

    def land(self, event):
        chain, step = event
        for copy in self.moving[event]:
            copy.wait_recv()
        self.share(self.links.chips - step, chain)
        if step != self.steps:
            self.share(step, chain)

    def settle(self):
        for copy in self.arriving:
            copy.wait_recv()


class Queue:
    def __init__(self, rings, depth=4):
        self.waiting = [(ring, event) for ring in rings for event in ring.events]
        self.depth = depth
        self.flying = []
        self.landed = set()
        self.fill()

    def fill(self):
        for item in list(self.waiting):
            if len(self.flying) == self.depth:
                break
            ring, (chain, step) = item
            if step == 1 or (id(ring), chain, step - 1) in self.landed:
                ring.issue((chain, step))
                self.waiting.remove(item)
                self.flying.append(item)

    def pump(self, count=1):
        for _ in range(count):
            if self.flying:
                ring, event = self.flying.pop(0)
                ring.land(event)
                self.landed.add((id(ring), *event))
                self.fill()

    def through(self, ring):
        while any(item[0] is ring for item in self.flying + self.waiting):
            self.pump()


TILE = 512


def rms_inverse(rows):
    return lax.rsqrt(jnp.mean(rows * rows, axis=-1, keepdims=True) + EPS)


def windows_of(wide, count):
    blocks = wide // 128
    edges = [blocks * i // count * 128 for i in range(count + 1)]
    return [(low, high - low) for low, high in zip(edges, edges[1:])]


CHAINS = (4, 4, 2)


def forward_kernel(dims, *refs):
    layers, chips, width, q_width, kv_width, ff = dims
    slots = 2 * chips
    parts = len(CHAINS)
    it = iter(refs)
    x_ref, g_ref = next(it), next(it)
    shards = [next(it) for _ in range(parts * layers)]
    cos_ref, sin_ref, kpos_ref, qpos_ref, qstart_ref = (next(it) for _ in range(5))
    weights = [next(it) for _ in range(parts * layers)]
    saved = [next(it) for _ in range(10)]
    x_out_ref, gain_ref, g_rows_ref = next(it), next(it), next(it)
    kept = [next(it) for _ in range(10)]
    (
        kv_ref, normed_a_ref, qt_ref, lse_ref, att_ref, middle_ref, normed_m_ref, gate_ref, up_ref, act_ref
    ) = kept
    (
        wt, wo, acc, proj_t, att_t, b_send, b_recv, gain_block,
        g_rows, send_sems, recv_sems, load_sems, own_sems, save_sems,
    ) = (next(it) for _ in range(14))

    rows = x_ref.shape[0]
    db = width // slots
    heads_kv = kv_width // HEAD_SIZE
    group = q_width // kv_width
    qkv_width = q_width + 2 * kv_width
    links = Links(chips, send_sems, recv_sems)
    own_copies = []
    for i, (shard, weight) in enumerate(zip(shards, weights)):
        own_copies.append(pltpu.make_async_copy(shard, weight.at[0], own_sems.at[i]))
        own_copies[-1].start()
    links.greet()

    rings = []
    for i, (shard, weight) in enumerate(zip(shards, weights)):
        chains = [(0, db, c0, cn) for c0, cn in windows_of(shard.shape[1], CHAINS[i % parts])]
        rings.append(RingGather(links, weight, chains, first=shard))
    queue = Queue(rings)

    def ready(i):
        queue.through(rings[i])
        rings[i].settle()
        own_copies[i].wait()

    def load(i, column, wide, target, sem):
        copy = pltpu.make_async_copy(
            weights[i].at[:, :, pl.ds(column, wide)], target, load_sems.at[sem]
        )
        copy.start()
        return copy

    def flat(ref):
        return ref[...].reshape(width, ref.shape[-1])

    saving = []

    def save(i, layer):
        copy = pltpu.make_async_copy(
            kept[i].at[layer], saved[i].at[layer], save_sems.at[layer * len(kept) + i]
        )
        copy.start()
        saving.append(copy)

    g_rows[0:rows, :] = g_ref[...]
    g_swap = links.to_head(g_rows.at[pl.ds(0, rows), :], g_rows.at[pl.ds(rows, rows), :])

    ready(0)
    side = qkv_width + q_width
    load(0, side, 128, gain_block, 0).wait()
    gain_ref[...] = flat(gain_block).astype(F32).T[: gain_ref.shape[0], :]

    for layer in range(layers):
        attn, gate_up, down_w = parts * layer, parts * layer + 1, parts * layer + 2
        if layer:
            ready(attn)
        tiles = qkv_width // TILE
        order = list(reversed(range(tiles)))
        tile_loads = {t: load(attn, t * TILE, TILE, wt.at[t], t) for t in order}
        out_load = load(attn, qkv_width, q_width, wo, 6)

        x = x_ref[...] if layer == 0 else x_out_ref[layer - 1]
        gain_a = gain_ref[layer : layer + 1, :]
        normed_a_ref[layer, 0:rows, :] = (x * rms_inverse(x) * gain_a).astype(BF16)
        swap = links.to_head(
            normed_a_ref.at[layer, pl.ds(0, rows), :], normed_a_ref.at[layer, pl.ds(rows, rows), :]
        )

        def project(t, at):
            part = dot(normed_a_ref[layer, at : at + rows, :], flat(wt.at[t]))
            proj_t[t * TILE : (t + 1) * TILE, at : at + rows] = part.T

        for t in order:
            tile_loads[t].wait()
            project(t, 0)
        swap.wait_recv()
        first_kv = q_width // TILE
        for t in order:
            if t >= first_kv:
                project(t, rows)

        cosine, sine = cos_ref[...], sin_ref[...]

        def turned(at):
            low = proj_t[at : at + HALF, :]
            high = proj_t[at + HALF : at + HEAD_SIZE, :]
            return low * cosine - high * sine, high * cosine + low * sine

        for h in range(heads_kv):
            low, high = turned(q_width + h * HEAD_SIZE)
            kv_ref[layer, 0, h * HEAD_SIZE : h * HEAD_SIZE + HALF, :] = low.astype(BF16)
            kv_ref[layer, 0, h * HEAD_SIZE + HALF : (h + 1) * HEAD_SIZE, :] = high.astype(BF16)
        kv_ref[layer, 0, kv_width : 2 * kv_width, :] = proj_t[
            q_width + kv_width : qkv_width, :
        ].astype(BF16)
        wide = kv_ref.shape[-1]
        half = kv_width // 2
        kv_rings = [
            RingGather(
                links,
                kv_ref.at[layer],
                [(i * half, half, 0, wide), (kv_width + i * half, half, 0, wide)],
            )
            for i in range(2)
        ]
        kv_queue = Queue(kv_rings)
        for t in order:
            if t < first_kv:
                project(t, rows)
        scale = HEAD_SIZE ** (-0.5)
        for h in range(q_width // HEAD_SIZE):
            low, high = turned(h * HEAD_SIZE)
            qt_ref[layer, h * HEAD_SIZE : h * HEAD_SIZE + HALF, :] = (low * scale).astype(BF16)
            qt_ref[layer, h * HEAD_SIZE + HALF : (h + 1) * HEAD_SIZE, :] = (high * scale).astype(
                BF16
            )
        save(1, layer)
        save(2, layer)

        def unit(u, carry):
            h, s = u // SEQS, u % SEQS
            k_rows = pl.ds(pl.multiple_of(h * HEAD_SIZE, HEAD_SIZE), HEAD_SIZE)
            v_rows = pl.ds(pl.multiple_of(kv_width + h * HEAD_SIZE, HEAD_SIZE), HEAD_SIZE)
            lanes = pl.ds(pl.multiple_of(s * ROWS, ROWS), ROWS)
            kt = jnp.concatenate([kv_ref[layer, j, k_rows, lanes] for j in range(slots)], axis=1)
            vt = jnp.concatenate([kv_ref[layer, j, v_rows, lanes] for j in range(slots)], axis=1)
            q_rows = [
                pl.ds(pl.multiple_of((h * group + g) * HEAD_SIZE, HEAD_SIZE), HEAD_SIZE)
                for g in range(group)
            ]
            qt = jnp.concatenate([qt_ref[layer, at, lanes] for at in q_rows], axis=1)
            kpos, qpos, qstart = kpos_ref[s], qpos_ref[s], qstart_ref[s]
            allowed = (kpos <= qpos) & (kpos >= qstart)
            scores = masked(dot_tn(qt, kt), [allowed] * group)
            top = jnp.max(scores, axis=1, keepdims=True)
            raised = jnp.exp(scores - top)
            norm = jnp.sum(raised, axis=1, keepdims=True)
            probs = (raised * (1.0 / norm)).astype(BF16)
            mixed = dot_nt(vt, probs)
            for g, at in enumerate(q_rows):
                att_t[at, lanes] = mixed[:, g * ROWS : (g + 1) * ROWS]
            lse_ref[layer, u] = top + jnp.log(norm)
            return carry

        units = SEQS * heads_kv
        for i, ring in enumerate(kv_rings):
            kv_queue.through(ring)
            ring.settle()
            queue.pump(2)
            low, high = units * i // 2, units * (i + 1) // 2
            if i == 0:
                for u in range(low, high):
                    lax.fori_loop(u, u + 1, unit, 0)
                    kv_queue.pump(2)
            else:
                save(0, layer)
                middle_unit = (low + high) // 2
                lax.fori_loop(low, middle_unit, unit, 0)
                queue.pump(2)
                lax.fori_loop(middle_unit, high, unit, 0)
        queue.pump(2)
        att_ref[layer] = att_t[...].T.astype(BF16)
        save(3, layer)
        save(4, layer)

        out_load.wait()
        branch = (layer * 2) % b_send.shape[0]
        other = dot_nt(att_ref[layer, rows : 2 * rows, :], flat(wo))
        b_send[branch] = other.astype(BF16)
        swap = links.to_head(b_send.at[branch], b_recv.at[branch])
        mine = dot_nt(att_ref[layer, 0:rows, :], flat(wo))
        queue.pump(2)
        swap.wait_recv()
        middle = x + mine + b_recv[branch].astype(F32)
        middle_ref[layer] = middle
        save(5, layer)
        gain_m = gain_ref[layers + layer : layers + layer + 1, :]
        normed_m_ref[layer, 0:rows, :] = (middle * rms_inverse(middle) * gain_m).astype(BF16)
        swap = links.to_head(
            normed_m_ref.at[layer, pl.ds(0, rows), :], normed_m_ref.at[layer, pl.ds(rows, rows), :]
        )
        ready(gate_up)

        def load_tile(t):
            at = (t % 2) * 2
            return [
                load(gate_up, part * ff + t * TILE, TILE, wt.at[at + part], at + part)
                for part in range(2)
            ]

        pending = load_tile(0)
        swap.wait_recv()
        save(6, layer)
        normed = normed_m_ref[layer]
        count = ff // TILE
        for t in range(count):
            following = load_tile(t + 1) if t + 1 < count else None
            for copy in pending:
                copy.wait()
            at = (t % 2) * 2
            columns = slice(t * TILE, (t + 1) * TILE)
            gate = dot(normed, flat(wt.at[at]))
            up = dot(normed, flat(wt.at[at + 1]))
            gate_ref[layer, :, columns] = gate.astype(BF16)
            up_ref[layer, :, columns] = up.astype(BF16)
            act_ref[layer, :, columns] = (gate * jax.nn.sigmoid(gate) * up).astype(BF16)
            pending = following
            queue.pump()
        for i in (7, 8, 9):
            save(i, layer)
        ready(down_w)
        if layer == layers - 1:
            break

        def load_down(t):
            return load(down_w, t * TILE, TILE, wt.at[4 + t % 2], 4 + t % 2)

        pending = load_down(0)
        for t in range(count):
            following = load_down(t + 1) if t + 1 < count else None
            pending.wait()
            down = dot_nt(act_ref[layer, :, t * TILE : (t + 1) * TILE], flat(wt.at[4 + t % 2]))
            if t == 0:
                acc[...] = down
            else:
                acc[...] += down
            pending = following
        branch = (layer * 2 + 1) % b_send.shape[0]
        b_send[branch] = acc[rows : 2 * rows, :].astype(BF16)
        swap = links.to_head(b_send.at[branch], b_recv.at[branch])
        queue.pump(2)
        swap.wait_recv()
        x_out_ref[layer] = middle_ref[layer] + acc[0:rows, :] + b_recv[branch].astype(F32)
    g_swap.wait_recv()
    g_copy = pltpu.make_async_copy(g_rows, g_rows_ref, load_sems.at[0])
    g_copy.start()
    g_copy.wait()
    for copy in saving:
        copy.wait()
    links.finish()


def forward(x, grad, shards, cosine, sine, kpos, qpos, qstart, chips, q_width, kv_width, ff):
    parts = len(CHAINS)
    layers = len(shards) // parts
    rows, width = x.shape
    db = shards[0].shape[0]
    slots = 2 * chips
    group = q_width // kv_width
    tokens = 2 * rows
    units = SEQS * kv_width // HEAD_SIZE
    dims = (layers, chips, width, q_width, kv_width, ff)
    copies = layers * (RingGather.copies(chips, sum(CHAINS) + 4) + 4)
    any_spec = pl.BlockSpec(memory_space=pltpu.HBM)
    vmem = pl.BlockSpec(memory_space=pltpu.VMEM)
    saved = [
        ((layers, slots, 2 * kv_width, tokens), BF16),
        ((layers, tokens, width), BF16),
        ((layers, q_width, tokens), BF16),
        ((layers, units, group * ROWS, 1), F32),
        ((layers, tokens, q_width), BF16),
        ((layers, rows, width), F32),
        ((layers, tokens, width), BF16),
        ((layers, tokens, ff), BF16),
        ((layers, tokens, ff), BF16),
        ((layers, tokens, ff), BF16),
    ]
    out = pl.pallas_call(
        functools.partial(forward_kernel, dims),
        out_shape=[jax.ShapeDtypeStruct((slots,) + shard.shape, BF16) for shard in shards]
        + [jax.ShapeDtypeStruct(*entry) for entry in saved]
        + [
            jax.ShapeDtypeStruct((layers - 1, rows, width), F32),
            jax.ShapeDtypeStruct((2 * layers, width), F32),
            jax.ShapeDtypeStruct((tokens, width), BF16),
        ],
        in_specs=[vmem] * 2 + [any_spec] * len(shards) + [vmem] * 5,
        out_specs=[any_spec] * (len(shards) + len(saved)) + [vmem] * 2 + [any_spec],
        scratch_shapes=[pltpu.VMEM(*entry) for entry in saved]
        + [
            pltpu.VMEM((6, slots, db, TILE), BF16),
            pltpu.VMEM((slots, db, q_width), BF16),
            pltpu.VMEM((tokens, width), F32),
            pltpu.VMEM((q_width + 2 * kv_width, tokens), F32),
            pltpu.VMEM((q_width, tokens), F32),
            pltpu.VMEM((2 * layers, rows, width), BF16),
            pltpu.VMEM((2 * layers, rows, width), BF16),
            pltpu.VMEM((slots, db, 128), BF16),
            pltpu.VMEM((tokens, width), BF16),
            pltpu.SemaphoreType.DMA((copies,)),
            pltpu.SemaphoreType.DMA((copies,)),
            pltpu.SemaphoreType.DMA((7,)),
            pltpu.SemaphoreType.DMA((len(shards),)),
            pltpu.SemaphoreType.DMA((layers * len(saved),)),
        ],
        compiler_params=pltpu.CompilerParams(
            collective_id=0, has_side_effects=True, vmem_limit_bytes=KERNEL_VMEM
        ),
    )(x, grad, *shards, cosine, sine, kpos, qpos, qstart)
    return out[: len(shards)], out[len(shards) :]


class RingScatter:
    def __init__(self, links, windows, landings, finish, stage=None, sems=None):
        self.links, self.windows, self.landings = links, windows, landings
        self.stage, self.sems, self.finish = stage, sems, finish
        self.last = links.chips - 1
        self.step = 0
        self.moving = []

    def issue(self):
        self.step += 1
        chips = self.links.chips
        slots = ((chips - self.step) % chips, self.step % chips)
        sends = (self.links.to_right, self.links.to_left)
        self.moving = [
            sends[d](self.windows[d](slots[d]), self.landings[d](self.step - 1)) for d in range(2)
        ]

    def arrive(self, place=0):
        self.here, self.loads = [], []
        for d in range(2):
            self.moving[d].wait_recv()
            self.links.sent(self.moving[d])
            here = self.landings[d](self.step - 1)
            if self.stage is not None:
                there = self.stage.at[place, d, :, pl.ds(0, here.shape[-1])]
                load = pltpu.make_async_copy(here, there, self.sems.at[2 * place + d])
                load.start()
                self.loads.append(load)
                here = there
            self.here.append(here)

    def absorb(self):
        chips = self.links.chips
        for load in self.loads:
            load.wait()
        slots = ((chips - 1 - self.step) % chips, (1 + self.step) % chips)
        for d in range(2):
            window = self.windows[d](slots[d])
            total = window[...].astype(F32) + self.here[d][...].astype(F32)
            if self.step < self.last:
                window[...] = total.astype(window.dtype)
            else:
                self.finish(d, total)
        if self.step < self.last:
            self.issue()
            return False
        return True


class Rounds:
    def __init__(self, at_once=False):
        self.active, self.loading, self.place, self.at_once = [], None, 0, at_once

    def start(self, ring):
        ring.issue()
        self.active.append(ring)
        return ring

    def absorb(self):
        if self.loading is not None:
            ring, self.loading = self.loading, None
            if not ring.absorb():
                self.active.append(ring)

    def pump(self, count=1):
        self.absorb()
        for _ in range(count):
            if not self.active:
                break
            ring = self.active.pop(0)
            self.place = 1 - self.place
            ring.arrive(self.place)
            self.absorb()
            self.loading = ring
        if self.at_once:
            self.absorb()

    def drain(self, rings=None):
        def under_way():
            pending = self.active + ([] if self.loading is None else [self.loading])
            return [ring for ring in pending if rings is None or any(ring is one for one in rings)]

        while under_way():
            self.pump()


def backward_kernel(dims, *refs):
    layers, chips, width, q_width, kv_width, ff = dims
    slots = 2 * chips
    it = iter(refs)
    g_ref, g_rows_ref = next(it), next(it)
    parts = len(CHAINS)
    weights = [next(it) for _ in range(parts * layers)]
    (
        kv_ref, normed_a_ref, qt_ref, lse_ref, att_ref, middle_ref, normed_m_ref,
        gate_ref, up_ref, act_ref, x_first_ref, x_next_ref, gain_ref,
        cos_ref, sin_ref, kpos_ref, qpos_ref, qstart_ref,
    ) = (next(it) for _ in range(18))
    d_hidden_ref, d_gain_out_ref, x_out_ref = next(it), next(it), next(it)
    d_query_ref, d_key_ref, d_value_ref, d_out_ref, d_w_gate_ref, d_w_up_ref, d_down_ref = (
        next(it) for _ in range(7)
    )
    land_down, land_gu, land_out, land_q = (next(it) for _ in range(4))
    (
        wt, kv_buf, dkv_sib, dw_mlp, dw_attn, a_sib, at_buf, g_act, g_gu, g_att, acc,
        g_low, g2_low, b_send, b_recv, qt_l, lse_l, da_t, dq_t, dkv_sum, gu_buf, rows_f32, n_own,
        stage, out_stage, turn_stage, land_kv, land_dkv, d_gain_ref, d_gain_in, gain_slots, land_gain, send_sems, recv_sems, load_sems, stage_sems,
    ) = (next(it) for _ in range(36))

    rows = g_ref.shape[0]
    tokens = 2 * rows
    db = width // slots
    side = width // 2
    heads_kv = kv_width // HEAD_SIZE
    group = q_width // kv_width
    qkv_width = q_width + 2 * kv_width
    links = Links(chips, send_sems, recv_sems)
    links.greet()
    g_qkv = g_gu.at[:, pl.ds(0, qkv_width)]
    rounds = Rounds()
    cosine, sine = cos_ref[...], sin_ref[...]
    scale = HEAD_SIZE ** (-0.5)

    def local(src, dst, sem):
        copy = pltpu.make_async_copy(src, dst, load_sems.at[sem])
        copy.start()
        return copy

    def load(i, column, wide, target, sem):
        return local(weights[i].at[:, :, pl.ds(column, wide)], target, sem)

    def flat(ref):
        return ref[...].reshape(width, ref.shape[-1])

    def write(d, total, target, turned):
        if turned:
            total = total.T
            source = turn_stage.at[d, pl.ds(0, total.shape[0]), :]
        else:
            source = out_stage.at[d, :, pl.ds(0, total.shape[1])]
        source[...] = total
        copy = pltpu.make_async_copy(source, target, stage_sems.at[4 + d])
        copy.start()
        copy.wait()

    def scatter(ref, column, sizes, landing, out, at, turned=False, staged=True):
        offsets = (0, sizes[0])

        def window(d):
            return lambda slot: ref.at[slot, :, pl.ds(column + offsets[d], sizes[d])]

        def land(d):
            return lambda step: landing.at[d, step, :, pl.ds(0, sizes[d])]

        def finish(d, total):
            there = pl.ds(at + offsets[d], sizes[d])
            write(d, total, out.at[there, :] if turned else out.at[:, there], turned)

        return rounds.start(
            RingScatter(
                links,
                (window(0), window(1)),
                (land(0), land(1)),
                finish,
                stage if staged else None,
                stage_sems,
            )
        )

    def turn_columns(own, sib):
        at_buf[:, 0:tokens] = own.astype(F32).T.astype(BF16)
        at_buf[:, tokens : 2 * tokens] = sib.astype(F32).T.astype(BF16)

    def weight_grad(target, column, right, wide):
        for c in range(0, wide, TILE):
            size = min(TILE, wide - c)
            part = dot(at_buf[...], right[:, c : c + size])
            target[:, :, column + c : column + c + size] = part.reshape(chips, db, size).astype(
                BF16
            )

    def norm_back(grad, value, gain, row):
        inverse = rms_inverse(value)
        normalized = value * inverse
        d_gain_ref[row : row + 1, :] = jnp.sum(grad * normalized, axis=0, keepdims=True)
        scaled = grad * gain
        mean = jnp.mean(scaled * normalized, axis=-1, keepdims=True)
        d_hidden_ref[...] += inverse * (scaled - normalized * mean)


    local(g_ref, d_hidden_ref, 10).wait()
    pairs = (heads_kv + 1) // 2
    mlp_rings, attn_rings = [], []
    for layer in reversed(range(layers)):
        attn, gate_up, down_w = parts * layer, parts * layer + 1, parts * layer + 2
        gain_a = gain_ref[layer : layer + 1, :]
        gain_m = gain_ref[layers + layer : layers + layer + 1, :]
        links.finish()

        def load_tile(t):
            at = (t % 2) * 3
            columns = pl.ds(t * TILE, TILE)
            return [
                load(down_w, t * TILE, TILE, wt.at[at + 2], at + 2),
                load(gate_up, t * TILE, TILE, wt.at[at], at),
                load(gate_up, ff + t * TILE, TILE, wt.at[at + 1], at + 1),
                local(gate_ref.at[layer, :, columns], gu_buf.at[t % 2, 0], 6 + t % 2 * 2),
                local(up_ref.at[layer, :, columns], gu_buf.at[t % 2, 1], 7 + t % 2 * 2),
            ]

        if layer == layers - 1:
            g_load = local(g_rows_ref, g_low, 11)
        else:
            g_low[0:rows, :] = d_hidden_ref[...].astype(BF16)
            swap = links.to_head(g_low.at[pl.ds(0, rows), :], g_low.at[pl.ds(rows, rows), :])
        far = pl.ds(side, side)
        other_rows = pl.ds(tokens, tokens)
        from_sib_act = links.to_sibling(act_ref.at[layer], g_act.at[other_rows, :])
        here_act = local(act_ref.at[layer], g_act.at[pl.ds(0, tokens), :], 10)
        pending = load_tile(0)
        from_sib = [
            links.to_sibling(normed_m_ref.at[layer, :, far], a_sib.at[1]),
            links.to_sibling(normed_a_ref.at[layer, :, far], a_sib.at[3]),
            links.to_sibling(att_ref.at[layer], g_att.at[other_rows, :]),
        ]
        here = [
            local(normed_m_ref.at[layer, :, pl.ds(0, side)], n_own, 13),
            local(att_ref.at[layer], g_att.at[pl.ds(0, tokens), :], 15),
            local(middle_ref.at[layer], rows_f32, 14),
            local(qt_ref.at[layer], qt_l, 16),
            local(lse_ref.at[layer], lse_l, 17),
        ]
        rounds.drain(mlp_rings)
        if layer == layers - 1:
            g_load.wait()
        else:
            swap.wait_recv()
        from_sib_g = links.to_sibling(g_low.at[:, far], a_sib.at[0])
        here_act.wait()
        from_sib_act.wait_recv()
        from_sib_g.wait_recv()
        turn_columns(g_low[:, 0:side], a_sib[0])
        weight_grad(dw_mlp.at[0], 0, g_act, ff)
        mlp_rings = []
        for i in range(2):
            size = ff // 4
            mlp_rings.append(
                scatter(
                    dw_mlp.at[0],
                    2 * i * size,
                    (size, size),
                    land_down.at[layer, i],
                    d_down_ref.at[layer],
                    2 * i * size,
                    turned=True,
                )
            )
        count = ff // TILE
        from_sib_gu = []
        for t in range(count):
            following = load_tile(t + 1) if t + 1 < count else None
            for copy in pending:
                copy.wait()
            at = (t % 2) * 3
            gate = gu_buf[t % 2, 0].astype(F32)
            up = gu_buf[t % 2, 1].astype(F32)
            d_act = dot(g_low[...], flat(wt.at[at + 2]))
            sig = jax.nn.sigmoid(gate)
            d_gate = (d_act * up * sig * (1.0 + gate * (1.0 - sig))).astype(BF16)
            d_up = (d_act * gate * sig).astype(BF16)
            for part, grad in enumerate((d_gate, d_up)):
                column = part * ff + t * TILE
                g_gu[0:tokens, column : column + TILE] = grad
                from_sib_gu.append(
                    links.to_sibling(
                        g_gu.at[pl.ds(0, tokens), pl.ds(column, TILE)],
                        g_gu.at[other_rows, pl.ds(column, TILE)],
                    )
                )
            if t == 0:
                acc[...] = dot_nt(d_gate, flat(wt.at[at]))
            else:
                acc[...] += dot_nt(d_gate, flat(wt.at[at]))
            acc[...] += dot_nt(d_up, flat(wt.at[at + 1]))
            pending = following
            rounds.pump(2 if len(rounds.active) > 2 else 1)
        b_send[0] = acc[rows:tokens, :].astype(BF16)
        swap = links.to_head(b_send.at[0], b_recv.at[0])
        out_loads = [
            load(attn, qkv_width, TILE, wt.at[4], 4),
            load(attn, qkv_width + TILE, q_width - TILE, wt.at[5, :, :, pl.ds(0, q_width - TILE)], 5),
        ]
        for copy in here:
            copy.wait()
        for copy in from_sib + from_sib_gu:
            copy.wait_recv()

        def gate_up_grad(part):
            weight_grad(dw_mlp.at[1 + part], 0, g_gu.at[:, pl.ds(part * ff, ff)], ff)
            out = (d_w_gate_ref, d_w_up_ref)[part].at[layer]
            return scatter(
                dw_mlp.at[1 + part], 0, (ff // 2, ff // 2), land_gu.at[layer, part], out, 0
            )

        turn_columns(n_own[...], a_sib[1])
        here = [local(normed_a_ref.at[layer, :, pl.ds(0, side)], n_own, 12)]
        mlp_rings.append(gate_up_grad(0))
        rounds.pump(2)
        swap.wait_recv()
        norm_back(
            acc[0:rows, :] + b_recv[0].astype(F32), rows_f32[...], gain_m, layers + layer
        )
        g2_low[0:rows, :] = d_hidden_ref[...].astype(BF16)
        swap = links.to_head(g2_low.at[pl.ds(0, rows), :], g2_low.at[pl.ds(rows, rows), :])
        mlp_rings.append(gate_up_grad(1))
        rounds.pump(2)
        rounds.drain(attn_rings)

        swap.wait_recv()
        from_sib_g = links.to_sibling(g2_low.at[:, far], a_sib.at[2])
        for i, copy in enumerate(out_loads):
            copy.wait()
            size = TILE if i == 0 else q_width - TILE
            part = dot(g2_low[...], flat(wt.at[4 + i, :, :, pl.ds(0, size)]))
            da_t[i * TILE : i * TILE + size, :] = part.T.astype(BF16)
        rounds.pump()
        if layer == layers - 1:
            def load_down(t):
                return load(down_w, t * TILE, TILE, wt.at[4 + t % 2], 4 + t % 2)

            pending = load_down(0)
            for t in range(count):
                following = load_down(t + 1) if t + 1 < count else None
                pending.wait()
                down = dot_nt(g_act[0:tokens, t * TILE : (t + 1) * TILE], flat(wt.at[4 + t % 2]))
                if t == 0:
                    acc[...] = down
                else:
                    acc[...] += down
                pending = following
            b_send[2] = acc[rows:tokens, :].astype(BF16)
            out_swap = links.to_head(b_send.at[2], b_recv.at[2])
            rows_f32[...] += acc[0:rows, :]
            rounds.pump(2)

        units = SEQS * heads_kv

        def unit_copies(u, at):
            h, s = u // SEQS, u % SEQS
            lanes = pl.ds(pl.multiple_of(s * ROWS, ROWS), ROWS)
            return [
                pltpu.make_async_copy(
                    kv_ref.at[
                        layer,
                        :,
                        pl.ds(pl.multiple_of(part * kv_width + h * HEAD_SIZE, HEAD_SIZE), HEAD_SIZE),
                        lanes,
                    ],
                    kv_buf.at[at, part],
                    load_sems.at[6 + 2 * at + part],
                )
                for part in range(2)
            ]

        def unit(u, carry):
            at = u % 2
            h, s = u // SEQS, u % SEQS
            for copy in unit_copies(u, at):
                copy.wait()
            ahead = jnp.minimum(u + 1, units - 1)

            @pl.when(u + 1 < units)
            def _():
                for copy in unit_copies(ahead, 1 - at):
                    copy.start()

            kt = jnp.concatenate([kv_buf[at, 0, j] for j in range(slots)], axis=1)
            vt = jnp.concatenate([kv_buf[at, 1, j] for j in range(slots)], axis=1)
            lanes = pl.ds(pl.multiple_of(s * ROWS, ROWS), ROWS)
            allowed = (kpos_ref[s] <= qpos_ref[s]) & (kpos_ref[s] >= qstart_ref[s])
            dkt = dvt = None
            for g in range(group):
                head_rows = pl.ds(
                    pl.multiple_of((h * group + g) * HEAD_SIZE, HEAD_SIZE), HEAD_SIZE
                )
                qt = qt_l[head_rows, lanes]
                dot_t = da_t[head_rows, lanes]
                scores = masked(dot_tn(qt, kt), [allowed])
                probs = jnp.exp(scores - lse_l[u, g * ROWS : (g + 1) * ROWS, :])
                dprobs = dot_tn(dot_t, vt)
                delta = jnp.sum(probs * dprobs, axis=1, keepdims=True)
                dscores = (probs * (dprobs - delta)).astype(BF16)
                dq_t[head_rows, lanes] = dot_nt(kt, dscores)
                dk_part = dot(qt, dscores)
                dv_part = dot(dot_t, probs.astype(BF16))
                dkt = dk_part if dkt is None else dkt + dk_part
                dvt = dv_part if dvt is None else dvt + dv_part
            spot = pl.ds(pl.multiple_of((h % 2) * SEQS * ROWS + s * ROWS, ROWS), ROWS)
            for j in range(slots):
                wt[h // 2, j, :, spot] = dkt[:, j * ROWS : (j + 1) * ROWS].astype(BF16)
                wt[pairs + h // 2, j, :, spot] = dvt[:, j * ROWS : (j + 1) * ROWS].astype(BF16)
            return carry

        sums = Rounds(at_once=True)
        sent = {}

        def offer(i):
            for j in (i, pairs + i):
                sent[j] = links.to_sibling(wt.at[j, pl.ds(chips, chips)], dkv_sib.at[j])

        def total_up(i):
            for j in (i, pairs + i):
                sent[j].wait_recv()
                for slot in range(chips):
                    wt[j, slot] = (wt[j, slot].astype(F32) + dkv_sib[j, slot].astype(F32)).astype(
                        BF16
                    )

            def finish(d, total):
                dkv_sum[d * pairs + i] = total

            sums.start(
                RingScatter(
                    links,
                    (lambda slot: wt.at[i, slot], lambda slot: wt.at[pairs + i, slot]),
                    (
                        lambda step: land_dkv.at[i, 0, step],
                        lambda step: land_dkv.at[i, 1, step],
                    ),
                    finish,
                )
            )

        for copy in unit_copies(0, 0):
            copy.start()
        for i in range(pairs):
            low, high = units * i // pairs, units * (i + 1) // pairs
            if i == 0:
                middle_unit = (low + high) // 2
                lax.fori_loop(low, middle_unit, unit, 0)
                rounds.pump(3)
                lax.fori_loop(middle_unit, high, unit, 0)
                rounds.pump(3)
            else:
                for u in range(low, high):
                    lax.fori_loop(u, u + 1, unit, 0)
                    if u == low:
                        total_up(i - 1)
                    else:
                        sums.pump(2)
                    if u % 2:
                        rounds.pump()
            offer(i)

        if layer == layers - 1:
            out_swap.wait_recv()
            links.sent(out_swap)
            b_send[2] = (rows_f32[...] + b_recv[2].astype(F32)).astype(BF16)
            local(b_send.at[2], x_out_ref, 11).wait()
        x_in = x_next_ref.at[layer - 1] if layer else x_first_ref
        here.append(local(x_in, rows_f32, 15))
        from_sib_g.wait_recv()
        turn_columns(g2_low[:, 0:side], a_sib[2])
        weight_grad(dw_attn, qkv_width, g_att, q_width)
        half = q_width // 2
        attn_rings = [
            scatter(
                dw_attn, qkv_width, (half, half), land_out.at[layer], d_out_ref.at[layer], 0, turned=True
            )
        ]
        total_up(pairs - 1)

        def turned_back(low, high):
            return low * cosine + high * sine, high * cosine - low * sine

        for h in range(q_width // HEAD_SIZE):
            at = h * HEAD_SIZE
            low, high = turned_back(
                dq_t[at : at + HALF, :], dq_t[at + HALF : at + HEAD_SIZE, :]
            )
            dq_t[at : at + HALF, :] = low * scale
            dq_t[at + HALF : at + HEAD_SIZE, :] = high * scale
        for copy in from_sib_gu:
            links.sent(copy)
        g_qkv[0:tokens, 0:q_width] = dq_t[...].T.astype(BF16)
        mine = pl.ds(0, tokens)
        from_sib_q = links.to_sibling(
            g_qkv.at[mine, pl.ds(0, q_width)], g_qkv.at[other_rows, pl.ds(0, q_width)]
        )
        step = 0
        while sums.active:
            sums.pump()
            step += 1
            if step % 4 == 0:
                rounds.pump()
            if step == 4:
                from_sib_q.wait_recv()
                for copy in here:
                    copy.wait()
                turn_columns(n_own[...], a_sib[3])
                weight_grad(dw_attn, 0, g_qkv, q_width)
                attn_rings.append(
                    scatter(
                        dw_attn, 0, (half, half), land_q.at[layer], d_query_ref.at[layer], 0
                    )
                )
        for h in range(heads_kv):
            spot = slice((h % 2) * SEQS * ROWS, (h % 2 + 1) * SEQS * ROWS)
            block = dkv_sum[h // 2, :, spot]
            low, high = turned_back(block[0:HALF, :], block[HALF:HEAD_SIZE, :])
            at = h * HEAD_SIZE
            dq_t[at : at + HALF, :] = low
            dq_t[at + HALF : at + HEAD_SIZE, :] = high
            dq_t[kv_width + at : kv_width + at + HEAD_SIZE, :] = dkv_sum[pairs + h // 2, :, spot]
        g_qkv[0:tokens, q_width:qkv_width] = dq_t[0 : 2 * kv_width, :].T.astype(BF16)
        from_sib_kv = links.to_sibling(
            g_qkv.at[mine, pl.ds(q_width, 2 * kv_width)],
            g_qkv.at[other_rows, pl.ds(q_width, 2 * kv_width)],
        )
        links.finish()
        tiles = [
            load(attn, t * TILE, TILE, wt.at[t], t) for t in range(qkv_width // TILE)
        ]
        for t, tile in enumerate(tiles):
            tile.wait()
            back = dot_nt(g_qkv[0:tokens, t * TILE : (t + 1) * TILE], flat(wt.at[t]))
            if t == 0:
                acc[...] = back
            else:
                acc[...] += back
        b_send[1] = acc[rows:tokens, :].astype(BF16)
        swap = links.to_head(b_send.at[1], b_recv.at[1])
        from_sib_kv.wait_recv()
        weight_grad(dw_attn, q_width, g_qkv.at[:, pl.ds(q_width, 2 * kv_width)], 2 * kv_width)
        long = -(-kv_width // 256) * 128
        short = kv_width - long
        for i, (out, sizes) in enumerate(
            ((d_key_ref, (long, short)), (d_value_ref, (short, long)))
        ):
            attn_rings.append(
                scatter(
                    dw_attn,
                    q_width + i * kv_width,
                    sizes,
                    land_kv.at[i],
                    out.at[layer],
                    0,
                    staged=False,
                )
            )
        rounds.pump()
        swap.wait_recv()
        norm_back(acc[0:rows, :] + b_recv[1].astype(F32), rows_f32[...], gain_a, layer)
    swap = links.to_head(d_gain_ref, d_gain_in.at[0])
    rounds.pump(2)
    swap.wait_recv()
    gain_sum = d_gain_ref[...] + d_gain_in[0]
    d_gain_in[1] = gain_sum
    swap = links.to_sibling(d_gain_in.at[1, :, pl.ds(side, side)], d_gain_in.at[2, :, pl.ds(0, side)])
    rounds.pump(2)
    swap.wait_recv()
    gain_sum = gain_sum[:, 0:side] + d_gain_in[2, :, 0:side]
    gain_slots[...] = jnp.zeros_like(gain_slots)
    for slot in range(chips):
        for d in range(2):
            gain_slots[slot, d, 0:layers, 0:db] = gain_sum[
                d * layers : (d + 1) * layers, slot * db : (slot + 1) * db
            ]

    def gain_finish(d, total):
        d_gain_out_ref[d] = total

    rounds.start(
        RingScatter(
            links,
            (lambda slot: gain_slots.at[slot, 0], lambda slot: gain_slots.at[slot, 1]),
            (lambda step: land_gain.at[0, step], lambda step: land_gain.at[1, step]),
            gain_finish,
        )
    )
    rounds.drain()
    links.finish()


def backward(grad, grad_rows, weights, saved, tables, chips, q_width, kv_width, ff):
    layers = len(weights) // len(CHAINS)
    rows, width = grad.shape
    slots = 2 * chips
    db = width // slots
    tokens = 2 * rows
    heads_kv = kv_width // HEAD_SIZE
    units = SEQS * heads_kv
    pairs = (heads_kv + 1) // 2
    group = q_width // kv_width
    steps = chips - 1
    qkv_width = q_width + 2 * kv_width
    dims = (layers, chips, width, q_width, kv_width, ff)
    rings = 4 + 4 + pairs
    copies = 3 + 2 * steps + layers * (rings * 2 * steps + 4 + 4 + 1 + 2 * (ff // TILE) + 1 + 2 * pairs + 2)
    any_spec = pl.BlockSpec(memory_space=pltpu.HBM)
    vmem = pl.BlockSpec(memory_space=pltpu.VMEM)

    def landing(*shape):
        return jax.ShapeDtypeStruct(shape, BF16)

    out = pl.pallas_call(
        functools.partial(backward_kernel, dims),
        out_shape=[
            jax.ShapeDtypeStruct((rows, width), F32),
            jax.ShapeDtypeStruct((2, 8, 128), F32),
            jax.ShapeDtypeStruct((rows, width), BF16),
            jax.ShapeDtypeStruct((layers, db, q_width), F32),
            jax.ShapeDtypeStruct((layers, db, kv_width), F32),
            jax.ShapeDtypeStruct((layers, db, kv_width), F32),
            jax.ShapeDtypeStruct((layers, q_width, db), F32),
            jax.ShapeDtypeStruct((layers, db, ff), F32),
            jax.ShapeDtypeStruct((layers, db, ff), F32),
            jax.ShapeDtypeStruct((layers, ff, db), F32),
            landing(layers, 2, 2, steps, db, ff // 4),
            landing(layers, 2, 2, steps, db, ff // 2),
            landing(layers, 2, steps, db, q_width // 2),
            landing(layers, 2, steps, db, q_width // 2),
        ],
        in_specs=[any_spec] * (len(weights) + 14) + [vmem] * 6,
        out_specs=[vmem] * 2 + [any_spec] * 12,
        scratch_shapes=[
            pltpu.VMEM((6, slots, db, TILE), BF16),
            pltpu.VMEM((2, 2, slots, HEAD_SIZE, ROWS), BF16),
            pltpu.VMEM((2 * pairs, chips, HEAD_SIZE, 2 * SEQS * ROWS), BF16),
            pltpu.VMEM((3, chips, db, ff), BF16),
            pltpu.VMEM((chips, db, qkv_width + q_width), BF16),
            pltpu.VMEM((4, tokens, width // 2), BF16),
            pltpu.VMEM((width // 2, 2 * tokens), BF16),
            pltpu.VMEM((2 * tokens, ff), BF16),
            pltpu.VMEM((2 * tokens, 2 * ff), BF16),
            pltpu.VMEM((2 * tokens, q_width), BF16),
            pltpu.VMEM((tokens, width), F32),
            pltpu.VMEM((tokens, width), BF16),
            pltpu.VMEM((tokens, width), BF16),
            pltpu.VMEM((3, rows, width), BF16),
            pltpu.VMEM((3, rows, width), BF16),
            pltpu.VMEM((q_width, tokens), BF16),
            pltpu.VMEM((units, group * ROWS, 1), F32),
            pltpu.VMEM((q_width, tokens), BF16),
            pltpu.VMEM((q_width, tokens), F32),
            pltpu.VMEM((2 * pairs, HEAD_SIZE, 2 * SEQS * ROWS), F32),
            pltpu.VMEM((2, 2, tokens, TILE), BF16),
            pltpu.VMEM((rows, width), F32),
            pltpu.VMEM((tokens, width // 2), BF16),
            pltpu.VMEM((2, 2, db, ff // 2), BF16),
            pltpu.VMEM((2, db, ff // 2), F32),
            pltpu.VMEM((2, ff // 4, db), F32),
            pltpu.VMEM((2, 2, steps, db, -(-kv_width // 256) * 128), BF16),
            pltpu.VMEM((pairs, 2, steps, HEAD_SIZE, 2 * SEQS * ROWS), BF16),
            pltpu.VMEM((2 * layers, width), F32),
            pltpu.VMEM((3, 2 * layers, width), F32),
            pltpu.VMEM((chips, 2, 8, 128), F32),
            pltpu.VMEM((2, steps, 8, 128), F32),
            pltpu.SemaphoreType.DMA((copies,)),
            pltpu.SemaphoreType.DMA((copies,)),
            pltpu.SemaphoreType.DMA((18,)),
            pltpu.SemaphoreType.DMA((6,)),
        ],
        compiler_params=pltpu.CompilerParams(
            collective_id=1, has_side_effects=True, vmem_limit_bytes=KERNEL_VMEM
        ),
    )(grad, grad_rows, *weights, *saved, *tables)
    return out[:10]


def build(n_ctx):
    chips = n_ctx // 2
    ring = ring_of(chips)

    def shifted(step):
        pairs = []
        for at, chip in enumerate(ring):
            target = ring[(at + step) % chips]
            pairs += [(chip * 2 + core, target * 2 + core) for core in range(2)]
        return pairs

    up, down = shifted(1), shifted(-1)
    sibling = [(i, i ^ 1) for i in range(n_ctx)]

    def send_up(value):
        return lax.ppermute(value, "ctx", up)

    def send_down(value):
        return lax.ppermute(value, "ctx", down)

    def swap_core(value):
        return lax.ppermute(value, "ctx", sibling)

    def swap_head(value):
        return lax.ppermute(value, "head", [(0, 1), (1, 0)])

    def ring_gather(shard):
        half = chips // 2

        def step(carry, unused):
            carry = (send_up(carry[0]), send_down(carry[1]))
            return carry, carry

        (low, high), (lows, highs) = lax.scan(step, (shard, shard), None, length=half - 1)
        cut = shard.shape[0] // 2
        across = jnp.concatenate([send_up(low[:cut]), send_down(high[cut:])], axis=0)
        return jnp.concatenate([shard[None], highs, across[None], lows[::-1]], axis=0)

    def ring_scatter(lows, highs):
        def own(parts, slot):
            return lax.dynamic_index_in_dim(parts, slot, 0, keepdims=False).astype(F32)

        def step(carry, at):
            low, high = (send_up(carry[0]), send_down(carry[1]))
            low = low.astype(F32) + own(lows, (chips - 1 - at) % chips)
            high = high.astype(F32) + own(highs, (1 + at) % chips)
            return (low.astype(BF16), high.astype(BF16)), None

        start = (lows[chips - 1].astype(BF16), highs[1].astype(BF16))
        steps = jnp.arange(1, chips - 1, dtype=jnp.int32)
        (low, high), unused = lax.scan(step, start, steps)
        return (
            send_up(low).astype(F32) + lows[0].astype(F32),
            send_down(high).astype(F32) + highs[0].astype(F32),
        )

    def gather(shard):
        own = ring_gather(shard).reshape(chips * shard.shape[0], shard.shape[1])
        return jnp.concatenate([own, swap_core(own)], axis=0)

    def weight_scatter(grad):
        db, cut = grad.shape[0] // chips, grad.shape[1] // 2
        parts = grad.reshape(chips, db, grad.shape[1])
        return jnp.concatenate(ring_scatter(parts[:, :, :cut], parts[:, :, cut:]), axis=1)

    def local(
        hidden_in,
        block_order,
        doc_ids,
        attn_gain,
        w_query,
        w_key,
        w_value,
        w_out,
        mlp_gain,
        w_gate,
        w_up,
        w_down,
        cotangent,
    ):
        layers, db = w_query.shape[0], w_query.shape[1]
        width = db * n_ctx
        side = width // 2
        q_width, kv_width, ff_width = w_query.shape[2], w_key.shape[2], w_gate.shape[2]
        heads_q, heads_kv = q_width // HEAD_SIZE, kv_width // HEAD_SIZE
        group = heads_q // heads_kv
        own_rows = hidden_in.shape[0]
        token_rows = own_rows * 2
        ctx = lax.axis_index("ctx")
        head = lax.axis_index("head")
        core = ctx % 2
        place_of = [0] * chips
        for at, chip in enumerate(ring):
            place_of[chip] = at
        place = jnp.array(place_of, jnp.int32)[ctx // 2]

        slot_ids = jnp.arange(n_ctx, dtype=jnp.int32)
        along = (place + slot_ids % chips) % chips
        chip_of = jnp.where(along < chips // 2, 2 * along, 2 * (chips - 1 - along) + 1)
        block_of = chip_of * 2 + (core + slot_ids // chips) % 2
        block_hot = (block_of[:, None] == slot_ids[None, :]).astype(F32)
        feature = jnp.arange(width, dtype=jnp.int32)
        wanted = jnp.repeat(block_of, db) * db + feature % db
        to_ring = (feature[:, None] == wanted[None, :]).astype(BF16)

        def reorder(rows):
            return dot(rows, to_ring)

        def restore(rows):
            return dot_nt(rows, to_ring)

        def thirds(rows):
            high = lax.reduce_precision(rows, 8, 7)
            middle = lax.reduce_precision(rows - high, 8, 7)
            return [part.astype(BF16) for part in (high, middle, rows - high - middle)]

        offsets = jnp.arange(BLK, dtype=jnp.int32)

        def own_first(table):
            return jnp.where(head == 0, table, jnp.stack([table[1], table[0]], axis=0))

        order, docs = own_first(block_order), own_first(doc_ids)
        own_blocks = lax.dynamic_slice(order, (jnp.int32(0), 2 * ctx), (SEQS, 2))
        q_positions = (own_blocks[:, :, None] * BLK + offsets[None, None, :]).reshape(SEQS, ROWS)
        ring_blocks = jnp.einsum(
            "ac,scb->sab", block_hot, order.reshape(SEQS, n_ctx, 2).astype(F32)
        ).astype(jnp.int32)
        k_positions = (ring_blocks[..., None] * BLK + offsets).reshape(SEQS, 1, n_ctx * ROWS)
        doc_blocks = docs.reshape(SEQS, -1, BLK)
        own_hot = (own_blocks[:, :, None] == jnp.arange(doc_blocks.shape[1])).astype(F32)
        q_docs = jnp.einsum("sab,sbj->saj", own_hot, doc_blocks.astype(F32)).astype(jnp.int32)
        q_docs = q_docs.reshape(SEQS, ROWS)
        q_starts = jnp.sum((docs[:, None, :] < q_docs[:, :, None]).astype(jnp.int32), axis=2)
        kpos = k_positions
        qpos, qstart = q_positions[:, :, None], q_starts[:, :, None]
        cosine, sine_table = rope_tables(q_positions.reshape(token_rows))
        scale_q = HEAD_SIZE ** (-0.5)

        def both_rows(rows):
            return jnp.concatenate([rows, swap_head(rows)], axis=0)

        def to_owner(parts):
            return parts[:own_rows] + swap_head(parts[own_rows:].astype(BF16)).astype(F32)

        def project(rows, weight, lo, hi):
            return dot(rows, weight[:, lo:hi])

        def project_back(rows, weight, lo, hi):
            return dot_nt(rows, weight[:, lo:hi])

        def weight_grad(left, right):
            lefts = jnp.concatenate([left[:, :side], swap_core(left[:, side:])], axis=0)
            rights = jnp.concatenate([right, swap_core(right)], axis=0)
            return dot_tn(lefts, rights)

        def units(rows):
            shaped = rows.reshape(SEQS, ROWS, heads_kv, group, HEAD_SIZE)
            return shaped.transpose(0, 2, 3, 1, 4).reshape(SEQS, heads_kv, group * ROWS, HEAD_SIZE)

        def from_units(parts):
            shaped = parts.reshape(SEQS, heads_kv, group, ROWS, HEAD_SIZE)
            return shaped.transpose(0, 3, 1, 2, 4).reshape(token_rows, q_width)

        qkv_width = q_width + 2 * kv_width
        attn_width = qkv_width + q_width
        both = reorder(jnp.concatenate([hidden_in, cotangent], axis=0))
        grad_res = both[own_rows:]
        attn_shards = [
            jnp.concatenate(
                [w_query[layer], w_key[layer], w_value[layer], w_out[layer].T], axis=1
            )
            for layer in range(layers)
        ]
        gate_up_shards = [
            jnp.concatenate([w_gate[layer], w_up[layer]], axis=1) for layer in range(layers)
        ]

        def forward_by_ops(residual):
            gains = lax.all_gather(
                jnp.concatenate([attn_gain, mlp_gain], axis=0), "ctx", axis=1, tiled=True
            )
            gains = reorder(gains)
            fetched = [
                (
                    gather(attn_shards[layer]),
                    gather(
                        jnp.concatenate([gate_up_shards[layer], w_down[layer].T], axis=1)
                    ),
                )
                for layer in range(layers)
            ]
            records = []
            for layer in range(layers):
                attn_w, mlp_w = fetched[layer]
                gain_a, gain_m = gains[layer], gains[layers + layer]
                residual_in = residual
                normed_a = both_rows((residual * rms_inverse(residual) * gain_a).astype(BF16))
                projected = project(normed_a, attn_w, 0, qkv_width)
                q_rows = rotate(
                    projected[:, :q_width].reshape(token_rows, heads_q, HEAD_SIZE),
                    cosine,
                    sine_table,
                )
                queries = units((q_rows * scale_q).astype(BF16).reshape(token_rows, q_width))
                keys = rotate(
                    projected[:, q_width : q_width + kv_width].reshape(
                        token_rows, heads_kv, HEAD_SIZE
                    ),
                    cosine,
                    sine_table,
                ).reshape(token_rows, kv_width)
                kv_shard = jnp.concatenate([keys, projected[:, q_width + kv_width :]], axis=1)
                kv_own = ring_gather(kv_shard.astype(BF16).T)
                kv = jnp.concatenate([kv_own, swap_core(kv_own)], axis=0)
                mixed, lse = attend_forward(queries, kv, kpos, qpos, qstart)
                attended = from_units(mixed)
                middle = residual + to_owner(
                    project_back(attended, attn_w, qkv_width, attn_width)
                )
                normed_m = both_rows((middle * rms_inverse(middle) * gain_m).astype(BF16))
                gate_up = project(normed_m, mlp_w, 0, 2 * ff_width)
                gate_part, up_part = gate_up[:, :ff_width], gate_up[:, ff_width:]
                activated = (jax.nn.silu(gate_part) * up_part).astype(BF16)
                residual = middle + to_owner(
                    project_back(activated, mlp_w, 2 * ff_width, 3 * ff_width)
                )
                records.append(
                    (
                        residual_in,
                        normed_a,
                        queries,
                        kv,
                        lse,
                        attended,
                        middle,
                        normed_m,
                        gate_part,
                        up_part,
                        activated,
                    )
                )
            return fetched, gains, records, residual

        def forward_by_kernel(residual):
            columns = jnp.concatenate([attn_gain, mlp_gain], axis=0).T
            columns = jnp.pad(columns, ((0, 0), (0, 128 - columns.shape[1])))
            shards = []
            for layer in range(layers):
                attn = attn_shards[layer]
                if layer == 0:
                    attn = jnp.concatenate([attn, columns], axis=1)
                shards += [attn, gate_up_shards[layer], w_down[layer].T]
            weights, saved = forward(
                residual,
                grad_res.astype(BF16),
                shards,
                cosine.T,
                sine_table.T,
                kpos,
                qpos,
                qstart,
                chips,
                q_width,
                kv_width,
                ff_width,
            )
            tables = (cosine.T, sine_table.T, kpos, qpos, qstart)
            records = [*saved[:10], residual, saved[10], saved[11]]
            return weights, tables, records, saved[12]

        in_kernel = n_ctx * ROWS <= 2048 and db == HEAD_SIZE
        run_forward = forward_by_kernel if in_kernel else forward_by_ops
        fetched, gains, records, last = run_forward(both[:own_rows])
        def norm_back(grad_res, normed_gradient, value_rows, inverse_norm, gain):
            normalized = value_rows * inverse_norm
            gain_gradient = jnp.sum(normed_gradient * normalized, axis=0)
            scaled = normed_gradient * gain
            mean = jnp.mean(scaled * normalized, axis=-1, keepdims=True)
            return grad_res + inverse_norm * (scaled - normalized * mean), gain_gradient

        def backward_by_ops(grad_res):
            d_attn = [None] * layers
            d_mlp = [None] * layers
            d_gains = [None] * (2 * layers)
            for layer in reversed(range(layers)):
                attn_w, mlp_w = fetched[layer]
                gain_a, gain_m = gains[layer], gains[layers + layer]
                (
                    residual_in,
                    normed_a,
                    queries,
                    kv,
                    lse,
                    attended,
                    middle,
                    normed_m,
                    gate_part,
                    up_part,
                    activated,
                ) = records[layer]
                inverse_a, inverse_m = rms_inverse(residual_in), rms_inverse(middle)
                grad_rows_m = both_rows(grad_res.astype(BF16))
                grad_act = project(grad_rows_m, mlp_w, 2 * ff_width, 3 * ff_width)
                sigmoid_g = jax.nn.sigmoid(gate_part)
                grad_gate = grad_act * up_part * sigmoid_g * (1.0 + gate_part * (1.0 - sigmoid_g))
                grad_up = grad_act * gate_part * sigmoid_g
                grad_gu = jnp.concatenate([grad_gate, grad_up], axis=1).astype(BF16)
                grad_norm_m = to_owner(project_back(grad_gu, mlp_w, 0, 2 * ff_width))
                d_down = weight_scatter(weight_grad(grad_rows_m, activated))
                d_gu = weight_scatter(weight_grad(normed_m, grad_gu))
                grad_res, d_gains[layers + layer] = norm_back(
                    grad_res, grad_norm_m, middle, inverse_m, gain_m
                )
                grad_rows_a = both_rows(grad_res.astype(BF16))
                grad_attended = project(grad_rows_a, attn_w, qkv_width, attn_width).astype(BF16)
                d_out = weight_grad(grad_rows_a, attended)
                grad_q, dk, dv = attend_backward(
                    queries, units(grad_attended), lse, kv, kpos, qpos, qstart
                )
                dk_back, dv_back = swap_core(dk[chips:]), swap_core(dv[chips:])
                grad_k, grad_v = ring_scatter(
                    dk[:chips].astype(F32) + dk_back.astype(F32),
                    dv[:chips].astype(F32) + dv_back.astype(F32),
                )
                grad_q_pre = rotate_back(
                    from_units(grad_q).reshape(token_rows, heads_q, HEAD_SIZE), cosine, sine_table
                )
                grad_k_pre = rotate_back(
                    grad_k.T.reshape(token_rows, heads_kv, HEAD_SIZE), cosine, sine_table
                )
                grad_qkv = jnp.concatenate(
                    [
                        (grad_q_pre * scale_q).reshape(token_rows, q_width),
                        grad_k_pre.reshape(token_rows, kv_width),
                        grad_v.T,
                    ],
                    axis=1,
                ).astype(BF16)
                grad_norm_a = to_owner(project_back(grad_qkv, attn_w, 0, qkv_width))
                d_qkv = weight_grad(normed_a, grad_qkv)
                d_attn[layer] = weight_scatter(jnp.concatenate([d_qkv, d_out], axis=1))
                d_mlp[layer] = (d_gu, d_down)
                grad_res, d_gains[layer] = norm_back(
                    grad_res, grad_norm_a, residual_in, inverse_a, gain_a
                )
            attn_grads, mlp_grads = jnp.stack(d_attn, axis=0), [jnp.stack(part) for part in zip(*d_mlp)]
            k_at, v_at = q_width, q_width + kv_width
            return (
                grad_res,
                jnp.stack(d_gains, axis=0),
                last.astype(BF16),
                attn_grads[:, :, :k_at],
                attn_grads[:, :, k_at:v_at],
                attn_grads[:, :, v_at:qkv_width],
                attn_grads[:, :, qkv_width:].transpose(0, 2, 1),
                mlp_grads[0][:, :, :ff_width],
                mlp_grads[0][:, :, ff_width:],
                mlp_grads[1].transpose(0, 2, 1),
            )

        if in_kernel:
            grads = backward(
                grad_res, last, fetched, records, gains, chips, q_width, kv_width, ff_width
            )
            grad_res, d_gains, x_out, *weight_grads = grads
            d_gains = d_gains[:, :layers, :db].reshape(2 * layers, db)
        else:
            grad_res, d_gains, x_out, *weight_grads = backward_by_ops(grad_res)
            parts = restore(jnp.concatenate(thirds(d_gains), axis=0))
            d_gains = parts.reshape(3, 2 * layers, width).sum(axis=0)
            d_gains = d_gains + swap_head(d_gains)
            bit = 1
            while bit < n_ctx:
                pairs = [(i, i ^ bit) for i in range(n_ctx)]
                d_gains = d_gains + lax.ppermute(d_gains, "ctx", pairs)
                bit *= 2
            d_gains = lax.dynamic_slice(d_gains, (0, ctx * db), (2 * layers, db))
        restored = restore(jnp.concatenate([x_out, *thirds(grad_res)], axis=0))
        out_hidden = restored[:own_rows].astype(BF16)
        d_hidden = restored[own_rows:].reshape(3, own_rows, width).sum(axis=0)
        return (
            out_hidden,
            d_hidden,
            d_gains[:layers],
            *weight_grads[:4],
            d_gains[layers:],
            *weight_grads[4:],
        )

    return local


def solution(mesh):
    return jax.shard_map(
        build(mesh.shape["ctx"]),
        mesh=mesh,
        in_specs=(
            P(("ctx", "head"), None),
            P(),
            P(),
            P(None, "ctx"),
            P(None, "ctx", "head"),
            P(None, "ctx", "head"),
            P(None, "ctx", "head"),
            P(None, "head", "ctx"),
            P(None, "ctx"),
            P(None, "ctx", "head"),
            P(None, "ctx", "head"),
            P(None, "head", "ctx"),
            P(("ctx", "head"), None),
        ),
        out_specs=(
            P(("ctx", "head"), None),
            P(("ctx", "head"), None),
            P(None, "ctx"),
            P(None, "ctx", "head"),
            P(None, "ctx", "head"),
            P(None, "ctx", "head"),
            P(None, "head", "ctx"),
            P(None, "ctx"),
            P(None, "ctx", "head"),
            P(None, "ctx", "head"),
            P(None, "head", "ctx"),
        ),
        check_vma=False,
    )
```
